32 devices in a mesh: lat: 8 (over z, x), lon: 4 (over y, core).
Axes of the slice: x: 2, y: 2, z: 4, core: 2. Of those that a mesh axis runs over, the one named last changes fastest.
Arguments:
- field_in: bfloat16 [80, 384, 512], P('lat', 'lon'), may hold values from -6 to 6
- kernel_taps: bfloat16 [3, 80, 3, 33], P(None, 'lat'), may hold values from -0.8984375 to 0.8984375
- row_reach: int32 [80], P('lat'), may hold values from 1 to 16, as said below
- mix_weight: bfloat16 [3, 512, 512], replicated, may hold values from -0.15625 to 0.15625
- up_weight: bfloat16 [512, 1024], replicated, may hold values from -0.25 to 0.25
- down_weight: bfloat16 [1024, 512], replicated, may hold values from -0.1875 to 0.1875
- cotangent: bfloat16 [80, 384, 512], P('lat', 'lon'), may hold values from -6 to 6
Outputs:
- block_out: bfloat16 [80, 384, 512], P('lat', 'lon')
- grad_field: bfloat16 [80, 384, 512], P('lat', 'lon')
- grad_mix: bfloat16 [3, 512, 512], replicated
- grad_up: bfloat16 [512, 1024], replicated
- grad_down: bfloat16 [1024, 512], replicated
The draws below stay inside these ranges and needn't reach their ends.
Inputs may be any that keep to these rules, and one draw needn't show every extreme that they name: `row_reach`: how many longitude cells each latitude row's kernel reaches on either side.
All inputs are finite; a program needn't handle non-finite values.
Results may differ from the reference program's by a relative error of at most 0.0068.
Values may be sent and summed in bfloat16 or wider, within the bound.
No kernel may reach another device: no remote copies, remote signals or barrier semaphores. Data moves between devices by JAX's collectives and lax.ppermute only.
A program may use at most 128 MiB of HBM per device.

```python
import jax
import jax.numpy as jnp
from jax import lax

C = 512
F = 1024
K = 3
HMAX = 16
ROWS_DEV = 10
TAPS = 33
NLAT = 80
NLON = 384
POINTS = 30720


def draw_row_reach(key, part):
    rows_all = jnp.arange(NLAT, dtype=jnp.int32)
    pole_gap = jnp.minimum(rows_all, NLAT - 1 - rows_all)
    jitter = jax.random.randint(key, (NLAT,), 0, 3, dtype=jnp.int32)
    widen = HMAX * ROWS_DEV // (pole_gap + ROWS_DEV)
    spread = jnp.clip(widen - jitter, 1, HMAX)
    return jnp.where(pole_gap == 0, HMAX, spread).astype(jnp.int32)


def level_of(own_key, dims, split, least, high):
    level, own = 1.0, jax.random.fold_in(own_key, 6)
    for position, blocks in split:
        draws = jnp.exp(jax.random.uniform(jax.random.fold_in(own, position), (blocks,), jnp.float32, least / len(split), high / len(split)))
        level = level * jnp.repeat(draws, dims[position] // blocks).reshape([-1 if axis == position else 1 for axis in range(len(dims))])
    return level


def centred(rng, extent, scale, bound, split=(), kind=jnp.bfloat16):
    drawn = scale * jax.random.normal(rng, extent, jnp.float32)
    if split:
        drawn = drawn * level_of(rng, extent, split, -0.22, 0.18)
    return jnp.clip(drawn, -bound, bound).astype(kind)


def setup_inputs(seed: int = 0) -> dict:
    splits = jax.random.split(jax.random.key(seed), 8)
    field_in = centred(splits[0], (NLAT, NLON, C), 1.0, 6.0, ((0, 8), (1, 4)))
    kernel_taps = centred(splits[1], (K, NLAT, 3, TAPS), 0.15, 0.8984375, ((1, 8),))
    row_reach = draw_row_reach(jax.random.fold_in(splits[7], 71), 0)
    mix_weight = centred(splits[3], (K, C, C), (K * C) ** -0.5, 0.15625)
    up_weight = centred(splits[4], (C, F), C ** -0.5, 0.25)
    down_weight = centred(splits[5], (F, C), F ** -0.5, 0.1875)
    cotangent = centred(splits[6], (NLAT, NLON, C), 1.0, 6.0, ((0, 8), (1, 4)))
    return dict(field_in=field_in, kernel_taps=kernel_taps, row_reach=row_reach, mix_weight=mix_weight, up_weight=up_weight, down_weight=down_weight, cotangent=cotangent)


inv_root_two = 0.7071067811865476
inv_root_tau = 0.3989422804014327

def gelu_exact(value):
    return 0.5 * value * (1.0 + jax.scipy.special.erf(value * inv_root_two))

def gelu_slope(value):
    return 0.5 * (1.0 + jax.scipy.special.erf(value * inv_root_two)) + value * jnp.exp(-0.5 * value * value) * inv_root_tau

def features_of(field, kernel_taps, row_reach):
    offsets = jnp.arange(TAPS, dtype=jnp.int32) - HMAX
    col_index = (jnp.arange(NLON, dtype=jnp.int32)[:, None] + offsets[None, :]) % NLON
    north_row = jnp.roll(field[0], -(NLON // 2), axis=0)
    south_row = jnp.roll(field[NLAT - 1], -(NLON // 2), axis=0)
    padded = jnp.concatenate([north_row[None], field, south_row[None]], axis=0)
    tap_mask = jnp.abs(offsets)[None, :] <= row_reach[:, None]
    weights = jnp.where(tap_mask[None, :, None, :], kernel_taps.astype(jnp.float32), jnp.zeros((), jnp.float32))

    def one_row(index):
        three = lax.dynamic_slice_in_dim(padded, index, 3, 0)
        windows = three[:, col_index]
        row_taps = lax.dynamic_index_in_dim(weights, index, 1, keepdims=False)
        return jnp.einsum('kdt,djtc->kjc', row_taps, windows, precision=lax.Precision.HIGHEST)
    return lax.map(one_row, jnp.arange(NLAT, dtype=jnp.int32))

def reference(field_in, kernel_taps, row_reach, mix_weight, up_weight, down_weight, cotangent):
    features = features_of(field_in.astype(jnp.float32), kernel_taps, row_reach).astype(jnp.bfloat16)
    flat_features = jnp.transpose(features, (1, 0, 2, 3)).reshape(K, POINTS, C)
    flat_field = field_in.reshape(POINTS, C)
    conv_sum = jnp.zeros((POINTS, C), jnp.float32)
    for basis in range(K):
        conv_sum = conv_sum + jnp.dot(flat_features[basis], mix_weight[basis], preferred_element_type=jnp.float32)
    hidden = (flat_field.astype(jnp.float32) + conv_sum).astype(jnp.bfloat16)
    pre_act = jnp.dot(hidden, up_weight, preferred_element_type=jnp.float32)
    activated = gelu_exact(pre_act).astype(jnp.bfloat16)
    block_out = (hidden.astype(jnp.float32) + jnp.dot(activated, down_weight, preferred_element_type=jnp.float32)).astype(jnp.bfloat16)
    grad_rows = cotangent.reshape(POINTS, C)
    act_grad = jnp.dot(grad_rows, down_weight.T, preferred_element_type=jnp.float32)
    pre_grad = (act_grad * gelu_slope(pre_act)).astype(jnp.bfloat16)
    grad_scale = 1.0 / jnp.sqrt(jnp.float32(POINTS))
    grad_down = (jnp.dot(activated.T, grad_rows, preferred_element_type=jnp.float32) * grad_scale).astype(jnp.bfloat16)
    grad_up = (jnp.dot(hidden.T, pre_grad, preferred_element_type=jnp.float32) * grad_scale).astype(jnp.bfloat16)
    hidden_grad = (grad_rows.astype(jnp.float32) + jnp.dot(pre_grad, up_weight.T, preferred_element_type=jnp.float32)).astype(jnp.bfloat16)
    mix_parts = []
    feat_parts = []
    for basis in range(K):
        mix_parts.append(jnp.dot(flat_features[basis].T, hidden_grad, preferred_element_type=jnp.float32) * grad_scale)
        feat_parts.append(jnp.dot(hidden_grad, mix_weight[basis].T, preferred_element_type=jnp.float32).astype(jnp.bfloat16))
    grad_mix = jnp.stack(mix_parts).astype(jnp.bfloat16)
    feat_grad = jnp.stack(feat_parts).reshape(K, NLAT, NLON, C)
    feat_grad_rows = jnp.transpose(feat_grad, (1, 0, 2, 3)).astype(jnp.float32)
    unused, pullback = jax.vjp(lambda value: features_of(value, kernel_taps, row_reach), field_in.astype(jnp.float32))
    adjoint = pullback(feat_grad_rows)[0]
    grad_field = (hidden_grad.astype(jnp.float32).reshape(NLAT, NLON, C) + adjoint).astype(jnp.bfloat16)
    return (block_out.reshape(NLAT, NLON, C), grad_field, grad_mix, grad_up, grad_down)
```

```python
import math

import jax
import jax.numpy as jnp
from jax import lax
from jax.sharding import PartitionSpec as P

inv_root_two = 0.7071067811865476
inv_root_tau = 0.3989422804014327
AXES = ("lat", "lon")


def gelu_exact(value):
    return 0.5 * value * (1.0 + jax.scipy.special.erf(value * inv_root_two))


def gelu_slope(value):
    return (
        0.5 * (1.0 + jax.scipy.special.erf(value * inv_root_two))
        + value * jnp.exp(-0.5 * value * value) * inv_root_tau
    )


class Place:
    def __init__(self):
        self.lats = lax.axis_size("lat")
        self.lons = lax.axis_size("lon")
        self.count = self.lats * self.lons
        self.lat = lax.axis_index("lat")
        self.lon = lax.axis_index("lon")
        self.flat = self.lat * self.lons + self.lon
        lats, lons = self.lats, self.lons
        self.east = [(i, (i + 1) % lons) for i in range(lons)]
        self.west = [(j, i) for i, j in self.east]
        self.pairs = [
            (r * lons + c, (r ^ 1) * lons + c) for r in range(lats) for c in range(lons)
        ]
        self.bridges = []
        for r in range(lats):
            other = r - 1 if r % 2 == 0 else r + 1
            for c in range(lons):
                if 0 <= other < lats:
                    self.bridges.append((r * lons + c, other * lons + c))
                else:
                    self.bridges.append((r * lons + c, r * lons + (c + lons // 2) % lons))
        self.even = self.lat % 2 == 0


def flip_route(place, mask_of):
    return [(i, i ^ mask_of(i)) for i in range(place.count)]


def pick(array, index, axis):
    return lax.dynamic_index_in_dim(array, index, axis, keepdims=False)


def reduce_to_owner(place, partial):
    low = jnp.bfloat16
    count, rows, channels = partial.shape
    core = place.flat % 2
    buf = partial.reshape(count // 2, 2, rows, channels)
    got = lax.ppermute(pick(buf, 1 - core, 1).astype(low), AXES, flip_route(place, lambda i: 1))
    buf = pick(buf, core, 1) + got.astype(jnp.float32)

    quad = (place.flat // 2) % 4
    first = jnp.where(core == 0, 1, 2)
    second = 3 - first
    buf = buf.reshape(count // 8, 4, rows, channels)
    send = jnp.stack([pick(buf, quad ^ first, 1), pick(buf, quad ^ 3, 1)], axis=1)
    got = lax.ppermute(
        send.astype(low), AXES, flip_route(place, lambda i: 2 if i % 2 == 0 else 4)
    ).astype(jnp.float32)
    keep = pick(buf, quad, 1) + got[:, 0]
    send = pick(buf, quad ^ second, 1) + got[:, 1]
    got = lax.ppermute(
        send.astype(low), AXES, flip_route(place, lambda i: 4 if i % 2 == 0 else 2)
    )
    buf = keep + got.astype(jnp.float32)

    bit = 8
    while bit < count:
        mine = (place.flat // bit) % 2
        buf = buf.reshape(buf.shape[0] // 2, 2, rows, channels)
        send = pick(buf, 1 - mine, 1).astype(low)
        got = lax.ppermute(send, AXES, flip_route(place, lambda i, bit=bit: bit))
        buf = pick(buf, mine, 1) + got.astype(jnp.float32)
        bit *= 2
    return buf[0]


def local(field_in, kernel_taps, row_reach, mix_weight, up_weight, down_weight, cotangent):
    lat_rows, lon_cols, channels = field_in.shape
    basis_count = kernel_taps.shape[0]
    tap_count = kernel_taps.shape[3]
    reach = (tap_count - 1) // 2
    hidden_units = up_weight.shape[1]
    place = Place()

    west = lax.ppermute(field_in[:, lon_cols - reach :], "lon", place.east)
    east = lax.ppermute(field_in[:, :reach], "lon", place.west)
    top, bottom = field_in[0], field_in[lat_rows - 1]
    inner = lax.ppermute(jnp.where(place.even, bottom, top), AXES, place.pairs)
    outer = lax.ppermute(jnp.where(place.even, top, bottom), AXES, place.bridges)
    north = jnp.where(place.even, outer, inner)
    south = jnp.where(place.even, inner, outer)
    rims = jnp.stack([north, south])
    rims_west = lax.ppermute(rims[:, lon_cols - reach :], "lon", place.east)
    rims_east = lax.ppermute(rims[:, :reach], "lon", place.west)
    extended = jnp.concatenate(
        [
            jnp.concatenate([rims_west[:1], rims[:1], rims_east[:1]], axis=1),
            jnp.concatenate([west, field_in, east], axis=1),
            jnp.concatenate([rims_west[1:], rims[1:], rims_east[1:]], axis=1),
        ],
        axis=0,
    )

    padded_width = lon_cols + 2 * reach
    offsets = jnp.arange(tap_count, dtype=jnp.int32) - reach
    tap_mask = jnp.abs(offsets)[None, :] <= row_reach[:, None]
    masked_taps = jnp.where(
        tap_mask[None, :, None, :], kernel_taps, jnp.zeros((), kernel_taps.dtype)
    )
    selector = (
        jnp.arange(padded_width, dtype=jnp.int32)[None, :, None]
        - jnp.arange(lon_cols, dtype=jnp.int32)[:, None, None]
        == jnp.arange(tap_count, dtype=jnp.int32)[None, None, :]
    ).astype(jnp.bfloat16)
    band_matrix = jnp.einsum(
        "krdt,jat->krjda", masked_taps, selector, preferred_element_type=jnp.float32
    ).astype(jnp.bfloat16)
    windows = jnp.stack(
        [extended[0:lat_rows], extended[1 : lat_rows + 1], extended[2 : lat_rows + 2]], axis=1
    )
    features = jnp.einsum(
        "krjda,rdac->krjc", band_matrix, windows, preferred_element_type=jnp.float32
    ).astype(jnp.bfloat16)
    points = lat_rows * lon_cols
    flat_features = features.reshape(basis_count, points, channels)
    flat_field = field_in.reshape(points, channels)
    conv_sum = jnp.einsum(
        "kpc,kcd->pd", flat_features, mix_weight, preferred_element_type=jnp.float32
    )
    hidden = (flat_field.astype(jnp.float32) + conv_sum).astype(jnp.bfloat16)
    pre_act = jnp.dot(hidden, up_weight, preferred_element_type=jnp.float32)
    activated = gelu_exact(pre_act).astype(jnp.bfloat16)
    grad_rows = cotangent.reshape(points, channels)
    act_grad = lax.dot_general(
        grad_rows, down_weight, (((1,), (1,)), ((), ())), preferred_element_type=jnp.float32
    )
    pre_grad = (act_grad * gelu_slope(pre_act)).astype(jnp.bfloat16)

    over_points = (((0,), (0,)), ((), ()))
    down_local = lax.dot_general(
        activated, grad_rows, over_points, preferred_element_type=jnp.float32
    )
    up_local = lax.dot_general(
        pre_grad, hidden, over_points, preferred_element_type=jnp.float32
    )
    mlp_local = jnp.concatenate(
        [down_local, up_local], axis=0
    ).reshape(place.count, -1, channels)
    mlp_own = reduce_to_owner(place, mlp_local)

    hidden_grad = (
        grad_rows.astype(jnp.float32)
        + lax.dot_general(
            pre_grad, up_weight, (((1,), (1,)), ((), ())), preferred_element_type=jnp.float32
        )
    ).astype(jnp.bfloat16)
    mix_local = jnp.einsum(
        "kpc,pd->kcd", flat_features, hidden_grad, preferred_element_type=jnp.float32
    )
    mix_own = reduce_to_owner(place, mix_local.reshape(place.count, -1, channels))

    grad_scale = 1.0 / math.sqrt(points * place.count)
    mlp_all = lax.all_gather(
        (mlp_own * grad_scale).astype(jnp.bfloat16), AXES, axis=0, tiled=True
    )
    mix_all = lax.all_gather(
        (mix_own * grad_scale).astype(jnp.bfloat16), AXES, axis=0, tiled=True
    )
    down_out = mlp_all[:hidden_units]
    up_out = mlp_all[hidden_units:].T
    mix_out = mix_all.reshape(mix_weight.shape)

    block_out = (
        hidden.astype(jnp.float32)
        + jnp.dot(activated, down_weight, preferred_element_type=jnp.float32)
    ).astype(jnp.bfloat16)

    feat_grad = jnp.einsum(
        "pd,kcd->kpc", hidden_grad, mix_weight, preferred_element_type=jnp.float32
    ).astype(jnp.bfloat16)
    feat_grad_rows = feat_grad.reshape(basis_count, lat_rows, lon_cols, channels)
    spread = jnp.einsum(
        "krjda,krjc->rdac", band_matrix, feat_grad_rows, preferred_element_type=jnp.float32
    )
    pulled = (
        jnp.pad(spread[:, 0], ((0, 2), (0, 0), (0, 0)))
        + jnp.pad(spread[:, 1], ((1, 1), (0, 0), (0, 0)))
        + jnp.pad(spread[:, 2], ((2, 0), (0, 0), (0, 0)))
    )
    low = jnp.bfloat16
    edge_rows = jnp.stack([pulled[0], pulled[lat_rows + 1]])
    from_east = lax.ppermute(edge_rows[:, :reach].astype(low), "lon", place.west)
    from_west = lax.ppermute(edge_rows[:, lon_cols + reach :].astype(low), "lon", place.east)
    rims = edge_rows[:, reach : reach + lon_cols]
    rims = rims.at[:, lon_cols - reach :].add(from_east.astype(jnp.float32))
    rims = rims.at[:, :reach].add(from_west.astype(jnp.float32)).astype(low)
    inner = lax.ppermute(jnp.where(place.even, rims[1], rims[0]), AXES, place.pairs)
    outer = lax.ppermute(jnp.where(place.even, rims[0], rims[1]), AXES, place.bridges)
    body = pulled[1 : lat_rows + 1]
    from_east = lax.ppermute(body[:, :reach].astype(low), "lon", place.west)
    from_west = lax.ppermute(body[:, lon_cols + reach :].astype(low), "lon", place.east)
    adjoint = body[:, reach : reach + lon_cols]
    adjoint = adjoint.at[:, lon_cols - reach :].add(from_east.astype(jnp.float32))
    adjoint = adjoint.at[:, :reach].add(from_west.astype(jnp.float32))
    adjoint = adjoint.at[0].add(jnp.where(place.even, outer, inner).astype(jnp.float32))
    adjoint = adjoint.at[lat_rows - 1].add(
        jnp.where(place.even, inner, outer).astype(jnp.float32)
    )
    grad_field = (
        hidden_grad.astype(jnp.float32).reshape(lat_rows, lon_cols, channels) + adjoint
    ).astype(jnp.bfloat16)
    return (block_out.reshape(lat_rows, lon_cols, channels), grad_field, mix_out, up_out, down_out)


def solution(mesh):
    placed = (
        P("lat", "lon", None),
        P(None, "lat", None, None),
        P("lat"),
        P(),
        P(),
        P(),
        P("lat", "lon", None),
    )
    return jax.shard_map(
        local,
        mesh=mesh,
        in_specs=placed,
        out_specs=(P("lat", "lon", None), P("lat", "lon", None), P(), P(), P()),
        check_vma=False,
    )
```

```python
import functools
import math

import jax
import jax.numpy as jnp
from jax import lax
from jax.experimental import pallas as pl
from jax.experimental.pallas import tpu as pltpu
from jax.sharding import PartitionSpec as P

inv_root_two = 0.7071067811865476
inv_root_tau = 0.3989422804014327
AXES = ("lat", "lon")


def gelu_exact(value):
    return 0.5 * value * (1.0 + jax.scipy.special.erf(value * inv_root_two))


def gelu_slope(value):
    return (
        0.5 * (1.0 + jax.scipy.special.erf(value * inv_root_two))
        + value * jnp.exp(-0.5 * value * value) * inv_root_tau
    )


class Place:
    def __init__(self):
        self.lats = lax.axis_size("lat")
        self.lons = lax.axis_size("lon")
        self.count = self.lats * self.lons
        self.lat = lax.axis_index("lat")
        self.lon = lax.axis_index("lon")
        self.flat = self.lat * self.lons + self.lon
        lats, lons = self.lats, self.lons
        self.east = [(i, (i + 1) % lons) for i in range(lons)]
        self.west = [(j, i) for i, j in self.east]
        self.pairs = [
            (r * lons + c, (r ^ 1) * lons + c) for r in range(lats) for c in range(lons)
        ]
        self.bridges = []
        for r in range(lats):
            other = r - 1 if r % 2 == 0 else r + 1
            for c in range(lons):
                if 0 <= other < lats:
                    self.bridges.append((r * lons + c, other * lons + c))
                else:
                    self.bridges.append((r * lons + c, r * lons + (c + lons // 2) % lons))
        self.even = self.lat % 2 == 0


def route(place, mask_of):
    return [(i, i ^ mask_of(i)) for i in range(place.count)]


def send_along(place, block, mask_of):
    return lax.ppermute(block, AXES, route(place, mask_of))


def first_mask(i):
    return 2 if i % 2 == 0 else 4


def second_mask(i):
    return 4 if i % 2 == 0 else 2


def pick(array, index):
    return lax.dynamic_index_in_dim(array, index, 0, keepdims=False)


class Ring:
    def __init__(self, place):
        self.place = place
        self.core = place.flat % 2
        self.quad = (place.flat // 2) % 4
        self.z = place.flat // 8
        self.first = 1 + self.core
        self.second = 2 - self.core

    def scatter(self, keep, send):
        low, place = jnp.bfloat16, self.place
        buf = keep + send_along(place, send, lambda i: 1).astype(jnp.float32)
        out = jnp.stack([pick(buf, self.quad ^ self.first), pick(buf, self.quad ^ 3)])
        got = send_along(place, out.astype(low), first_mask).astype(jnp.float32)
        keep = pick(buf, self.quad) + got[0]
        out = pick(buf, self.quad ^ self.second) + got[1]
        buf = keep + send_along(place, out.astype(low), second_mask).astype(jnp.float32)
        total = pick(buf, self.z)
        for m in (1, 2, 3):
            out = pick(buf, self.z ^ m).astype(low)
            total = total + send_along(place, out, lambda i, m=m: m * 8).astype(jnp.float32)
        return total

    def gather(self, piece):
        place = self.place
        buf = jnp.stack(
            [piece] + [send_along(place, piece, lambda i, m=m: m * 8) for m in (1, 2, 3)]
        )
        buf = jnp.concatenate([buf, send_along(place, buf, second_mask)])
        buf = jnp.concatenate([buf, send_along(place, buf, first_mask)])
        return buf, send_along(place, buf, lambda i: 1)

    def order(self):
        mask = jnp.arange(4, dtype=jnp.int32) ^ self.quad
        rest = jnp.arange(4, dtype=jnp.int32) ^ self.z
        low, high = mask % 2, mask // 2
        by_y = (low * 2 + high)[:, None] * 4 + rest[None, :]
        by_x = (high * 2 + low)[:, None] * 4 + rest[None, :]
        both = jnp.stack([by_y.reshape(16), by_x.reshape(16)])
        return jnp.concatenate([both, jnp.full((1, 16), self.core, jnp.int32)])


def assemble_kernel(order, own, other, *refs, places):
    outs, sems = refs[:-1], refs[-1]
    core = order[2, 0]

    def copies(half, chunk):
        out, where = places(half, chunk)
        source = order[half, chunk]
        target = outs[out].at[where]
        sem = sems.at[half * 16 + chunk]
        return (
            pltpu.make_async_copy(own.at[source], target, sem),
            pltpu.make_async_copy(other.at[source], target, sem),
        )

    for half in range(2):
        for chunk in range(16):
            mine, theirs = copies(half, chunk)
            pl.when(core == half)(mine.start)
            pl.when(core != half)(theirs.start)
    for half in range(2):
        for chunk in range(16):
            copies(half, chunk)[0].wait()


def assemble(order, own, other, shapes, places):
    anywhere = pl.BlockSpec(memory_space=pl.ANY)
    return pl.pallas_call(
        functools.partial(assemble_kernel, places=places),
        out_shape=[jax.ShapeDtypeStruct(shape, jnp.bfloat16) for shape in shapes],
        in_specs=[pl.BlockSpec(memory_space=pltpu.SMEM), anywhere, anywhere],
        out_specs=[anywhere] * len(shapes),
        scratch_shapes=[pltpu.SemaphoreType.DMA((32,))],
        cost_estimate=pl.CostEstimate(
            flops=0, bytes_accessed=4 * own.size * 2, transcendentals=0
        ),
    )(order, own, other)


def local(field_in, kernel_taps, row_reach, mix_weight, up_weight, down_weight, cotangent):
    lat_rows, lon_cols, channels = field_in.shape
    basis_count = kernel_taps.shape[0]
    tap_count = kernel_taps.shape[3]
    reach = (tap_count - 1) // 2
    hidden_units = up_weight.shape[1]
    place = Place()

    west = lax.ppermute(field_in[:, lon_cols - reach :], "lon", place.east)
    east = lax.ppermute(field_in[:, :reach], "lon", place.west)
    top, bottom = field_in[0], field_in[lat_rows - 1]
    inner = lax.ppermute(jnp.where(place.even, bottom, top), AXES, place.pairs)
    outer = lax.ppermute(jnp.where(place.even, top, bottom), AXES, place.bridges)
    north = jnp.where(place.even, outer, inner)
    south = jnp.where(place.even, inner, outer)
    rims = jnp.stack([north, south])
    rims_west = lax.ppermute(rims[:, lon_cols - reach :], "lon", place.east)
    rims_east = lax.ppermute(rims[:, :reach], "lon", place.west)
    extended = jnp.concatenate(
        [
            jnp.concatenate([rims_west[:1], rims[:1], rims_east[:1]], axis=1),
            jnp.concatenate([west, field_in, east], axis=1),
            jnp.concatenate([rims_west[1:], rims[1:], rims_east[1:]], axis=1),
        ],
        axis=0,
    )

    padded_width = lon_cols + 2 * reach
    offsets = jnp.arange(tap_count, dtype=jnp.int32) - reach
    tap_mask = jnp.abs(offsets)[None, :] <= row_reach[:, None]
    masked_taps = jnp.where(
        tap_mask[None, :, None, :], kernel_taps, jnp.zeros((), kernel_taps.dtype)
    )
    selector = (
        jnp.arange(padded_width, dtype=jnp.int32)[None, :, None]
        - jnp.arange(lon_cols, dtype=jnp.int32)[:, None, None]
        == jnp.arange(tap_count, dtype=jnp.int32)[None, None, :]
    ).astype(jnp.bfloat16)
    band_matrix = jnp.einsum(
        "krdt,jat->krjda", masked_taps, selector, preferred_element_type=jnp.float32
    ).astype(jnp.bfloat16)
    windows = jnp.stack(
        [extended[0:lat_rows], extended[1 : lat_rows + 1], extended[2 : lat_rows + 2]], axis=1
    )
    features = jnp.einsum(
        "krjda,rdac->krjc", band_matrix, windows, preferred_element_type=jnp.float32
    ).astype(jnp.bfloat16)
    points = lat_rows * lon_cols
    flat_features = features.reshape(basis_count, points, channels)
    flat_field = field_in.reshape(points, channels)
    conv_sum = jnp.einsum(
        "kpc,kcd->pd", flat_features, mix_weight, preferred_element_type=jnp.float32
    )
    hidden = (flat_field.astype(jnp.float32) + conv_sum).astype(jnp.bfloat16)
    pre_act = jnp.dot(hidden, up_weight, preferred_element_type=jnp.float32)
    activated = gelu_exact(pre_act).astype(jnp.bfloat16)
    grad_rows = cotangent.reshape(points, channels)
    act_grad = lax.dot_general(
        grad_rows, down_weight, (((1,), (1,)), ((), ())), preferred_element_type=jnp.float32
    )
    pre_grad = (act_grad * gelu_slope(pre_act)).astype(jnp.bfloat16)

    over_points = (((0,), (0,)), ((), ()))

    def summed(left, right):
        return lax.dot_general(left, right, over_points, preferred_element_type=jnp.float32)

    hidden_grad = (
        grad_rows.astype(jnp.float32)
        + lax.dot_general(
            pre_grad, up_weight, (((1,), (1,)), ((), ())), preferred_element_type=jnp.float32
        )
    ).astype(jnp.bfloat16)
    grad_scale = 1.0 / math.sqrt(points * place.count)
    if place.count == 32:
        ring = Ring(place)
        half_units, half_channels = hidden_units // 2, channels // 2

        def mlp_half(half):
            start = half * half_units
            act = lax.dynamic_slice_in_dim(activated, start, half_units, 1)
            pre = lax.dynamic_slice_in_dim(pre_grad, start, half_units, 1)
            return jnp.concatenate([summed(act, grad_rows), summed(hidden, pre)])

        def mix_half(half):
            part = lax.dynamic_slice_in_dim(flat_features, half * half_channels, half_channels, 2)
            return jnp.stack(
                [summed(part[k], hidden_grad).reshape(16, -1, channels) for k in range(basis_count)],
                axis=1,
            )

        def exchanged(half_of, shape):
            send = half_of(1 - ring.core).astype(jnp.bfloat16).reshape(shape)
            return ring.scatter(half_of(ring.core).reshape(shape), send)

        mlp_rows = (half_units + channels) // 16
        mlp_own = exchanged(mlp_half, (4, 4, mlp_rows, channels))
        mix_own = exchanged(mix_half, (4, 4, basis_count, half_channels // 16, channels))
        mlp_all = ring.gather((mlp_own * grad_scale).astype(jnp.bfloat16))
        mix_all = ring.gather((mix_own * grad_scale).astype(jnp.bfloat16))
        order = ring.order()

        def mlp_place(half, chunk):
            if chunk < 8:
                return 0, (pl.ds(half * half_units + chunk * mlp_rows, mlp_rows),)
            return 1, (
                pl.ds((chunk - 8) * mlp_rows, mlp_rows),
                pl.ds(half * half_units, half_units),
            )

        def mix_place(half, chunk):
            rows = half_channels // 16
            return 0, (slice(None), pl.ds(half * half_channels + chunk * rows, rows))

        down_out, up_out = assemble(
            order, *mlp_all, (down_weight.shape, up_weight.shape), mlp_place
        )
        (mix_out,) = assemble(order, *mix_all, (mix_weight.shape,), mix_place)
    else:
        mix_local = jnp.einsum(
            "kpc,pd->kcd", flat_features, hidden_grad, preferred_element_type=jnp.float32
        )
        totals = lax.psum(
            (mix_local, summed(hidden, pre_grad), summed(activated, grad_rows)), AXES
        )
        mix_out, up_out, down_out = [(t * grad_scale).astype(jnp.bfloat16) for t in totals]

    block_out = (
        hidden.astype(jnp.float32)
        + jnp.dot(activated, down_weight, preferred_element_type=jnp.float32)
    ).astype(jnp.bfloat16)

    feat_grad = jnp.einsum(
        "pd,kcd->kpc", hidden_grad, mix_weight, preferred_element_type=jnp.float32
    ).astype(jnp.bfloat16)
    feat_grad_rows = feat_grad.reshape(basis_count, lat_rows, lon_cols, channels)
    spread = jnp.einsum(
        "krjda,krjc->rdac", band_matrix, feat_grad_rows, preferred_element_type=jnp.float32
    )
    pulled = (
        jnp.pad(spread[:, 0], ((0, 2), (0, 0), (0, 0)))
        + jnp.pad(spread[:, 1], ((1, 1), (0, 0), (0, 0)))
        + jnp.pad(spread[:, 2], ((2, 0), (0, 0), (0, 0)))
    )
    low = jnp.bfloat16
    edge_rows = jnp.stack([pulled[0], pulled[lat_rows + 1]])
    from_east = lax.ppermute(edge_rows[:, :reach].astype(low), "lon", place.west)
    from_west = lax.ppermute(edge_rows[:, lon_cols + reach :].astype(low), "lon", place.east)
    rims = edge_rows[:, reach : reach + lon_cols]
    rims = rims.at[:, lon_cols - reach :].add(from_east.astype(jnp.float32))
    rims = rims.at[:, :reach].add(from_west.astype(jnp.float32)).astype(low)
    inner = lax.ppermute(jnp.where(place.even, rims[1], rims[0]), AXES, place.pairs)
    outer = lax.ppermute(jnp.where(place.even, rims[0], rims[1]), AXES, place.bridges)
    body = pulled[1 : lat_rows + 1]
    from_east = lax.ppermute(body[:, :reach].astype(low), "lon", place.west)
    from_west = lax.ppermute(body[:, lon_cols + reach :].astype(low), "lon", place.east)
    adjoint = body[:, reach : reach + lon_cols]
    adjoint = adjoint.at[:, lon_cols - reach :].add(from_east.astype(jnp.float32))
    adjoint = adjoint.at[:, :reach].add(from_west.astype(jnp.float32))
    adjoint = adjoint.at[0].add(jnp.where(place.even, outer, inner).astype(jnp.float32))
    adjoint = adjoint.at[lat_rows - 1].add(
        jnp.where(place.even, inner, outer).astype(jnp.float32)
    )
    grad_field = (
        hidden_grad.astype(jnp.float32).reshape(lat_rows, lon_cols, channels) + adjoint
    ).astype(jnp.bfloat16)
    return (block_out.reshape(lat_rows, lon_cols, channels), grad_field, mix_out, up_out, down_out)


def solution(mesh):
    placed = (
        P("lat", "lon", None),
        P(None, "lat", None, None),
        P("lat"),
        P(),
        P(),
        P(),
        P("lat", "lon", None),
    )
    return jax.shard_map(
        local,
        mesh=mesh,
        in_specs=placed,
        out_specs=(P("lat", "lon", None), P("lat", "lon", None), P(), P(), P()),
        check_vma=False,
    )
```

```python
import functools
import math

import jax
import jax.numpy as jnp
from jax import lax
from jax.experimental import pallas as pl
from jax.experimental.pallas import tpu as pltpu
from jax.sharding import PartitionSpec as P

inv_root_two = 0.7071067811865476
inv_root_tau = 0.3989422804014327
AXES = ("lat", "lon")


class Place:
    def __init__(self):
        self.lats = lax.axis_size("lat")
        self.lons = lax.axis_size("lon")
        self.count = self.lats * self.lons
        self.lat = lax.axis_index("lat")
        self.lon = lax.axis_index("lon")
        self.flat = self.lat * self.lons + self.lon
        lats, lons = self.lats, self.lons
        self.east = [(i, (i + 1) % lons) for i in range(lons)]
        self.west = [(j, i) for i, j in self.east]
        self.pairs = [
            (r * lons + c, (r ^ 1) * lons + c) for r in range(lats) for c in range(lons)
        ]
        self.bridges = []
        for r in range(lats):
            other = r - 1 if r % 2 == 0 else r + 1
            for c in range(lons):
                if 0 <= other < lats:
                    self.bridges.append((r * lons + c, other * lons + c))
                else:
                    self.bridges.append((r * lons + c, r * lons + (c + lons // 2) % lons))
        self.even = self.lat % 2 == 0


def route(place, mask_of):
    return [(i, i ^ mask_of(i)) for i in range(place.count)]


def send_along(place, block, mask_of):
    return lax.ppermute(block, AXES, route(place, mask_of))


def first_mask(i):
    return 2 if i % 2 == 0 else 4


def second_mask(i):
    return 4 if i % 2 == 0 else 2


def pick(array, index):
    return lax.dynamic_index_in_dim(array, index, 0, keepdims=False)


class Ring:
    def __init__(self, place):
        self.place = place
        self.core = place.flat % 2
        self.quad = (place.flat // 2) % 4
        self.z = place.flat // 8
        self.first = 1 + self.core
        self.second = 2 - self.core

    def scatter(self, keep, send):
        low, place = jnp.bfloat16, self.place
        buf = keep + send_along(place, send, lambda i: 1).astype(jnp.float32)
        out = jnp.stack([pick(buf, self.quad ^ self.first), pick(buf, self.quad ^ 3)])
        got = send_along(place, out.astype(low), first_mask).astype(jnp.float32)
        keep = pick(buf, self.quad) + got[0]
        out = pick(buf, self.quad ^ self.second) + got[1]
        buf = keep + send_along(place, out.astype(low), second_mask).astype(jnp.float32)
        near = self.z % 2
        out = pick(buf, 1 - near).astype(low)
        buf = pick(buf, near) + send_along(place, out, lambda i: 8).astype(jnp.float32)
        own = buf.astype(low)
        far = send_along(place, own, lambda i: 16)
        return own.astype(jnp.float32) + far.astype(jnp.float32)

    def gather(self, piece):
        place = self.place
        buf = piece[None]
        for mask_of in (lambda i: 8, second_mask, first_mask):
            buf = jnp.concatenate([buf, send_along(place, buf, mask_of)])
        return buf, send_along(place, buf, lambda i: 1)

    def order(self):
        mask = jnp.arange(4, dtype=jnp.int32) ^ self.quad
        near = jnp.arange(2, dtype=jnp.int32) ^ (self.z % 2)
        low, high = mask % 2, mask // 2
        by_y = (low * 2 + high)[:, None] * 2 + near[None, :]
        by_x = (high * 2 + low)[:, None] * 2 + near[None, :]
        both = jnp.concatenate([by_y.reshape(8), by_x.reshape(8)])
        return jnp.concatenate([both, self.core[None].astype(jnp.int32)])


def assemble_kernel(order, own, other, *outs, places):
    core = order[16]

    def place_half(half, source):
        for chunk in range(8):
            out, where = places(half, chunk)
            outs[out][where] = source[order[half * 8 + chunk]]

    for half in range(2):
        pl.when(core == half)(functools.partial(place_half, half, own))
        pl.when(core != half)(functools.partial(place_half, half, other))


def assemble(order, own, other, shapes, places):
    whole = pl.BlockSpec(memory_space=pltpu.VMEM)
    return pl.pallas_call(
        functools.partial(assemble_kernel, places=places),
        out_shape=[jax.ShapeDtypeStruct(shape, jnp.bfloat16) for shape in shapes],
        in_specs=[pl.BlockSpec(memory_space=pltpu.SMEM), whole, whole],
        out_specs=[whole] * len(shapes),
        compiler_params=pltpu.CompilerParams(vmem_limit_bytes=VMEM_LIMIT),
        cost_estimate=pl.CostEstimate(
            flops=0, bytes_accessed=4 * own.size * 2, transcendentals=0
        ),
    )(order, own, other)


OVER_ROWS = (((0,), (0,)), ((), ()))
OVER_LANES = (((1,), (1,)), ((), ()))
VMEM_LIMIT = 56 * 1024 * 1024


def dot(left, right, dims=(((1,), (0,)), ((), ()))):
    return lax.dot_general(left, right, dims, preferred_element_type=jnp.float32)


def tiles(count, size, body):
    def step(i, carry):
        body(pl.ds(pl.multiple_of(i * size, size), size))
        return carry

    lax.fori_loop(0, count // size, step, 0)


def before_kernel(taps, cot, down, ag, bands, *, rows, cols, tile):
    basis, width = taps.shape[0], taps.shape[3]

    def one_row(r, carry):
        for k in range(basis):
            for d in range(3):
                line = jnp.broadcast_to(taps[k, r, pl.ds(d, 1)], (cols, width))
                band = pltpu.roll(line, 0, 1, stride=1, stride_axis=0)
                bands[r, k * cols : (k + 1) * cols, d * width : (d + 1) * width] = band.astype(
                    bands.dtype
                )
        return carry

    lax.fori_loop(0, rows, one_row, 0)

    def product(at):
        ag[at, :] = dot(cot[at, :], down[...], OVER_LANES)

    tiles(rows * cols, tile, product)


def main_kernel(
    core_ref, field, west, east, north, south, rims_west, rims_east, bands_in, mix_in, up_in,
    cot_in, ag_in,
    hidden_out, act_out, hg_out, mlp_send, mlp_keep, mix_send, mix_keep,
    ext, bands, mix, up, cot, ag, feats, hidden, act, pre_grad, hg, sems, *, tile
):
    core = core_ref[0]
    rows, cols, channels = field.shape
    reach = west.shape[1]
    basis = mix.shape[0]
    points = rows * cols
    units = up.shape[1]
    half_units, half_channels = units // 2, channels // 2
    body, inner = pl.ds(1, rows), pl.ds(reach, cols)
    begin, end = pl.ds(0, reach), pl.ds(reach + cols, reach)
    loads = [
        (field, ext.at[body, inner]),
        (west, ext.at[body, begin]),
        (east, ext.at[body, end]),
        (north, ext.at[0, inner]),
        (south, ext.at[rows + 1, inner]),
        (rims_west.at[0], ext.at[0, begin]),
        (rims_west.at[1], ext.at[rows + 1, begin]),
        (rims_east.at[0], ext.at[0, end]),
        (rims_east.at[1], ext.at[rows + 1, end]),
        (bands_in, bands),
        (mix_in, mix),
        (up_in, up),
        (ag_in, ag),
        (cot_in, cot),
    ]
    loads = [pltpu.make_async_copy(a, b, sems.at[i]) for i, (a, b) in enumerate(loads)]
    for load in loads:
        load.start()
    for load in loads[:10]:
        load.wait()

    def one_row(r, carry):
        window = ext[pl.ds(r, 3)].reshape(3 * ext.shape[1], channels)
        out = dot(bands[r], window).astype(feats.dtype)
        at = pl.ds(pl.multiple_of(r * cols, cols), cols)
        for k in range(basis):
            feats[k, at, :] = out[k * cols : (k + 1) * cols]
        hidden[at, :] = ext[r + 1, inner, :]
        return carry

    lax.fori_loop(0, rows, one_row, 0)
    loads[10].wait()

    def mixing(at):
        total = hidden[at, :].astype(jnp.float32)
        for k in range(basis):
            total = total + dot(feats[k, at, :], mix[k])
        hidden[at, :] = total.astype(hidden.dtype)

    tiles(points, tile, mixing)
    loads[11].wait()
    loads[12].wait()

    def mlp(at):
        value = dot(hidden[at, :], up[...])
        phi = 0.5 * (1.0 + lax.erf(value * inv_root_two))
        act[at, :] = (value * phi).astype(act.dtype)
        slope = phi + value * jnp.exp(-0.5 * value * value) * inv_root_tau
        pre_grad[at, :] = (ag[at, :] * slope).astype(pre_grad.dtype)

    tiles(points, tile // 2, mlp)
    loads[13].wait()
    stores = [
        pltpu.make_async_copy(hidden, hidden_out, sems.at[14]),
        pltpu.make_async_copy(act, act_out, sems.at[15]),
    ]
    for store in stores:
        store.start()

    def mlp_sums(half, out):
        at = pl.ds(pl.multiple_of(half * half_units, half_units), half_units)
        out[:half_units] = dot(act[:, at], cot[...], OVER_ROWS).astype(out.dtype)
        out[half_units:] = dot(hidden[...], pre_grad[:, at], OVER_ROWS).astype(out.dtype)

    mlp_sums(1 - core, mlp_send)
    mlp_sums(core, mlp_keep)

    def back(at):
        total = cot[at, :].astype(jnp.float32) + dot(pre_grad[at, :], up[...], OVER_LANES)
        hg[at, :] = total.astype(hg.dtype)

    tiles(points, tile, back)
    stores.append(pltpu.make_async_copy(hg, hg_out, sems.at[16]))
    stores[-1].start()

    def mix_sums(half, out):
        at = pl.ds(pl.multiple_of(half * half_channels, half_channels), half_channels)
        for k in range(basis):
            part = dot(feats[k, :, at], hg[...], OVER_ROWS).astype(out.dtype)
            out[:, k] = part.reshape(out.shape[0], -1, channels)

    mix_sums(1 - core, mix_send)
    mix_sums(core, mix_keep)
    for store in stores:
        store.wait()


def after_kernel(
    hidden_in, act_in, down_in, hg_in, mix_in, bands_in,
    block, inner_out, rim_out, corner_west, corner_east, side_west, side_east,
    hidden, act, down, hg, mix, bands, grads, pulled, sems, *, rows, cols, tile
):
    basis, channels = mix.shape[0], mix.shape[1]
    width = pulled.shape[1]
    reach = (width - cols) // 2
    loads = [(mix_in, mix), (hg_in, hg), (bands_in, bands), (act_in, act), (down_in, down),
             (hidden_in, hidden)]
    loads = [pltpu.make_async_copy(a, b, sems.at[i]) for i, (a, b) in enumerate(loads)]
    for load in loads:
        load.start()
    pulled[...] = jnp.zeros(pulled.shape, pulled.dtype)
    loads[0].wait()
    loads[1].wait()
    group = 5 if rows % 5 == 0 else 1

    def feature_grads(i, carry):
        at = pl.ds(pl.multiple_of(i * group * cols, group * cols), group * cols)
        for k in range(basis):
            part = dot(hg[at, :], mix[k], OVER_LANES).astype(grads.dtype)
            grads[pl.ds(i * group, group), pl.ds(k * cols, cols)] = part.reshape(
                group, cols, channels
            )
        return carry

    lax.fori_loop(0, rows // group, feature_grads, 0)
    loads[2].wait()

    def one_row(r, carry):
        part = dot(bands[r], grads[r], OVER_ROWS)
        pulled[pl.ds(r, 3)] += part.reshape(3, width, channels)
        return carry

    lax.fori_loop(0, rows, one_row, 0)
    low = jnp.bfloat16
    inner_out[...] = pulled[1 : rows + 1, reach : reach + cols]
    side_west[...] = pulled[1 : rows + 1, :reach].astype(low)
    side_east[...] = pulled[1 : rows + 1, reach + cols :].astype(low)
    for n, r in enumerate((0, rows + 1)):
        rim_out[n] = pulled[r, reach : reach + cols]
        corner_west[n] = pulled[r, :reach].astype(low)
        corner_east[n] = pulled[r, reach + cols :].astype(low)
    for load in loads[3:]:
        load.wait()

    def forward(at):
        total = hidden[at, :].astype(jnp.float32) + dot(act[at, :], down[...])
        block[at, :] = total.astype(block.dtype)

    tiles(rows * cols, tile, forward)


def call(kernel, operands, kinds, shapes, out_kinds, scratch, flops, nbytes):
    return pl.pallas_call(
        kernel,
        out_shape=[jax.ShapeDtypeStruct(shape, kind) for shape, kind in shapes],
        in_specs=[pl.BlockSpec(memory_space=kind) for kind in kinds],
        out_specs=[pl.BlockSpec(memory_space=kind) for kind in out_kinds],
        scratch_shapes=scratch,
        compiler_params=pltpu.CompilerParams(vmem_limit_bytes=VMEM_LIMIT),
        cost_estimate=pl.CostEstimate(flops=flops, bytes_accessed=nbytes, transcendentals=0),
    )(*operands)


def local(field_in, kernel_taps, row_reach, mix_weight, up_weight, down_weight, cotangent):
    lat_rows, lon_cols, channels = field_in.shape
    basis_count = kernel_taps.shape[0]
    tap_count = kernel_taps.shape[3]
    reach = (tap_count - 1) // 2
    hidden_units = up_weight.shape[1]
    place = Place()

    west = lax.ppermute(field_in[:, lon_cols - reach :], "lon", place.east)
    east = lax.ppermute(field_in[:, :reach], "lon", place.west)
    top, bottom = field_in[0], field_in[lat_rows - 1]
    inner = lax.ppermute(jnp.where(place.even, bottom, top), AXES, place.pairs)
    outer = lax.ppermute(jnp.where(place.even, top, bottom), AXES, place.bridges)
    north = jnp.where(place.even, outer, inner)
    south = jnp.where(place.even, inner, outer)
    side = jnp.stack([north[lon_cols - reach :], south[lon_cols - reach :]])
    rims_west = lax.ppermute(side, "lon", place.east)
    side = jnp.stack([north[:reach], south[:reach]])
    rims_east = lax.ppermute(side, "lon", place.west)

    low, full = jnp.bfloat16, jnp.float32
    points = lat_rows * lon_cols
    width = lon_cols + 2 * reach
    tile = points // 3
    vmem, anywhere = pltpu.VMEM, pl.ANY
    offsets = jnp.arange(tap_count, dtype=jnp.int32) - reach
    tap_mask = jnp.abs(offsets)[None, :] <= row_reach[:, None]
    taps = jnp.where(tap_mask[None, :, None, :], kernel_taps, jnp.zeros((), kernel_taps.dtype))
    taps = jnp.pad(taps.astype(full), ((0, 0), (0, 0), (0, 0), (0, width - tap_count)))
    cot = cotangent.reshape(points, channels)
    band_shape = (lat_rows, basis_count * lon_cols, 3 * width)
    gemm = 2 * points * channels * hidden_units
    mix_gemm = 2 * points * channels * channels * basis_count
    band_gemm = 2 * lat_rows * basis_count * lon_cols * 3 * width * channels
    act_grad, bands = call(
        functools.partial(before_kernel, rows=lat_rows, cols=lon_cols, tile=tile),
        (taps, cot, down_weight),
        [vmem] * 3,
        [((points, hidden_units), full), (band_shape, low)],
        [vmem] * 2,
        [],
        gemm,
        points * hidden_units * 4,
    )

    half_units, half_channels = hidden_units // 2, channels // 2
    mlp_half = (half_units + channels, channels)
    mix_half = (8, basis_count, half_channels // 8, channels)
    big = (points, channels)
    core = place.flat % 2
    hidden, activated, hidden_grad, mlp_send, mlp_keep, mix_send, mix_keep = call(
        functools.partial(main_kernel, tile=tile),
        (
            core[None].astype(jnp.int32), field_in, west, east, north, south, rims_west,
            rims_east, bands, mix_weight, up_weight, cot, act_grad,
        ),
        [pltpu.SMEM] + [anywhere] * 12,
        [
            (big, low), ((points, hidden_units), low), (big, low), (mlp_half, low),
            (mlp_half, full), (mix_half, low), (mix_half, full),
        ],
        [anywhere] * 3 + [vmem] * 4,
        [
            pltpu.VMEM((lat_rows + 2, width, channels), low),
            pltpu.VMEM(band_shape, low),
            pltpu.VMEM(mix_weight.shape, low),
            pltpu.VMEM(up_weight.shape, low),
            pltpu.VMEM(big, low),
            pltpu.VMEM((points, hidden_units), full),
            pltpu.VMEM((basis_count,) + big, low),
            pltpu.VMEM(big, low),
            pltpu.VMEM((points, hidden_units), low),
            pltpu.VMEM((points, hidden_units), low),
            pltpu.VMEM(big, low),
            pltpu.SemaphoreType.DMA((17,)),
        ],
        band_gemm + 2 * mix_gemm + 4 * gemm,
        4 * points * hidden_units * 4,
    )

    grad_scale = 1.0 / math.sqrt(points * place.count)
    if place.count == 32:
        ring = Ring(place)

        def total(keep, send, block_shape):
            own = ring.scatter(keep.reshape(block_shape), send.reshape(block_shape))
            own, other = ring.gather((own * grad_scale).astype(low))
            return own, other

        mlp_rows = mlp_half[0] // 8
        mlp_all = total(mlp_keep, mlp_send, (4, 2, mlp_rows, channels))
        mix_all = total(mix_keep, mix_send, (4, 2) + mix_half[1:])
        order = ring.order()

        def mlp_place(half, chunk):
            if chunk < 4:
                return 0, (pl.ds(half * half_units + chunk * mlp_rows, mlp_rows),)
            return 1, (
                pl.ds((chunk - 4) * mlp_rows, mlp_rows),
                pl.ds(half * half_units, half_units),
            )

        def mix_place(half, chunk):
            rows = half_channels // 8
            return 0, (slice(None), pl.ds(half * half_channels + chunk * rows, rows))

        down_out, up_out = assemble(
            order, *mlp_all, (down_weight.shape, up_weight.shape), mlp_place
        )
        (mix_out,) = assemble(order, *mix_all, (mix_weight.shape,), mix_place)
    else:
        def whole(keep, send):
            keep, send = keep[None], send.astype(full)[None]
            both = jnp.where(core == 0, jnp.concatenate([keep, send]), jnp.concatenate([send, keep]))
            return lax.psum(both, AXES) * grad_scale

        mlp_sum = whole(mlp_keep, mlp_send).astype(low)
        mix_sum = whole(mix_keep, mix_send).astype(low)
        down_out = mlp_sum[:, :half_units].reshape(down_weight.shape)
        up_out = jnp.concatenate([mlp_sum[0, half_units:], mlp_sum[1, half_units:]], axis=1)
        mix_out = mix_sum.transpose(2, 0, 1, 3, 4).reshape(mix_weight.shape)

    rim_shape = (2, reach, channels)
    side_shape = (lat_rows, reach, channels)
    block_out, inner, rims, corner_west, corner_east, side_west, side_east = call(
        functools.partial(after_kernel, rows=lat_rows, cols=lon_cols, tile=tile),
        (hidden, activated, down_weight, hidden_grad, mix_weight, bands),
        [anywhere] * 6,
        [
            (big, low), ((lat_rows, lon_cols, channels), full), ((2, lon_cols, channels), full),
            (rim_shape, low), (rim_shape, low), (side_shape, low), (side_shape, low),
        ],
        [vmem] * 7,
        [
            pltpu.VMEM(big, low),
            pltpu.VMEM((points, hidden_units), low),
            pltpu.VMEM(down_weight.shape, low),
            pltpu.VMEM(big, low),
            pltpu.VMEM(mix_weight.shape, low),
            pltpu.VMEM(band_shape, low),
            pltpu.VMEM((lat_rows, basis_count * lon_cols, channels), low),
            pltpu.VMEM((lat_rows + 2, width, channels), full),
            pltpu.SemaphoreType.DMA((6,)),
        ],
        band_gemm + mix_gemm + gemm,
        3 * points * hidden_units * 4,
    )

    from_east = lax.ppermute(corner_west, "lon", place.west)
    from_west = lax.ppermute(corner_east, "lon", place.east)
    rims = rims.at[:, lon_cols - reach :].add(from_east.astype(full))
    rims = rims.at[:, :reach].add(from_west.astype(full)).astype(low)
    near = lax.ppermute(jnp.where(place.even, rims[1], rims[0]), AXES, place.pairs)
    far = lax.ppermute(jnp.where(place.even, rims[0], rims[1]), AXES, place.bridges)
    from_east = lax.ppermute(side_west, "lon", place.west)
    from_west = lax.ppermute(side_east, "lon", place.east)
    adjoint = inner.at[:, lon_cols - reach :].add(from_east.astype(full))
    adjoint = adjoint.at[:, :reach].add(from_west.astype(full))
    adjoint = adjoint.at[0].add(jnp.where(place.even, far, near).astype(full))
    adjoint = adjoint.at[lat_rows - 1].add(jnp.where(place.even, near, far).astype(full))
    grad_field = (
        hidden_grad.astype(full).reshape(lat_rows, lon_cols, channels) + adjoint
    ).astype(low)
    return (block_out.reshape(field_in.shape), grad_field, mix_out, up_out, down_out)


def solution(mesh):
    placed = (
        P("lat", "lon", None),
        P(None, "lat", None, None),
        P("lat"),
        P(),
        P(),
        P(),
        P("lat", "lon", None),
    )
    return jax.shard_map(
        local,
        mesh=mesh,
        in_specs=placed,
        out_specs=(P("lat", "lon", None), P("lat", "lon", None), P(), P(), P()),
        check_vma=False,
    )
```

```python
import functools
import math

import jax
import jax.numpy as jnp
from jax import lax
from jax.experimental import pallas as pl
from jax.experimental.pallas import tpu as pltpu
from jax.sharding import PartitionSpec as P

inv_root_two = 0.7071067811865476
inv_root_tau = 0.3989422804014327
AXES = ("lat", "lon")


class Place:
    def __init__(self):
        self.lats = lax.axis_size("lat")
        self.lons = lax.axis_size("lon")
        self.count = self.lats * self.lons
        self.lat = lax.axis_index("lat")
        self.lon = lax.axis_index("lon")
        self.flat = self.lat * self.lons + self.lon
        lats, lons = self.lats, self.lons
        self.east = [(i, (i + 1) % lons) for i in range(lons)]
        self.west = [(j, i) for i, j in self.east]
        self.pairs = [
            (r * lons + c, (r ^ 1) * lons + c) for r in range(lats) for c in range(lons)
        ]
        self.bridges = []
        for r in range(lats):
            other = r - 1 if r % 2 == 0 else r + 1
            for c in range(lons):
                if 0 <= other < lats:
                    self.bridges.append((r * lons + c, other * lons + c))
                else:
                    self.bridges.append((r * lons + c, r * lons + (c + lons // 2) % lons))
        self.even = self.lat % 2 == 0


def route(place, mask_of):
    return [(i, i ^ mask_of(i)) for i in range(place.count)]


def send_along(place, block, mask_of):
    return lax.ppermute(block, AXES, route(place, mask_of))


def first_mask(i):
    return 2 if i % 2 == 0 else 4


def second_mask(i):
    return 4 if i % 2 == 0 else 2


def pick(array, index):
    return lax.dynamic_index_in_dim(array, index, 0, keepdims=False)


def joined(bit, own, other):
    return jnp.concatenate([jnp.where(bit == 0, own, other), jnp.where(bit == 0, other, own)])


class Ring:
    def __init__(self, place):
        self.place = place
        self.core = place.flat % 2
        side_y, side_x = (place.flat // 2) % 2, (place.flat // 4) % 2
        self.first = jnp.where(self.core == 0, side_y, side_x)
        self.second = jnp.where(self.core == 0, side_x, side_y)
        self.near = (place.flat // 8) % 2

    def to_core(self, keep, send):
        return keep + send_along(self.place, send, lambda i: 1).astype(jnp.float32)

    def leaving(self, buf):
        return pick(buf, 1 - self.first).astype(jnp.bfloat16)

    def scatter(self, buf, out):
        low, place = jnp.bfloat16, self.place
        buf = pick(buf, self.first) + send_along(place, out, first_mask).astype(jnp.float32)
        out = pick(buf, 1 - self.second).astype(low)
        buf = pick(buf, self.second) + send_along(place, out, second_mask).astype(jnp.float32)
        out = pick(buf, 1 - self.near).astype(low)
        buf = pick(buf, self.near) + send_along(place, out, lambda i: 8).astype(jnp.float32)
        own = buf.astype(low)
        far = send_along(place, own, lambda i: 16)
        return own.astype(jnp.float32) + far.astype(jnp.float32)

    def gather(self, piece):
        place = self.place
        buf = piece[None]
        for bit, mask_of in (
            (self.near, lambda i: 8), (self.second, second_mask), (self.first, first_mask)
        ):
            buf = joined(bit, buf, send_along(place, buf, mask_of))
        other = send_along(place, buf, lambda i: 1)
        return jnp.where(self.core == 0, buf, other), jnp.where(self.core == 0, other, buf)


OVER_ROWS = (((0,), (0,)), ((), ()))
OVER_LANES = (((1,), (1,)), ((), ()))
VMEM_LIMIT = 56 * 1024 * 1024


def dot(left, right, dims=(((1,), (0,)), ((), ()))):
    return lax.dot_general(left, right, dims, preferred_element_type=jnp.float32)


def tiles(count, size, body):
    def step(i, carry):
        body(pl.ds(pl.multiple_of(i * size, size), size))
        return carry

    lax.fori_loop(0, count // size, step, 0)


def band_kernel(reach_ref, taps, bands, lines, *, cols):
    basis, rows, _, count = taps.shape
    width = lines.shape[2]
    away = jnp.abs(lax.broadcasted_iota(jnp.int32, (3, count), 1) - (count - 1) // 2)
    lines[...] = jnp.zeros(lines.shape, lines.dtype)

    def one_row(r, carry):
        inside = away <= reach_ref[r]
        for k in range(basis):
            lines[k, :, :count] = jnp.where(inside, taps[k, r].astype(jnp.float32), 0.0)
            for d in range(3):
                line = jnp.broadcast_to(lines[k, pl.ds(d, 1)], (cols, width))
                band = pltpu.roll(line, 0, 1, stride=1, stride_axis=0)
                bands[r, k * cols : (k + 1) * cols, d * width : (d + 1) * width] = band.astype(
                    bands.dtype
                )
        return carry

    lax.fori_loop(0, rows, one_row, 0)


def started(pairs, sems, first=0):
    copies = [pltpu.make_async_copy(a, b, sems.at[first + i]) for i, (a, b) in enumerate(pairs)]
    for copy in copies:
        copy.start()
    return copies


def finish(copies):
    for copy in copies:
        copy.wait()


def forward_kernel(
    core_ref, field, north, south, west, east, bands_in, mix_in, up_in, down_in, cot_in,
    feats_out, hidden_out, act_out, pre_out, send, keep,
    ext, bands, mix, up, down, cot, feats, hidden, act, pre_grad, turned, pre_a, pre_b, ag_a,
    ag_b, sems
):
    core = core_ref[0]
    rows, cols, channels = field.shape
    reach = west.shape[1]
    basis = mix.shape[0]
    points = rows * cols
    half_units = up.shape[1] // 2
    body, inner = pl.ds(1, rows), pl.ds(reach, cols)
    loads = started(
        [
            (field, ext.at[body, inner]),
            (west, ext.at[:, pl.ds(0, reach)]),
            (east, ext.at[:, pl.ds(reach + cols, reach)]),
            (north, ext.at[0, inner]),
            (south, ext.at[rows + 1, inner]),
            (bands_in, bands),
            (mix_in, mix),
            (up_in, up),
            (down_in, down),
            (cot_in, cot),
        ],
        sems,
    )
    finish(loads[:6])

    def two_rows(i, carry):
        for r in (2 * i, 2 * i + 1):
            window = ext[pl.ds(r, 3)].reshape(3 * ext.shape[1], channels)
            out = dot(bands[r], window).astype(feats.dtype)
            at = pl.ds(pl.multiple_of(r * cols, cols), cols)
            for k in range(basis):
                feats[k, at, :] = out[k * cols : (k + 1) * cols]
            hidden[at, :] = ext[r + 1, inner, :]
        return carry

    lax.fori_loop(0, rows // 2, two_rows, 0)
    stores = started([(feats, feats_out)], sems, 10)
    finish(loads[6:7])

    def mixing(at):
        total = hidden[at, :].astype(jnp.float32)
        for k in range(basis):
            total = total + dot(feats[k, at, :], mix[k])
        hidden[at, :] = total.astype(hidden.dtype)

    tiles(points, points // 3, mixing)
    finish(loads[7:])
    stores += started([(hidden, hidden_out)], sems, 11)
    size = pre_a.shape[0]
    slots = ((pre_a, ag_a), (pre_b, ag_b))

    def products(i):
        at = pl.ds(i * size, size)
        pre, ag = slots[i % 2]
        pre[...] = dot(hidden[at, :], up[...])
        ag[...] = dot(cot[at, :], down[...], OVER_LANES)

    def activation(i):
        at = pl.ds(i * size, size)
        pre, ag = slots[i % 2]
        value = pre[...]
        phi = 0.5 * (1.0 + lax.erf(value * inv_root_two))
        act[at, :] = (value * phi).astype(act.dtype)
        slope = phi + value * jnp.exp(-0.5 * value * value) * inv_root_tau
        pre_grad[at, :] = (ag[...] * slope).astype(pre_grad.dtype)

    products(0)
    for i in range(points // size):
        if (i + 1) * size < points:
            products(i + 1)
        activation(i)
    stores += started([(act, act_out), (pre_grad, pre_out)], sems, 12)
    turned[...] = hidden[...].T

    def sums(half, out):
        at = pl.ds(pl.multiple_of(half * half_units, half_units), half_units)
        out[:half_units] = dot(act[:, at], cot[...], OVER_ROWS).astype(out.dtype)
        out[half_units:] = dot(turned[...], pre_grad[:, at]).astype(out.dtype)

    sums(1 - core, send)
    sums(core, keep)
    finish(stores)


def backward_kernel(
    core_ref, pre_in, up_in, cot_in, feats_in, hg_out, send, keep,
    pre_grad, up, cot, feats, hg, sems
):
    core = core_ref[0]
    basis, points, channels = feats.shape
    half_channels = channels // 2
    loads = started([(pre_in, pre_grad), (up_in, up), (cot_in, cot), (feats_in, feats)], sems)
    finish(loads[:3])

    def back(at):
        total = cot[at, :].astype(jnp.float32) + dot(pre_grad[at, :], up[...], OVER_LANES)
        hg[at, :] = total.astype(hg.dtype)

    tiles(points, points // 3, back)
    stores = started([(hg, hg_out)], sems, 4)
    finish(loads[3:])

    def sums(half, out):
        at = pl.ds(pl.multiple_of(half * half_channels, half_channels), half_channels)
        for k in range(basis):
            part = dot(feats[k, :, at], hg[...], OVER_ROWS).astype(out.dtype)
            out[:, k] = part.reshape(out.shape[0], -1, channels)

    sums(1 - core, send)
    sums(core, keep)
    finish(stores)


def out_kernel(hidden, act, down, block):
    def forward(at):
        total = hidden[at, :].astype(jnp.float32) + dot(act[at, :], down[...])
        block[at, :] = total.astype(block.dtype)

    tiles(hidden.shape[0], hidden.shape[0] // 3, forward)


def adjoint_kernel(
    token, hg_in, mix_in, bands_in, inner_out, rim_out, west_out, east_out,
    hg, mix, bands, grads, pulled, sems, *, cols
):
    basis, channels = mix.shape[0], mix.shape[1]
    rows, width = pulled.shape[0] - 2, pulled.shape[1]
    reach = (width - cols) // 2
    loads = started([(mix_in, mix), (hg_in, hg), (bands_in, bands)], sems)
    pulled[...] = jnp.zeros(pulled.shape, pulled.dtype)
    finish(loads[:2])
    group = 5 if rows % 5 == 0 else 1

    def feature_grads(i, carry):
        at = pl.ds(pl.multiple_of(i * group * cols, group * cols), group * cols)
        for k in range(basis):
            part = dot(hg[at, :], mix[k], OVER_LANES).astype(grads.dtype)
            grads[pl.ds(i * group, group), pl.ds(k * cols, cols)] = part.reshape(
                group, cols, channels
            )
        return carry

    lax.fori_loop(0, rows // group, feature_grads, 0)
    finish(loads[2:])

    def one_row(r, carry):
        part = dot(bands[r], grads[r], OVER_ROWS)
        pulled[pl.ds(r, 3)] += part.reshape(3, width, channels)
        return carry

    lax.fori_loop(0, rows, one_row, 0)
    west_out[...] = pulled[:, :reach].astype(west_out.dtype)
    east_out[...] = pulled[:, reach + cols :].astype(east_out.dtype)
    inner_out[...] = pulled[1 : rows + 1, reach : reach + cols]
    for n, r in enumerate((0, rows + 1)):
        rim_out[n] = pulled[r, reach : reach + cols]


def call(kernel, operands, kinds, shapes, out_kinds, scratch, flops, nbytes):
    return pl.pallas_call(
        kernel,
        out_shape=[jax.ShapeDtypeStruct(shape, kind) for shape, kind in shapes],
        in_specs=[pl.BlockSpec(memory_space=kind) for kind in kinds],
        out_specs=[pl.BlockSpec(memory_space=kind) for kind in out_kinds],
        scratch_shapes=scratch,
        compiler_params=pltpu.CompilerParams(vmem_limit_bytes=VMEM_LIMIT),
        cost_estimate=pl.CostEstimate(flops=flops, bytes_accessed=nbytes, transcendentals=0),
    )(*operands)


def local(field_in, kernel_taps, row_reach, mix_weight, up_weight, down_weight, cotangent):
    lat_rows, lon_cols, channels = field_in.shape
    basis_count = kernel_taps.shape[0]
    tap_count = kernel_taps.shape[3]
    reach = (tap_count - 1) // 2
    hidden_units = up_weight.shape[1]
    place = Place()

    top, bottom = field_in[0], field_in[lat_rows - 1]
    inner = lax.ppermute(jnp.where(place.even, bottom, top), AXES, place.pairs)
    outer = lax.ppermute(jnp.where(place.even, top, bottom), AXES, place.bridges)
    north = jnp.where(place.even, outer, inner)
    south = jnp.where(place.even, inner, outer)

    def column(at):
        return jnp.concatenate([north[None, at], field_in[:, at], south[None, at]])

    west = lax.ppermute(column(slice(lon_cols - reach, lon_cols)), "lon", place.east)
    east = lax.ppermute(column(slice(0, reach)), "lon", place.west)

    low, full = jnp.bfloat16, jnp.float32
    points = lat_rows * lon_cols
    width = lon_cols + 2 * reach
    vmem, anywhere, smem = pltpu.VMEM, pl.ANY, pltpu.SMEM
    cot = cotangent.reshape(points, channels)
    band_shape = (lat_rows, basis_count * lon_cols, 3 * width)
    gemm = 2 * points * channels * hidden_units
    mix_gemm = 2 * points * channels * channels * basis_count
    band_gemm = 2 * lat_rows * basis_count * lon_cols * 3 * width * channels
    (bands,) = call(
        functools.partial(band_kernel, cols=lon_cols),
        (row_reach, kernel_taps),
        [smem, vmem],
        [(band_shape, low)],
        [vmem],
        [pltpu.VMEM((basis_count, 3, width), full)],
        0,
        2 * points * hidden_units * 4,
    )

    half_units, half_channels = hidden_units // 2, channels // 2
    mlp_half = (half_units + channels, channels)
    mix_half = (8, basis_count, half_channels // 8, channels)
    big, wide, many = (points, channels), (points, hidden_units), (basis_count, points, channels)
    core = place.flat % 2
    core_op = core[None].astype(jnp.int32)
    sized = (points // 5, hidden_units)
    feats, hidden, activated, pre_grad, mlp_send, mlp_keep = call(
        forward_kernel,
        (
            core_op, field_in, north, south, west, east, bands, mix_weight, up_weight,
            down_weight, cot,
        ),
        [smem] + [anywhere] * 10,
        [(many, low), (big, low), (wide, low), (wide, low), (mlp_half, low), (mlp_half, full)],
        [anywhere] * 4 + [vmem] * 2,
        [
            pltpu.VMEM((lat_rows + 2, width, channels), low),
            pltpu.VMEM(band_shape, low),
            pltpu.VMEM(mix_weight.shape, low),
            pltpu.VMEM(up_weight.shape, low),
            pltpu.VMEM(down_weight.shape, low),
            pltpu.VMEM(big, low),
            pltpu.VMEM(many, low),
            pltpu.VMEM(big, low),
            pltpu.VMEM(wide, low),
            pltpu.VMEM(wide, low),
            pltpu.VMEM((channels, points), low),
            pltpu.VMEM(sized, full),
            pltpu.VMEM(sized, full),
            pltpu.VMEM(sized, full),
            pltpu.VMEM(sized, full),
            pltpu.SemaphoreType.DMA((14,)),
        ],
        band_gemm + mix_gemm + 4 * gemm,
        4 * points * hidden_units * 4,
    )
    hidden_grad, mix_send, mix_keep = call(
        backward_kernel,
        (core_op, pre_grad, up_weight, cot, feats),
        [smem] + [anywhere] * 4,
        [(big, low), (mix_half, low), (mix_half, full)],
        [anywhere] + [vmem] * 2,
        [
            pltpu.VMEM(wide, low),
            pltpu.VMEM(up_weight.shape, low),
            pltpu.VMEM(big, low),
            pltpu.VMEM(many, low),
            pltpu.VMEM(big, low),
            pltpu.SemaphoreType.DMA((5,)),
        ],
        mix_gemm + gemm,
        3 * points * hidden_units * 4,
    )
    (block_out,) = call(
        out_kernel,
        (hidden, activated, down_weight),
        [vmem] * 3,
        [(big, low)],
        [vmem],
        [],
        gemm,
        2 * points * hidden_units * 4,
    )

    grad_scale = 1.0 / math.sqrt(points * place.count)
    token = row_reach[:1]
    if place.count == 32:
        ring = Ring(place)

        def begin(keep, send, block_shape):
            buf = ring.to_core(keep.reshape(block_shape), send.reshape(block_shape))
            return buf, ring.leaving(buf)

        def total(buf, out):
            return ring.gather((ring.scatter(buf, out) * grad_scale).astype(low))

        mlp_begun = begin(mlp_keep, mlp_send, (2, 2, 2, mlp_half[0] // 8, channels))
        mix_begun = begin(mix_keep, mix_send, (2, 2, 2) + mix_half[1:])
        token = (mlp_begun[1][0, 0, :1, 0] + mix_begun[1][0, 0, 0, :1, 0]).astype(full)
        mlp_halves = [half.reshape(mlp_half) for half in total(*mlp_begun)]
        mix_halves = [half.reshape(mix_half) for half in total(*mix_begun)]
        down_out = jnp.concatenate([half[:half_units] for half in mlp_halves])
        up_out = jnp.concatenate([half[half_units:] for half in mlp_halves], axis=1)
        mix_out = jnp.stack([half.swapaxes(0, 1) for half in mix_halves], axis=1)
        mix_out = mix_out.reshape(mix_weight.shape)
    else:
        token = token.astype(full)

        def whole(keep, send):
            keep, send = keep[None], send.astype(full)[None]
            both = jnp.where(core == 0, jnp.concatenate([keep, send]), jnp.concatenate([send, keep]))
            return lax.psum(both, AXES) * grad_scale

        mlp_sum = whole(mlp_keep, mlp_send).astype(low)
        mix_sum = whole(mix_keep, mix_send).astype(low)
        down_out = mlp_sum[:, :half_units].reshape(down_weight.shape)
        up_out = jnp.concatenate([mlp_sum[0, half_units:], mlp_sum[1, half_units:]], axis=1)
        mix_out = mix_sum.transpose(2, 0, 1, 3, 4).reshape(mix_weight.shape)

    side = (lat_rows + 2, reach, channels)
    inner, rims, to_west, to_east = call(
        functools.partial(adjoint_kernel, cols=lon_cols),
        (token, hidden_grad, mix_weight, bands),
        [smem] + [anywhere] * 3,
        [
            ((lat_rows, lon_cols, channels), full), ((2, lon_cols, channels), full),
            (side, low), (side, low),
        ],
        [vmem] * 4,
        [
            pltpu.VMEM(big, low),
            pltpu.VMEM(mix_weight.shape, low),
            pltpu.VMEM(band_shape, low),
            pltpu.VMEM((lat_rows, basis_count * lon_cols, channels), low),
            pltpu.VMEM((lat_rows + 2, width, channels), full),
            pltpu.SemaphoreType.DMA((3,)),
        ],
        band_gemm + mix_gemm,
        3 * points * hidden_units * 4,
    )

    from_east = lax.ppermute(to_west, "lon", place.west)
    from_west = lax.ppermute(to_east, "lon", place.east)
    corner_east = jnp.stack([from_east[0], from_east[lat_rows + 1]]).astype(full)
    corner_west = jnp.stack([from_west[0], from_west[lat_rows + 1]]).astype(full)
    rims = rims.at[:, lon_cols - reach :].add(corner_east)
    rims = rims.at[:, :reach].add(corner_west).astype(low)
    near = lax.ppermute(jnp.where(place.even, rims[1], rims[0]), AXES, place.pairs)
    far = lax.ppermute(jnp.where(place.even, rims[0], rims[1]), AXES, place.bridges)
    adjoint = inner.at[:, lon_cols - reach :].add(from_east[1 : lat_rows + 1].astype(full))
    adjoint = adjoint.at[:, :reach].add(from_west[1 : lat_rows + 1].astype(full))
    adjoint = adjoint.at[0].add(jnp.where(place.even, far, near).astype(full))
    adjoint = adjoint.at[lat_rows - 1].add(jnp.where(place.even, near, far).astype(full))
    grad_field = (
        hidden_grad.astype(full).reshape(lat_rows, lon_cols, channels) + adjoint
    ).astype(low)
    return (block_out.reshape(field_in.shape), grad_field, mix_out, up_out, down_out)


def solution(mesh):
    placed = (
        P("lat", "lon", None),
        P(None, "lat", None, None),
        P("lat"),
        P(),
        P(),
        P(),
        P("lat", "lon", None),
    )
    return jax.shard_map(
        local,
        mesh=mesh,
        in_specs=placed,
        out_specs=(P("lat", "lon", None), P("lat", "lon", None), P(), P(), P()),
        check_vma=False,
    )
```

```python
import functools
import math

import jax
import jax.numpy as jnp
from jax import lax
from jax.experimental import pallas as pl
from jax.experimental.pallas import tpu as pltpu
from jax.sharding import PartitionSpec as P

inv_root_two = 0.7071067811865476
inv_root_tau = 0.3989422804014327
AXES = ("lat", "lon")


class Place:
    def __init__(self):
        self.lats = lax.axis_size("lat")
        self.lons = lax.axis_size("lon")
        self.count = self.lats * self.lons
        self.lat = lax.axis_index("lat")
        self.lon = lax.axis_index("lon")
        self.flat = self.lat * self.lons + self.lon
        lats, lons = self.lats, self.lons
        self.east = [(i, (i + 1) % lons) for i in range(lons)]
        self.west = [(j, i) for i, j in self.east]
        self.pairs = [
            (r * lons + c, (r ^ 1) * lons + c) for r in range(lats) for c in range(lons)
        ]
        self.bridges = []
        for r in range(lats):
            other = r - 1 if r % 2 == 0 else r + 1
            for c in range(lons):
                if 0 <= other < lats:
                    self.bridges.append((r * lons + c, other * lons + c))
                else:
                    self.bridges.append((r * lons + c, r * lons + (c + lons // 2) % lons))
        self.even = self.lat % 2 == 0


def route(place, mask_of):
    return [(i, i ^ mask_of(i)) for i in range(place.count)]


def send_along(place, block, mask_of):
    return lax.ppermute(block, AXES, route(place, mask_of))


def first_mask(i):
    return 2 if i % 2 == 0 else 4


def second_mask(i):
    return 4 if i % 2 == 0 else 2


def after(value, *others):
    return lax.optimization_barrier((value, *others))[0]


def pick(array, index):
    return lax.dynamic_index_in_dim(array, index, 0, keepdims=False)


def joined(bit, own, other):
    return jnp.concatenate([jnp.where(bit == 0, own, other), jnp.where(bit == 0, other, own)])


class Ring:
    def __init__(self, place):
        self.place = place
        self.core = place.flat % 2
        side_y, side_x = (place.flat // 2) % 2, (place.flat // 4) % 2
        self.first = jnp.where(self.core == 0, side_y, side_x)
        self.second = jnp.where(self.core == 0, side_x, side_y)
        self.near = (place.flat // 8) % 2

    def to_core(self, keep, send):
        return keep + send_along(self.place, send, lambda i: 1).astype(jnp.float32)

    def leaving(self, buf, bit):
        return pick(buf, 1 - bit).astype(jnp.bfloat16)

    def step(self, buf, out, mask_of, bit):
        got = send_along(self.place, out, mask_of)
        return pick(buf, bit) + got.astype(jnp.float32)

    def stages(self, buf, scale):
        low, place = jnp.bfloat16, self.place
        out = yield self.leaving(buf, self.first)
        buf = self.step(buf, out, first_mask, self.first)
        out = yield self.leaving(buf, self.second)
        buf = self.step(buf, out, second_mask, self.second)
        out = yield self.leaving(buf, self.near)
        buf = self.step(buf, out, lambda i: 8, self.near)
        own = yield buf.astype(low)
        far = send_along(place, own, lambda i: 16)
        piece = ((own.astype(jnp.float32) + far.astype(jnp.float32)) * scale).astype(low)
        buf = yield piece[None]
        for bit, mask_of in (
            (self.near, lambda i: 8), (self.second, second_mask), (self.first, first_mask)
        ):
            buf = yield joined(bit, buf, send_along(place, buf, mask_of))
        other = send_along(place, buf, lambda i: 1)
        yield jnp.where(self.core == 0, buf, other), jnp.where(self.core == 0, other, buf)


OVER_ROWS = (((0,), (0,)), ((), ()))
OVER_LANES = (((1,), (1,)), ((), ()))
VMEM_LIMIT = 56 * 1024 * 1024


def dot(left, right, dims=(((1,), (0,)), ((), ()))):
    return lax.dot_general(left, right, dims, preferred_element_type=jnp.float32)


def tiles(count, size, body):
    def step(i, carry):
        body(pl.ds(pl.multiple_of(i * size, size), size))
        return carry

    lax.fori_loop(0, count // size, step, 0)


def band_kernel(reach_ref, taps, bands, lines, *, cols):
    basis, rows, _, count = taps.shape
    width = lines.shape[2]
    away = jnp.abs(lax.broadcasted_iota(jnp.int32, (3, count), 1) - (count - 1) // 2)
    lines[...] = jnp.zeros(lines.shape, lines.dtype)

    def one_row(r, carry):
        inside = away <= reach_ref[r]
        for k in range(basis):
            lines[k, :, :count] = jnp.where(inside, taps[k, r].astype(jnp.float32), 0.0)
            for d in range(3):
                line = jnp.broadcast_to(lines[k, pl.ds(d, 1)], (cols, width))
                band = pltpu.roll(line, 0, 1, stride=1, stride_axis=0)
                bands[r, k * cols : (k + 1) * cols, d * width : (d + 1) * width] = band.astype(
                    bands.dtype
                )
        return carry

    lax.fori_loop(0, rows, one_row, 0)


def started(pairs, sems, first=0):
    copies = [pltpu.make_async_copy(a, b, sems.at[first + i]) for i, (a, b) in enumerate(pairs)]
    for copy in copies:
        copy.start()
    return copies


def finish(copies):
    for copy in copies:
        copy.wait()


def forward_kernel(
    core_ref, field, north, south, west, east, bands_in, mix_in, up_in, down_in, cot_in,
    feats_out, hidden_out, act_out, pre_out, send, keep,
    ext, bands, mix, up, down, cot, feats, hidden, act, pre_grad, turned, pre_a, pre_b, ag_a,
    ag_b, sems
):
    core = core_ref[0]
    rows, cols, channels = field.shape
    reach = west.shape[1]
    basis = mix.shape[0]
    points = rows * cols
    half_units = up.shape[1] // 2
    body, inner = pl.ds(1, rows), pl.ds(reach, cols)
    loads = started(
        [
            (field, ext.at[body, inner]),
            (west, ext.at[:, pl.ds(0, reach)]),
            (east, ext.at[:, pl.ds(reach + cols, reach)]),
            (north, ext.at[0, inner]),
            (south, ext.at[rows + 1, inner]),
            (bands_in, bands),
            (mix_in, mix),
            (up_in, up),
            (down_in, down),
            (cot_in, cot),
        ],
        sems,
    )
    finish(loads[:6])

    def two_rows(i, carry):
        for r in (2 * i, 2 * i + 1):
            window = ext[pl.ds(r, 3)].reshape(3 * ext.shape[1], channels)
            out = dot(bands[r], window).astype(feats.dtype)
            at = pl.ds(pl.multiple_of(r * cols, cols), cols)
            for k in range(basis):
                feats[k, at, :] = out[k * cols : (k + 1) * cols]
            hidden[at, :] = ext[r + 1, inner, :]
        return carry

    lax.fori_loop(0, rows // 2, two_rows, 0)
    stores = started([(feats, feats_out)], sems, 10)
    finish(loads[6:7])

    def mixing(at):
        total = hidden[at, :].astype(jnp.float32)
        for k in range(basis):
            total = total + dot(feats[k, at, :], mix[k])
        hidden[at, :] = total.astype(hidden.dtype)

    tiles(points, points // 3, mixing)
    finish(loads[7:])
    stores += started([(hidden, hidden_out)], sems, 11)
    size = pre_a.shape[0]
    slots = ((pre_a, ag_a), (pre_b, ag_b))

    def products(i):
        at = pl.ds(i * size, size)
        pre, ag = slots[i % 2]
        pre[...] = dot(hidden[at, :], up[...])
        ag[...] = dot(cot[at, :], down[...], OVER_LANES)

    def activation(i):
        at = pl.ds(i * size, size)
        pre, ag = slots[i % 2]
        value = pre[...]
        phi = 0.5 * (1.0 + lax.erf(value * inv_root_two))
        act[at, :] = (value * phi).astype(act.dtype)
        slope = phi + value * jnp.exp(-0.5 * value * value) * inv_root_tau
        pre_grad[at, :] = (ag[...] * slope).astype(pre_grad.dtype)

    products(0)
    for i in range(points // size):
        if (i + 1) * size < points:
            products(i + 1)
        activation(i)
    stores += started([(act, act_out), (pre_grad, pre_out)], sems, 12)
    turned[...] = hidden[...].T

    def sums(half, out):
        at = pl.ds(pl.multiple_of(half * half_units, half_units), half_units)
        out[:half_units] = dot(act[:, at], cot[...], OVER_ROWS).astype(out.dtype)
        out[half_units:] = dot(turned[...], pre_grad[:, at]).astype(out.dtype)

    sums(1 - core, send)
    sums(core, keep)
    finish(stores)


def back_kernel(pre_in, up_in, cot_in, hg_out, pre_grad, up, cot, hg, sems):
    points = cot.shape[0]
    size = points // 3
    parts = [pl.ds(i * size, size) for i in range(3)]
    loads = started([(up_in, up)], sems)
    loads += started([(pre_in.at[at], pre_grad.at[at]) for at in parts], sems, 1)
    loads += started([(cot_in.at[at], cot.at[at]) for at in parts], sems, 4)
    finish(loads[:1])
    stores = []
    for i, at in enumerate(parts):
        finish([loads[1 + i], loads[4 + i]])
        total = cot[at, :].astype(jnp.float32) + dot(pre_grad[at, :], up[...], OVER_LANES)
        hg[at, :] = total.astype(hg.dtype)
        stores += started([(hg.at[at], hg_out.at[at])], sems, 7 + i)
    finish(stores)


def mix_kernel(core_ref, hg_in, feats_in, send, keep, hg, feats, sems):
    core = core_ref[0]
    basis, points, channels = feats.shape
    half_channels = channels // 2
    loads = started([(hg_in, hg)], sems)
    loads += started([(feats_in.at[k], feats.at[k]) for k in range(basis)], sems, 1)
    finish(loads[:1])

    def sums(half, out, waits):
        at = pl.ds(pl.multiple_of(half * half_channels, half_channels), half_channels)
        for k in range(basis):
            finish(waits[k : k + 1])
            part = dot(feats[k, :, at], hg[...], OVER_ROWS).astype(out.dtype)
            out[:, k] = part.reshape(out.shape[0], -1, channels)

    sums(1 - core, send, loads[1:])
    sums(core, keep, [])


def out_kernel(hidden, act, down, block):
    def forward(at):
        total = hidden[at, :].astype(jnp.float32) + dot(act[at, :], down[...])
        block[at, :] = total.astype(block.dtype)

    tiles(hidden.shape[0], hidden.shape[0] // 3, forward)


def feature_grad_kernel(hg_in, mix_in, grads_out, hg, mix, grads, sems, *, cols):
    basis, channels = mix.shape[0], mix.shape[1]
    rows = grads.shape[0]
    loads = started([(hg_in, hg)], sems)
    loads += started([(mix_in.at[k], mix.at[k]) for k in range(basis)], sems, 1)
    group = 5 if rows % 5 == 0 else 1
    finish(loads[:1])
    stores = []
    for k in range(basis):
        finish(loads[1 + k : 2 + k])
        spot = pl.ds(k * cols, cols)
        for r in range(0, rows, group):
            at = pl.ds(r * cols, group * cols)
            part = dot(hg[at, :], mix[k], OVER_LANES).astype(grads.dtype)
            grads[pl.ds(r, group), spot] = part.reshape(group, cols, channels)
        stores += started([(grads.at[:, spot], grads_out.at[:, spot])], sems, 4 + k)
    finish(stores)


def adjoint_kernel(
    grads_in, bands_in, inner_out, rim_out, west_out, east_out,
    grads, bands, pulled, sems, *, cols
):
    rows, width, channels = pulled.shape[0] - 2, pulled.shape[1], pulled.shape[2]
    reach = (width - cols) // 2
    loads = started([(bands_in.at[r], bands.at[r]) for r in range(rows)], sems)
    loads += started([(grads_in.at[r], grads.at[r]) for r in range(rows)], sems, rows)
    pulled[...] = jnp.zeros(pulled.shape, pulled.dtype)
    for r in range(rows):
        finish([loads[r], loads[rows + r]])
        part = dot(bands[r], grads[r], OVER_ROWS)
        pulled[pl.ds(r, 3)] += part.reshape(3, width, channels)
    west_out[...] = pulled[:, :reach].astype(west_out.dtype)
    east_out[...] = pulled[:, reach + cols :].astype(east_out.dtype)
    inner_out[...] = pulled[1 : rows + 1, reach : reach + cols]
    for n, r in enumerate((0, rows + 1)):
        rim_out[n] = pulled[r, reach : reach + cols]


def call(kernel, operands, kinds, shapes, out_kinds, scratch, flops, nbytes):
    return pl.pallas_call(
        kernel,
        out_shape=[jax.ShapeDtypeStruct(shape, kind) for shape, kind in shapes],
        in_specs=[pl.BlockSpec(memory_space=kind) for kind in kinds],
        out_specs=[pl.BlockSpec(memory_space=kind) for kind in out_kinds],
        scratch_shapes=scratch,
        compiler_params=pltpu.CompilerParams(vmem_limit_bytes=VMEM_LIMIT),
        cost_estimate=pl.CostEstimate(flops=flops, bytes_accessed=nbytes, transcendentals=0),
    )(*operands)


def local(field_in, kernel_taps, row_reach, mix_weight, up_weight, down_weight, cotangent):
    lat_rows, lon_cols, channels = field_in.shape
    basis_count = kernel_taps.shape[0]
    tap_count = kernel_taps.shape[3]
    reach = (tap_count - 1) // 2
    hidden_units = up_weight.shape[1]
    place = Place()

    top, bottom = field_in[0], field_in[lat_rows - 1]
    inner = lax.ppermute(jnp.where(place.even, bottom, top), AXES, place.pairs)
    outer = lax.ppermute(jnp.where(place.even, top, bottom), AXES, place.bridges)
    north = jnp.where(place.even, outer, inner)
    south = jnp.where(place.even, inner, outer)

    def column(at):
        return jnp.concatenate([north[None, at], field_in[:, at], south[None, at]])

    west = lax.ppermute(column(slice(lon_cols - reach, lon_cols)), "lon", place.east)
    east = lax.ppermute(column(slice(0, reach)), "lon", place.west)

    low, full = jnp.bfloat16, jnp.float32
    points = lat_rows * lon_cols
    width = lon_cols + 2 * reach
    vmem, anywhere, smem = pltpu.VMEM, pl.ANY, pltpu.SMEM
    cot = cotangent.reshape(points, channels)
    band_shape = (lat_rows, basis_count * lon_cols, 3 * width)
    gemm = 2 * points * channels * hidden_units
    mix_gemm = 2 * points * channels * channels * basis_count
    band_gemm = 2 * lat_rows * basis_count * lon_cols * 3 * width * channels
    (bands,) = call(
        functools.partial(band_kernel, cols=lon_cols),
        (row_reach, kernel_taps),
        [smem, vmem],
        [(band_shape, low)],
        [vmem],
        [pltpu.VMEM((basis_count, 3, width), full)],
        0,
        2 * points * hidden_units * 4,
    )

    half_units, half_channels = hidden_units // 2, channels // 2
    mlp_half = (half_units + channels, channels)
    mix_half = (8, basis_count, half_channels // 8, channels)
    big, wide, many = (points, channels), (points, hidden_units), (basis_count, points, channels)
    core = place.flat % 2
    core_op = core[None].astype(jnp.int32)
    sized = (points // 5, hidden_units)
    feats, hidden, activated, pre_grad, mlp_send, mlp_keep = call(
        forward_kernel,
        (
            core_op, field_in, north, south, west, east, bands, mix_weight, up_weight,
            down_weight, cot,
        ),
        [smem] + [anywhere] * 10,
        [(many, low), (big, low), (wide, low), (wide, low), (mlp_half, low), (mlp_half, full)],
        [anywhere] * 4 + [vmem] * 2,
        [
            pltpu.VMEM((lat_rows + 2, width, channels), low),
            pltpu.VMEM(band_shape, low),
            pltpu.VMEM(mix_weight.shape, low),
            pltpu.VMEM(up_weight.shape, low),
            pltpu.VMEM(down_weight.shape, low),
            pltpu.VMEM(big, low),
            pltpu.VMEM(many, low),
            pltpu.VMEM(big, low),
            pltpu.VMEM(wide, low),
            pltpu.VMEM(wide, low),
            pltpu.VMEM((channels, points), low),
            pltpu.VMEM(sized, full),
            pltpu.VMEM(sized, full),
            pltpu.VMEM(sized, full),
            pltpu.VMEM(sized, full),
            pltpu.SemaphoreType.DMA((14,)),
        ],
        band_gemm + mix_gemm + 4 * gemm,
        4 * points * hidden_units * 4,
    )
    (hidden_grad,) = call(
        back_kernel,
        (pre_grad, up_weight, cot),
        [anywhere] * 3,
        [(big, low)],
        [anywhere],
        [
            pltpu.VMEM(wide, low),
            pltpu.VMEM(up_weight.shape, low),
            pltpu.VMEM(big, low),
            pltpu.VMEM(big, low),
            pltpu.SemaphoreType.DMA((10,)),
        ],
        gemm,
        3 * points * hidden_units * 2,
    )

    def mix_sums(start):
        return call(
            mix_kernel,
            (core_op, after(hidden_grad, start), feats),
            [smem] + [anywhere] * 2,
            [(mix_half, low), (mix_half, full)],
            [vmem] * 2,
            [
                pltpu.VMEM(big, low),
                pltpu.VMEM(many, low),
                pltpu.SemaphoreType.DMA((4,)),
            ],
            mix_gemm,
            3 * points * hidden_units * 2,
        )

    def block_of(start):
        return call(
            out_kernel,
            (after(hidden, start), activated, down_weight),
            [vmem] * 3,
            [(big, low)],
            [vmem],
            [],
            gemm,
            2 * points * hidden_units * 2,
        )[0]

    grads_shape = (lat_rows, basis_count * lon_cols, channels)

    def feature_grads(*start):
        return call(
            functools.partial(feature_grad_kernel, cols=lon_cols),
            (after(hidden_grad, *start), mix_weight),
            [anywhere] * 2,
            [(grads_shape, low)],
            [anywhere],
            [
                pltpu.VMEM(big, low),
                pltpu.VMEM(mix_weight.shape, low),
                pltpu.VMEM(grads_shape, low),
                pltpu.SemaphoreType.DMA((7,)),
            ],
            mix_gemm,
            3 * points * hidden_units * 2,
        )[0]

    def adjoint_of(feat_grads, *start):
        side = (lat_rows + 2, reach, channels)
        return call(
            functools.partial(adjoint_kernel, cols=lon_cols),
            (after(feat_grads, *start), bands),
            [anywhere] * 2,
            [
                ((lat_rows, lon_cols, channels), full), ((2, lon_cols, channels), full),
                (side, low), (side, low),
            ],
            [vmem] * 4,
            [
                pltpu.VMEM(grads_shape, low),
                pltpu.VMEM(band_shape, low),
                pltpu.VMEM((lat_rows + 2, width, channels), full),
                pltpu.SemaphoreType.DMA((2 * lat_rows,)),
            ],
            band_gemm,
            4 * points * hidden_units * 2,
        )

    grad_scale = 1.0 / math.sqrt(points * place.count)
    if place.count == 32:
        ring = Ring(place)
        block_shape = (2, 2, 2, mlp_half[0] // 8, channels)
        mlp = ring.to_core(mlp_keep.reshape(block_shape), mlp_send.reshape(block_shape))
        mlp_steps = ring.stages(mlp, grad_scale)
        mlp_out = next(mlp_steps)
        mix_send, mix_keep = mix_sums(mlp_out)
        block_out = block_of(mix_send)
        block_shape = (2, 2, 2) + mix_half[1:]
        mix = ring.to_core(mix_keep.reshape(block_shape), mix_send.reshape(block_shape))
        mix_steps = ring.stages(mix, grad_scale)
        mix_out = after(next(mix_steps), block_out)
        for turn in range(1, 9):
            mlp_out = mlp_steps.send(mlp_out)
            if turn < 8:
                mlp_out = after(mlp_out, mix_out)
            if turn == 1:
                feat_grads = feature_grads(mlp_out)
                mix_out = mix_steps.send(mix_out)
                mix_out = after(mix_out, mlp_out, feat_grads)
                continue
            if turn == 2:
                inner, rims, to_west, to_east = adjoint_of(feat_grads, mlp_out)
                mix_out = mix_steps.send(mix_out)
                mix_out = after(mix_out, mlp_out, to_west)
                from_east = lax.ppermute(to_west, "lon", place.west)
                from_west = lax.ppermute(to_east, "lon", place.east)
                continue
            if turn == 4:
                from_east = after(from_east, mlp_out)
            mix_out = mix_steps.send(mix_out)
            if turn < 8:
                mix_out = after(mix_out, mlp_out)
        mlp_halves = [half.reshape(mlp_half) for half in mlp_out]
        mix_halves = [half.reshape(mix_half) for half in mix_out]
        down_out = jnp.concatenate([half[:half_units] for half in mlp_halves])
        up_out = jnp.concatenate([half[half_units:] for half in mlp_halves], axis=1)
        mix_out = jnp.stack([half.swapaxes(0, 1) for half in mix_halves], axis=1)
        mix_out = mix_out.reshape(mix_weight.shape)
    else:
        mix_send, mix_keep = mix_sums(mlp_send)
        block_out = block_of(mlp_send)
        inner, rims, to_west, to_east = adjoint_of(feature_grads())
        from_east = lax.ppermute(to_west, "lon", place.west)
        from_west = lax.ppermute(to_east, "lon", place.east)

        def whole(keep, send):
            keep, send = keep[None], send.astype(full)[None]
            both = jnp.where(core == 0, jnp.concatenate([keep, send]), jnp.concatenate([send, keep]))
            return lax.psum(both, AXES) * grad_scale

        mlp_sum = whole(mlp_keep, mlp_send).astype(low)
        mix_sum = whole(mix_keep, mix_send).astype(low)
        down_out = mlp_sum[:, :half_units].reshape(down_weight.shape)
        up_out = jnp.concatenate([mlp_sum[0, half_units:], mlp_sum[1, half_units:]], axis=1)
        mix_out = mix_sum.transpose(2, 0, 1, 3, 4).reshape(mix_weight.shape)

    corner_east = jnp.stack([from_east[0], from_east[lat_rows + 1]]).astype(full)
    corner_west = jnp.stack([from_west[0], from_west[lat_rows + 1]]).astype(full)
    rims = rims.at[:, lon_cols - reach :].add(corner_east)
    rims = rims.at[:, :reach].add(corner_west).astype(low)
    near = lax.ppermute(jnp.where(place.even, rims[1], rims[0]), AXES, place.pairs)
    far = lax.ppermute(jnp.where(place.even, rims[0], rims[1]), AXES, place.bridges)
    adjoint = inner.at[:, lon_cols - reach :].add(from_east[1 : lat_rows + 1].astype(full))
    adjoint = adjoint.at[:, :reach].add(from_west[1 : lat_rows + 1].astype(full))
    adjoint = adjoint.at[0].add(jnp.where(place.even, far, near).astype(full))
    adjoint = adjoint.at[lat_rows - 1].add(jnp.where(place.even, near, far).astype(full))
    grad_field = (
        hidden_grad.astype(full).reshape(lat_rows, lon_cols, channels) + adjoint
    ).astype(low)
    return (block_out.reshape(field_in.shape), grad_field, mix_out, up_out, down_out)


def solution(mesh):
    placed = (
        P("lat", "lon", None),
        P(None, "lat", None, None),
        P("lat"),
        P(),
        P(),
        P(),
        P("lat", "lon", None),
    )
    return jax.shard_map(
        local,
        mesh=mesh,
        in_specs=placed,
        out_specs=(P("lat", "lon", None), P("lat", "lon", None), P(), P(), P()),
        check_vma=False,
    )
```

```python
import functools
import math

import jax
import jax.numpy as jnp
from jax import lax
from jax.experimental import pallas as pl
from jax.experimental.pallas import tpu as pltpu
from jax.sharding import PartitionSpec as P

inv_root_two = 0.7071067811865476
inv_root_tau = 0.3989422804014327
AXES = ("lat", "lon")


class Place:
    def __init__(self):
        self.lats = lax.axis_size("lat")
        self.lons = lax.axis_size("lon")
        self.count = self.lats * self.lons
        self.lat = lax.axis_index("lat")
        self.lon = lax.axis_index("lon")
        self.flat = self.lat * self.lons + self.lon
        lats, lons = self.lats, self.lons
        self.east = [(i, (i + 1) % lons) for i in range(lons)]
        self.west = [(j, i) for i, j in self.east]
        self.pairs = [
            (r * lons + c, (r ^ 1) * lons + c) for r in range(lats) for c in range(lons)
        ]
        self.bridges = []
        for r in range(lats):
            other = r - 1 if r % 2 == 0 else r + 1
            for c in range(lons):
                if 0 <= other < lats:
                    self.bridges.append((r * lons + c, other * lons + c))
                else:
                    self.bridges.append((r * lons + c, r * lons + (c + lons // 2) % lons))
        self.even = self.lat % 2 == 0


def route(place, mask_of):
    return [(i, i ^ mask_of(i)) for i in range(place.count)]


def send_along(place, block, mask_of):
    return lax.ppermute(block, AXES, route(place, mask_of))


def first_mask(i):
    return 2 if i % 2 == 0 else 4


def second_mask(i):
    return 4 if i % 2 == 0 else 2


def after(value, *others):
    return lax.optimization_barrier((value, *others))[0]


def pick(array, index):
    return lax.dynamic_index_in_dim(array, index, 0, keepdims=False)


def joined(bit, own, other):
    return jnp.concatenate([jnp.where(bit == 0, own, other), jnp.where(bit == 0, other, own)])


class Ring:
    def __init__(self, place):
        self.place = place
        self.core = place.flat % 2
        side_y, side_x = (place.flat // 2) % 2, (place.flat // 4) % 2
        self.first = jnp.where(self.core == 0, side_y, side_x)
        self.second = jnp.where(self.core == 0, side_x, side_y)
        self.near = (place.flat // 8) % 2

    def to_core(self, keep, send):
        got = send_along(self.place, send, lambda i: 1)
        return keep.astype(jnp.float32) + got.astype(jnp.float32)

    def leaving_first(self, buf):
        return pick(buf, 1 - self.first).astype(jnp.bfloat16)

    def first_step(self, buf, out):
        got = send_along(self.place, out, first_mask)
        return pick(buf, self.first) + got.astype(jnp.float32)

    def block(self, buf, over_second, over_near):
        at_second = 1 - self.second if over_second else self.second
        at_near = 1 - self.near if over_near else self.near
        return pick(pick(buf, at_second), at_near)

    def leaving_second(self, buf):
        return [
            self.block(buf, *over).astype(jnp.bfloat16)
            for over in ((True, False), (False, True), (True, True))
        ]

    def masks(self):
        return second_mask, lambda i: 8, lambda i: 8 + second_mask(i)

    def second_step(self, buf, outs):
        total = self.block(buf, False, False)
        for out, mask_of in zip(outs, self.masks()):
            total = total + send_along(self.place, out, mask_of).astype(jnp.float32)
        return total.astype(jnp.bfloat16)

    def far_step(self, own, scale):
        far = send_along(self.place, own, lambda i: 16)
        return ((own.astype(jnp.float32) + far.astype(jnp.float32)) * scale).astype(own.dtype)

    def gather(self, piece):
        place = self.place
        piece = piece[None]
        over_second, over_near, over_both = [
            send_along(place, piece, mask_of) for mask_of in self.masks()
        ]
        buf = joined(
            self.second,
            joined(self.near, piece, over_near),
            joined(self.near, over_second, over_both),
        )
        buf = joined(self.first, buf, send_along(place, buf, first_mask))
        other = send_along(place, buf, lambda i: 1)
        return jnp.where(self.core == 0, buf, other), jnp.where(self.core == 0, other, buf)


OVER_ROWS = (((0,), (0,)), ((), ()))
OVER_LANES = (((1,), (1,)), ((), ()))
VMEM_LIMIT = 56 * 1024 * 1024


def dot(left, right, dims=(((1,), (0,)), ((), ()))):
    return lax.dot_general(left, right, dims, preferred_element_type=jnp.float32)


def tiles(count, size, body):
    def step(i, carry):
        body(pl.ds(pl.multiple_of(i * size, size), size))
        return carry

    lax.fori_loop(0, count // size, step, 0)


def band_kernel(reach_ref, taps, bands, lines, *, cols):
    basis, rows, _, count = taps.shape
    width = lines.shape[2]
    away = jnp.abs(lax.broadcasted_iota(jnp.int32, (3, count), 1) - (count - 1) // 2)
    lines[...] = jnp.zeros(lines.shape, lines.dtype)

    def one_row(r, carry):
        inside = away <= reach_ref[r]
        for k in range(basis):
            lines[k, :, :count] = jnp.where(inside, taps[k, r].astype(jnp.float32), 0.0)
            for d in range(3):
                line = jnp.broadcast_to(lines[k, pl.ds(d, 1)], (cols, width))
                band = pltpu.roll(line, 0, 1, stride=1, stride_axis=0)
                bands[r, k * cols : (k + 1) * cols, d * width : (d + 1) * width] = band.astype(
                    bands.dtype
                )
        return carry

    lax.fori_loop(0, rows, one_row, 0)


def started(pairs, sems, first=0):
    copies = [pltpu.make_async_copy(a, b, sems.at[first + i]) for i, (a, b) in enumerate(pairs)]
    for copy in copies:
        copy.start()
    return copies


def finish(copies):
    for copy in copies:
        copy.wait()


def forward_kernel(
    core_ref, field, north, south, west, east, bands_in, mix_in, up_in, down_in, cot_in,
    feats_out, hidden_out, act_out, pre_out, send, keep,
    ext, bands, mix, up, down, cot, feats, hidden, act, pre_grad, turned, pre_a, pre_b, ag_a,
    ag_b, sems
):
    core = core_ref[0]
    rows, cols, channels = field.shape
    reach = west.shape[1]
    basis = mix.shape[0]
    points = rows * cols
    half_units = up.shape[1] // 2
    body, inner = pl.ds(1, rows), pl.ds(reach, cols)
    loads = started(
        [
            (field, ext.at[body, inner]),
            (west, ext.at[:, pl.ds(0, reach)]),
            (east, ext.at[:, pl.ds(reach + cols, reach)]),
            (north, ext.at[0, inner]),
            (south, ext.at[rows + 1, inner]),
            (bands_in, bands),
            (mix_in, mix),
            (up_in, up),
            (down_in, down),
            (cot_in, cot),
        ],
        sems,
    )
    finish(loads[:6])

    def two_rows(i, carry):
        for r in (2 * i, 2 * i + 1):
            window = ext[pl.ds(r, 3)].reshape(3 * ext.shape[1], channels)
            out = dot(bands[r], window).astype(feats.dtype)
            at = pl.ds(pl.multiple_of(r * cols, cols), cols)
            for k in range(basis):
                feats[k, at, :] = out[k * cols : (k + 1) * cols]
            hidden[at, :] = ext[r + 1, inner, :]
        return carry

    lax.fori_loop(0, rows // 2, two_rows, 0)
    stores = started([(feats, feats_out)], sems, 10)
    finish(loads[6:7])

    def mixing(at):
        total = hidden[at, :].astype(jnp.float32)
        for k in range(basis):
            total = total + dot(feats[k, at, :], mix[k])
        hidden[at, :] = total.astype(hidden.dtype)

    tiles(points, points // 3, mixing)
    finish(loads[7:])
    stores += started([(hidden, hidden_out)], sems, 11)
    size = pre_a.shape[0]
    slots = ((pre_a, ag_a), (pre_b, ag_b))

    def products(i):
        at = pl.ds(i * size, size)
        pre, ag = slots[i % 2]
        pre[...] = dot(hidden[at, :], up[...])
        ag[...] = dot(cot[at, :], down[...], OVER_LANES)

    def activation(i):
        at = pl.ds(i * size, size)
        pre, ag = slots[i % 2]
        value = pre[...]
        phi = 0.5 * (1.0 + lax.erf(value * inv_root_two))
        act[at, :] = (value * phi).astype(act.dtype)
        slope = phi + value * jnp.exp(-0.5 * value * value) * inv_root_tau
        pre_grad[at, :] = (ag[...] * slope).astype(pre_grad.dtype)

    products(0)
    for i in range(points // size):
        if (i + 1) * size < points:
            products(i + 1)
        activation(i)
    stores += started([(act, act_out), (pre_grad, pre_out)], sems, 12)
    turned[...] = hidden[...].T

    def sums(half, out):
        at = pl.ds(pl.multiple_of(half * half_units, half_units), half_units)
        out[:half_units] = dot(act[:, at], cot[...], OVER_ROWS).astype(out.dtype)
        out[half_units:] = dot(turned[...], pre_grad[:, at]).astype(out.dtype)

    sums(1 - core, send)
    sums(core, keep)
    finish(stores)


def backward_kernel(
    core_ref, pre_in, up_in, cot_in, feats_in, hg_out, send, keep,
    pre_grad, up, cot, feats, hg, sems
):
    core = core_ref[0]
    basis, points, channels = feats.shape
    half_channels = channels // 2
    loads = started([(pre_in, pre_grad), (up_in, up), (cot_in, cot), (feats_in, feats)], sems)
    finish(loads[:3])

    def back(at):
        total = cot[at, :].astype(jnp.float32) + dot(pre_grad[at, :], up[...], OVER_LANES)
        hg[at, :] = total.astype(hg.dtype)

    tiles(points, points // 3, back)
    stores = started([(hg, hg_out)], sems, 4)
    finish(loads[3:])

    def sums(half, out):
        at = pl.ds(pl.multiple_of(half * half_channels, half_channels), half_channels)
        for k in range(basis):
            part = dot(feats[k, :, at], hg[...], OVER_ROWS).astype(out.dtype)
            out[:, k] = part.reshape(out.shape[0], -1, channels)

    sums(1 - core, send)
    sums(core, keep)
    finish(stores)


def out_kernel(hidden, act, down, block):
    def forward(at):
        total = hidden[at, :].astype(jnp.float32) + dot(act[at, :], down[...])
        block[at, :] = total.astype(block.dtype)

    tiles(hidden.shape[0], hidden.shape[0] // 3, forward)


def adjoint_kernel(
    hg_in, mix_in, bands_in, inner_out, rim_out, west_out, east_out,
    hg, mix, bands, grads, pulled, sems, *, cols
):
    basis, channels = mix.shape[0], mix.shape[1]
    rows, width = pulled.shape[0] - 2, pulled.shape[1]
    reach = (width - cols) // 2
    loads = started([(mix_in, mix), (hg_in, hg), (bands_in, bands)], sems)
    pulled[...] = jnp.zeros(pulled.shape, pulled.dtype)
    finish(loads[:2])
    group = 5 if rows % 5 == 0 else 1

    def feature_grads(i, carry):
        at = pl.ds(pl.multiple_of(i * group * cols, group * cols), group * cols)
        for k in range(basis):
            part = dot(hg[at, :], mix[k], OVER_LANES).astype(grads.dtype)
            grads[pl.ds(i * group, group), pl.ds(k * cols, cols)] = part.reshape(
                group, cols, channels
            )
        return carry

    lax.fori_loop(0, rows // group, feature_grads, 0)
    finish(loads[2:])

    def one_row(r, carry):
        part = dot(bands[r], grads[r], OVER_ROWS)
        pulled[pl.ds(r, 3)] += part.reshape(3, width, channels)
        return carry

    lax.fori_loop(0, rows, one_row, 0)
    west_out[...] = pulled[:, :reach].astype(west_out.dtype)
    east_out[...] = pulled[:, reach + cols :].astype(east_out.dtype)
    inner_out[...] = pulled[1 : rows + 1, reach : reach + cols]
    for n, r in enumerate((0, rows + 1)):
        rim_out[n] = pulled[r, reach : reach + cols]


def call(kernel, operands, kinds, shapes, out_kinds, scratch, flops, nbytes):
    return pl.pallas_call(
        kernel,
        out_shape=[jax.ShapeDtypeStruct(shape, kind) for shape, kind in shapes],
        in_specs=[pl.BlockSpec(memory_space=kind) for kind in kinds],
        out_specs=[pl.BlockSpec(memory_space=kind) for kind in out_kinds],
        scratch_shapes=scratch,
        compiler_params=pltpu.CompilerParams(vmem_limit_bytes=VMEM_LIMIT),
        cost_estimate=pl.CostEstimate(flops=flops, bytes_accessed=nbytes, transcendentals=0),
    )(*operands)


def local(field_in, kernel_taps, row_reach, mix_weight, up_weight, down_weight, cotangent):
    lat_rows, lon_cols, channels = field_in.shape
    basis_count = kernel_taps.shape[0]
    tap_count = kernel_taps.shape[3]
    reach = (tap_count - 1) // 2
    hidden_units = up_weight.shape[1]
    place = Place()

    top, bottom = field_in[0], field_in[lat_rows - 1]
    inner = lax.ppermute(jnp.where(place.even, bottom, top), AXES, place.pairs)
    outer = lax.ppermute(jnp.where(place.even, top, bottom), AXES, place.bridges)
    north = jnp.where(place.even, outer, inner)
    south = jnp.where(place.even, inner, outer)

    def column(at):
        return jnp.concatenate([north[None, at], field_in[:, at], south[None, at]])

    west = lax.ppermute(column(slice(lon_cols - reach, lon_cols)), "lon", place.east)
    east = lax.ppermute(column(slice(0, reach)), "lon", place.west)

    low, full = jnp.bfloat16, jnp.float32
    points = lat_rows * lon_cols
    width = lon_cols + 2 * reach
    vmem, anywhere, smem = pltpu.VMEM, pl.ANY, pltpu.SMEM
    cot = cotangent.reshape(points, channels)
    band_shape = (lat_rows, basis_count * lon_cols, 3 * width)
    gemm = 2 * points * channels * hidden_units
    mix_gemm = 2 * points * channels * channels * basis_count
    band_gemm = 2 * lat_rows * basis_count * lon_cols * 3 * width * channels
    (bands,) = call(
        functools.partial(band_kernel, cols=lon_cols),
        (row_reach, kernel_taps),
        [smem, vmem],
        [(band_shape, low)],
        [vmem],
        [pltpu.VMEM((basis_count, 3, width), full)],
        0,
        2 * points * hidden_units * 4,
    )

    half_units, half_channels = hidden_units // 2, channels // 2
    mlp_half = (half_units + channels, channels)
    mix_half = (8, basis_count, half_channels // 8, channels)
    big, wide, many = (points, channels), (points, hidden_units), (basis_count, points, channels)
    core = place.flat % 2
    core_op = core[None].astype(jnp.int32)
    sized = (points // 5, hidden_units)
    feats, hidden, activated, pre_grad, mlp_send, mlp_keep = call(
        forward_kernel,
        (
            core_op, field_in, north, south, west, east, bands, mix_weight, up_weight,
            down_weight, cot,
        ),
        [smem] + [anywhere] * 10,
        [(many, low), (big, low), (wide, low), (wide, low), (mlp_half, low), (mlp_half, low)],
        [anywhere] * 4 + [vmem] * 2,
        [
            pltpu.VMEM((lat_rows + 2, width, channels), low),
            pltpu.VMEM(band_shape, low),
            pltpu.VMEM(mix_weight.shape, low),
            pltpu.VMEM(up_weight.shape, low),
            pltpu.VMEM(down_weight.shape, low),
            pltpu.VMEM(big, low),
            pltpu.VMEM(many, low),
            pltpu.VMEM(big, low),
            pltpu.VMEM(wide, low),
            pltpu.VMEM(wide, low),
            pltpu.VMEM((channels, points), low),
            pltpu.VMEM(sized, full),
            pltpu.VMEM(sized, full),
            pltpu.VMEM(sized, full),
            pltpu.VMEM(sized, full),
            pltpu.SemaphoreType.DMA((14,)),
        ],
        band_gemm + mix_gemm + 4 * gemm,
        4 * points * hidden_units * 4,
    )
    def backward(start):
        return call(
            backward_kernel,
            (core_op, after(pre_grad, start), up_weight, cot, feats),
            [smem] + [anywhere] * 4,
            [(big, low), (mix_half, low), (mix_half, low)],
            [anywhere] + [vmem] * 2,
            [
                pltpu.VMEM(wide, low),
                pltpu.VMEM(up_weight.shape, low),
                pltpu.VMEM(big, low),
                pltpu.VMEM(many, low),
                pltpu.VMEM(big, low),
                pltpu.SemaphoreType.DMA((5,)),
            ],
            mix_gemm + gemm,
            3 * points * hidden_units * 4,
        )

    def block_of():
        return call(
            out_kernel,
            (hidden, activated, down_weight),
            [vmem] * 3,
            [(big, low)],
            [vmem],
            [],
            gemm,
            2 * points * hidden_units * 4,
        )[0]

    def adjoint_of(hidden_grad, *start):
        side = (lat_rows + 2, reach, channels)
        return call(
            functools.partial(adjoint_kernel, cols=lon_cols),
            (after(hidden_grad, *start), mix_weight, bands),
            [anywhere] * 3,
            [
                ((lat_rows, lon_cols, channels), full), ((2, lon_cols, channels), full),
                (side, low), (side, low),
            ],
            [vmem] * 4,
            [
                pltpu.VMEM(big, low),
                pltpu.VMEM(mix_weight.shape, low),
                pltpu.VMEM(band_shape, low),
                pltpu.VMEM((lat_rows, basis_count * lon_cols, channels), low),
                pltpu.VMEM((lat_rows + 2, width, channels), full),
                pltpu.SemaphoreType.DMA((3,)),
            ],
            band_gemm + mix_gemm,
            3 * points * hidden_units * 4,
        )

    grad_scale = 1.0 / math.sqrt(points * place.count)
    if place.count == 32:
        ring = Ring(place)
        block_shape = (2, 2, 2, mlp_half[0] // 8, channels)
        mlp = ring.to_core(mlp_keep.reshape(block_shape), mlp_send.reshape(block_shape))
        block_out = block_of()
        mlp_out = ring.leaving_first(after(mlp, block_out))
        hidden_grad, mix_send, mix_keep = backward(mlp_out)
        block_shape = (2, 2, 2) + mix_half[1:]
        mix = ring.to_core(mix_keep.reshape(block_shape), mix_send.reshape(block_shape))
        mix_out = ring.leaving_first(mix)
        mlp = after(ring.first_step(mlp, mlp_out), mix_out)
        mlp_out = ring.leaving_second(mlp)
        inner, rims, to_west, to_east = adjoint_of(hidden_grad, mix_out, *mlp_out)
        mix = after(ring.first_step(mix, mix_out), to_west, *mlp_out)
        mix_out = ring.leaving_second(mix)
        mlp = after(ring.second_step(mlp, mlp_out), *mix_out)
        mix = after(ring.second_step(mix, mix_out), mlp)
        from_east = lax.ppermute(to_west, "lon", place.west)
        from_west = lax.ppermute(to_east, "lon", place.east)
        mlp_halves = ring.gather(ring.far_step(mlp, grad_scale))
        mix_halves = ring.gather(ring.far_step(mix, grad_scale))
        from_east = after(from_east, mix)
        mlp_halves = [half.reshape(mlp_half) for half in mlp_halves]
        mix_halves = [half.reshape(mix_half) for half in mix_halves]
        down_out = jnp.concatenate([half[:half_units] for half in mlp_halves])
        up_out = jnp.concatenate([half[half_units:] for half in mlp_halves], axis=1)
        mix_out = jnp.stack([half.swapaxes(0, 1) for half in mix_halves], axis=1)
        mix_out = mix_out.reshape(mix_weight.shape)
    else:
        block_out = block_of()
        hidden_grad, mix_send, mix_keep = backward(mlp_send)
        inner, rims, to_west, to_east = adjoint_of(hidden_grad)
        from_east = lax.ppermute(to_west, "lon", place.west)
        from_west = lax.ppermute(to_east, "lon", place.east)

        def whole(keep, send):
            keep, send = keep.astype(full)[None], send.astype(full)[None]
            both = jnp.where(core == 0, jnp.concatenate([keep, send]), jnp.concatenate([send, keep]))
            return lax.psum(both, AXES) * grad_scale

        mlp_sum = whole(mlp_keep, mlp_send).astype(low)
        mix_sum = whole(mix_keep, mix_send).astype(low)
        down_out = mlp_sum[:, :half_units].reshape(down_weight.shape)
        up_out = jnp.concatenate([mlp_sum[0, half_units:], mlp_sum[1, half_units:]], axis=1)
        mix_out = mix_sum.transpose(2, 0, 1, 3, 4).reshape(mix_weight.shape)

    corner_east = jnp.stack([from_east[0], from_east[lat_rows + 1]]).astype(full)
    corner_west = jnp.stack([from_west[0], from_west[lat_rows + 1]]).astype(full)
    rims = rims.at[:, lon_cols - reach :].add(corner_east)
    rims = rims.at[:, :reach].add(corner_west).astype(low)
    near = lax.ppermute(jnp.where(place.even, rims[1], rims[0]), AXES, place.pairs)
    far = lax.ppermute(jnp.where(place.even, rims[0], rims[1]), AXES, place.bridges)
    adjoint = inner.at[:, lon_cols - reach :].add(from_east[1 : lat_rows + 1].astype(full))
    adjoint = adjoint.at[:, :reach].add(from_west[1 : lat_rows + 1].astype(full))
    adjoint = adjoint.at[0].add(jnp.where(place.even, far, near).astype(full))
    adjoint = adjoint.at[lat_rows - 1].add(jnp.where(place.even, near, far).astype(full))
    grad_field = (
        hidden_grad.astype(full).reshape(lat_rows, lon_cols, channels) + adjoint
    ).astype(low)
    return (block_out.reshape(field_in.shape), grad_field, mix_out, up_out, down_out)


def solution(mesh):
    placed = (
        P("lat", "lon", None),
        P(None, "lat", None, None),
        P("lat"),
        P(),
        P(),
        P(),
        P("lat", "lon", None),
    )
    return jax.shard_map(
        local,
        mesh=mesh,
        in_specs=placed,
        out_specs=(P("lat", "lon", None), P("lat", "lon", None), P(), P(), P()),
        check_vma=False,
    )
```

```python
import functools
import math

import jax
import jax.numpy as jnp
from jax import lax
from jax.experimental import pallas as pl
from jax.experimental.pallas import tpu as pltpu
from jax.sharding import PartitionSpec as P

inv_root_two = 0.7071067811865476
inv_root_tau = 0.3989422804014327
AXES = ("lat", "lon")


class Place:
    def __init__(self):
        self.lats = lax.axis_size("lat")
        self.lons = lax.axis_size("lon")
        self.count = self.lats * self.lons
        self.lat = lax.axis_index("lat")
        self.lon = lax.axis_index("lon")
        self.flat = self.lat * self.lons + self.lon
        lats, lons = self.lats, self.lons
        self.east = [(i, (i + 1) % lons) for i in range(lons)]
        self.west = [(j, i) for i, j in self.east]
        self.pairs = [
            (r * lons + c, (r ^ 1) * lons + c) for r in range(lats) for c in range(lons)
        ]
        self.bridges = []
        for r in range(lats):
            other = r - 1 if r % 2 == 0 else r + 1
            for c in range(lons):
                if 0 <= other < lats:
                    self.bridges.append((r * lons + c, other * lons + c))
                else:
                    self.bridges.append((r * lons + c, r * lons + (c + lons // 2) % lons))
        self.even = self.lat % 2 == 0


def route(place, mask_of):
    return [(i, i ^ mask_of(i)) for i in range(place.count)]


def send_along(place, block, mask_of):
    return lax.ppermute(block, AXES, route(place, mask_of))


def first_mask(i):
    return 2 if i % 2 == 0 else 4


def second_mask(i):
    return 4 if i % 2 == 0 else 2


def after(value, *others):
    return lax.optimization_barrier((value, *others))[0]


def pick(array, index):
    return lax.dynamic_index_in_dim(array, index, 0, keepdims=False)


def joined(bit, own, other):
    return jnp.concatenate([jnp.where(bit == 0, own, other), jnp.where(bit == 0, other, own)])


class Ring:
    def __init__(self, place):
        self.place = place
        self.core = place.flat % 2
        side_y, side_x = (place.flat // 2) % 2, (place.flat // 4) % 2
        self.first = jnp.where(self.core == 0, side_y, side_x)
        self.second = jnp.where(self.core == 0, side_x, side_y)
        self.near = (place.flat // 8) % 2

    def to_core(self, keep, send):
        got = send_along(self.place, send, lambda i: 1)
        return keep.astype(jnp.float32) + got.astype(jnp.float32)

    def leaving_first(self, buf):
        return pick(buf, 1 - self.first).astype(jnp.bfloat16)

    def first_step(self, buf, out):
        got = send_along(self.place, out, first_mask)
        return pick(buf, self.first) + got.astype(jnp.float32)

    def block(self, buf, over_second, over_near):
        at_second = 1 - self.second if over_second else self.second
        at_near = 1 - self.near if over_near else self.near
        return pick(pick(buf, at_second), at_near)

    def leaving_second(self, buf):
        return [
            self.block(buf, *over).astype(jnp.bfloat16)
            for over in ((True, False), (False, True), (True, True))
        ]

    def masks(self):
        return second_mask, lambda i: 8, lambda i: 8 + second_mask(i)

    def second_step(self, buf, outs):
        total = self.block(buf, False, False)
        for out, mask_of in zip(outs, self.masks()):
            total = total + send_along(self.place, out, mask_of).astype(jnp.float32)
        return total.astype(jnp.bfloat16)

    def far_step(self, own, scale):
        far = send_along(self.place, own, lambda i: 16)
        return ((own.astype(jnp.float32) + far.astype(jnp.float32)) * scale).astype(own.dtype)

    def gather(self, piece):
        place = self.place
        piece = piece[None]
        over_second, over_near, over_both = [
            send_along(place, piece, mask_of) for mask_of in self.masks()
        ]
        buf = joined(
            self.second,
            joined(self.near, piece, over_near),
            joined(self.near, over_second, over_both),
        )
        buf = joined(self.first, buf, send_along(place, buf, first_mask))
        other = send_along(place, buf, lambda i: 1)
        return jnp.where(self.core == 0, buf, other), jnp.where(self.core == 0, other, buf)


OVER_ROWS = (((0,), (0,)), ((), ()))
OVER_LANES = (((1,), (1,)), ((), ()))
VMEM_LIMIT = 56 * 1024 * 1024


def dot(left, right, dims=(((1,), (0,)), ((), ()))):
    return lax.dot_general(left, right, dims, preferred_element_type=jnp.float32)


def tiles(count, size, body):
    def step(i, carry):
        body(pl.ds(pl.multiple_of(i * size, size), size))
        return carry

    lax.fori_loop(0, count // size, step, 0)


def band_kernel(reach_ref, taps, bands, lines, *, cols):
    basis, rows, _, count = taps.shape
    width = lines.shape[2]
    away = jnp.abs(lax.broadcasted_iota(jnp.int32, (3, count), 1) - (count - 1) // 2)
    lines[...] = jnp.zeros(lines.shape, lines.dtype)

    def one_row(r, carry):
        inside = away <= reach_ref[r]
        for k in range(basis):
            lines[k, :, :count] = jnp.where(inside, taps[k, r].astype(jnp.float32), 0.0)
            for d in range(3):
                line = jnp.broadcast_to(lines[k, pl.ds(d, 1)], (cols, width))
                band = pltpu.roll(line, 0, 1, stride=1, stride_axis=0)
                bands[r, k * cols : (k + 1) * cols, d * width : (d + 1) * width] = band.astype(
                    bands.dtype
                )
        return carry

    lax.fori_loop(0, rows, one_row, 0)


def started(pairs, sems, first=0):
    copies = [pltpu.make_async_copy(a, b, sems.at[first + i]) for i, (a, b) in enumerate(pairs)]
    for copy in copies:
        copy.start()
    return copies


def finish(copies):
    for copy in copies:
        copy.wait()


def forward_kernel(
    core_ref, field, north, south, west, east, corners_west, corners_east, bands_in, mix_in,
    up_in, down_in, cot_in,
    feats_out, hidden_out, act_out, pre_out, send_out, keep_out,
    ext, bands, mix, up, down, cot, feats, hidden, act, pre_grad, turned, pre_a, pre_b, ag_a,
    ag_b, send, keep, sems
):
    core = core_ref[0]
    rows, cols, channels = field.shape
    reach = west.shape[1]
    basis = mix.shape[0]
    points = rows * cols
    half_units = up.shape[1] // 2
    body, inner = pl.ds(1, rows), pl.ds(reach, cols)
    begin, end = pl.ds(0, reach), pl.ds(reach + cols, reach)
    loads = started(
        [
            (field, ext.at[body, inner]),
            (west, ext.at[body, begin]),
            (east, ext.at[body, end]),
            (north, ext.at[0, inner]),
            (south, ext.at[rows + 1, inner]),
            (corners_west.at[0], ext.at[0, begin]),
            (corners_west.at[1], ext.at[rows + 1, begin]),
            (corners_east.at[0], ext.at[0, end]),
            (corners_east.at[1], ext.at[rows + 1, end]),
        ],
        sems,
    )
    band_loads = started([(bands_in.at[r], bands.at[r]) for r in range(rows)], sems, 9)
    late = 9 + rows
    weights = started([(mix_in, mix), (up_in, up), (down_in, down), (cot_in, cot)], sems, late)
    finish(loads)

    for r in range(rows):
        finish(band_loads[r : r + 1])
        window = ext[r : r + 3].reshape(3 * ext.shape[1], channels)
        out = dot(bands[r], window).astype(feats.dtype)
        at = pl.ds(r * cols, cols)
        for k in range(basis):
            feats[k, at, :] = out[k * cols : (k + 1) * cols]
        hidden[at, :] = ext[r + 1, inner, :]
    stores = started([(feats, feats_out)], sems, late + 4)
    finish(weights[:1])

    for i in range(3):
        at = pl.ds(i * (points // 3), points // 3)
        total = hidden[at, :].astype(jnp.float32)
        for k in range(basis):
            total = total + dot(feats[k, at, :], mix[k])
        hidden[at, :] = total.astype(hidden.dtype)
    finish(weights[1:])
    stores += started([(hidden, hidden_out)], sems, late + 5)
    size = pre_a.shape[0]
    slots = ((pre_a, ag_a), (pre_b, ag_b))

    def products(i):
        at = pl.ds(i * size, size)
        pre, ag = slots[i % 2]
        pre[...] = dot(hidden[at, :], up[...])
        ag[...] = dot(cot[at, :], down[...], OVER_LANES)

    def activation(i):
        at = pl.ds(i * size, size)
        pre, ag = slots[i % 2]
        value = pre[...]
        phi = 0.5 * (1.0 + lax.erf(value * inv_root_two))
        act[at, :] = (value * phi).astype(act.dtype)
        slope = phi + value * jnp.exp(-0.5 * value * value) * inv_root_tau
        pre_grad[at, :] = (ag[...] * slope).astype(pre_grad.dtype)

    products(0)
    for i in range(points // size):
        if (i + 1) * size < points:
            products(i + 1)
        activation(i)
    stores += started([(act, act_out), (pre_grad, pre_out)], sems, late + 6)
    turned[...] = hidden[...].T

    def sums(half, out):
        at = pl.ds(pl.multiple_of(half * half_units, half_units), half_units)
        out[:half_units] = dot(act[:, at], cot[...], OVER_ROWS).astype(out.dtype)
        out[half_units:] = dot(turned[...], pre_grad[:, at]).astype(out.dtype)

    sums(1 - core, send)
    stores += started([(send, send_out)], sems, late + 8)
    sums(core, keep)
    stores += started([(keep, keep_out)], sems, late + 9)
    finish(stores)


def backward_kernel(
    core_ref, pre_in, up_in, cot_in, feats_in, hg_out, send_out, keep_out,
    pre_grad, up, cot, feats, hg, send, keep, sems
):
    core = core_ref[0]
    basis, points, channels = feats.shape
    half_channels = channels // 2
    parts = [pl.ds(i * (points // 3), points // 3) for i in range(3)]
    weights = started([(up_in, up)], sems)
    loads = started([(pre_in.at[at], pre_grad.at[at]) for at in parts], sems, 1)
    cot_loads = started([(cot_in.at[at], cot.at[at]) for at in parts], sems, 4)
    feat_loads = started([(feats_in.at[k], feats.at[k]) for k in range(basis)], sems, 7)
    late = 7 + basis
    finish(weights)
    for i, at in enumerate(parts):
        finish([loads[i], cot_loads[i]])
        total = cot[at, :].astype(jnp.float32) + dot(pre_grad[at, :], up[...], OVER_LANES)
        hg[at, :] = total.astype(hg.dtype)
    stores = started([(hg, hg_out)], sems, late)
    finish(feat_loads)

    def sums(half, out):
        at = pl.ds(pl.multiple_of(half * half_channels, half_channels), half_channels)
        for k in range(basis):
            part = dot(feats[k, :, at], hg[...], OVER_ROWS).astype(out.dtype)
            out[:, k] = part.reshape(out.shape[0], -1, channels)

    sums(1 - core, send)
    stores += started([(send, send_out)], sems, late + 1)
    sums(core, keep)
    stores += started([(keep, keep_out)], sems, late + 2)
    finish(stores)


def out_kernel(hidden_in, act_in, down_in, block_out, hidden, act, down, block, sems):
    points = hidden.shape[0]
    parts = [pl.ds(i * (points // 3), points // 3) for i in range(3)]
    weights = started([(down_in, down)], sems)
    loads = started([(act_in.at[at], act.at[at]) for at in parts], sems, 1)
    more = started([(hidden_in.at[at], hidden.at[at]) for at in parts], sems, 4)
    finish(weights)
    stores = []
    for i, at in enumerate(parts):
        finish([loads[i], more[i]])
        total = hidden[at, :].astype(jnp.float32) + dot(act[at, :], down[...])
        block[at, :] = total.astype(block.dtype)
        stores += started([(block.at[at], block_out.at[at])], sems, 7 + i)
    finish(stores)


def adjoint_kernel(
    hg_in, mix_in, bands_in, inner_out, rim_out, west_out, east_out,
    hg, mix, bands, grads, pulled, inner, sems, *, cols
):
    basis, channels = mix.shape[0], mix.shape[1]
    rows, width = pulled.shape[0] - 2, pulled.shape[1]
    reach = (width - cols) // 2
    loads = started([(hg_in, hg)], sems)
    loads += started([(mix_in.at[k], mix.at[k]) for k in range(basis)], sems, 1)
    late = 1 + basis
    band_loads = started([(bands_in.at[r], bands.at[r]) for r in range(rows)], sems, late)
    pulled[...] = jnp.zeros(pulled.shape, pulled.dtype)
    group = 5 if rows % 5 == 0 else 1
    finish(loads[:1])
    for k in range(basis):
        finish(loads[1 + k : 2 + k])
        for r in range(0, rows, group):
            part = dot(hg[r * cols : (r + group) * cols, :], mix[k], OVER_LANES)
            grads[r : r + group, k * cols : (k + 1) * cols] = part.astype(grads.dtype).reshape(
                group, cols, channels
            )
    stores = []

    def give(row):
        own = hg[(row - 1) * cols : row * cols, :].astype(jnp.float32)
        inner[row - 1] = (pulled[row, reach : reach + cols] + own).astype(inner.dtype)
        copies = [(inner.at[row - 1], inner_out.at[row - 1])]
        stores.extend(started(copies, sems, late + rows + row - 1))

    for r in range(rows):
        finish(band_loads[r : r + 1])
        part = dot(bands[r], grads[r], OVER_ROWS)
        pulled[r : r + 3] += part.reshape(3, width, channels)
        if r:
            give(r)
    give(rows)
    west_out[...] = pulled[:, :reach].astype(west_out.dtype)
    east_out[...] = pulled[:, reach + cols :].astype(east_out.dtype)
    for n, r in enumerate((0, rows + 1)):
        rim_out[n] = pulled[r, reach : reach + cols]
    finish(stores)


def call(kernel, operands, kinds, shapes, out_kinds, scratch, flops, nbytes):
    return pl.pallas_call(
        kernel,
        out_shape=[jax.ShapeDtypeStruct(shape, kind) for shape, kind in shapes],
        in_specs=[pl.BlockSpec(memory_space=kind) for kind in kinds],
        out_specs=[pl.BlockSpec(memory_space=kind) for kind in out_kinds],
        scratch_shapes=scratch,
        compiler_params=pltpu.CompilerParams(vmem_limit_bytes=VMEM_LIMIT),
        cost_estimate=pl.CostEstimate(flops=flops, bytes_accessed=nbytes, transcendentals=0),
    )(*operands)


def local(field_in, kernel_taps, row_reach, mix_weight, up_weight, down_weight, cotangent):
    lat_rows, lon_cols, channels = field_in.shape
    basis_count = kernel_taps.shape[0]
    tap_count = kernel_taps.shape[3]
    reach = (tap_count - 1) // 2
    hidden_units = up_weight.shape[1]
    place = Place()

    top, bottom = field_in[0], field_in[lat_rows - 1]
    inner = lax.ppermute(jnp.where(place.even, bottom, top), AXES, place.pairs)
    outer = lax.ppermute(jnp.where(place.even, top, bottom), AXES, place.bridges)
    west = lax.ppermute(field_in[:, lon_cols - reach :], "lon", place.east)
    east = lax.ppermute(field_in[:, :reach], "lon", place.west)
    north = jnp.where(place.even, outer, inner)
    south = jnp.where(place.even, inner, outer)
    corners = jnp.stack([north[lon_cols - reach :], south[lon_cols - reach :]])
    corners_west = lax.ppermute(corners, "lon", place.east)
    corners = jnp.stack([north[:reach], south[:reach]])
    corners_east = lax.ppermute(corners, "lon", place.west)

    low, full = jnp.bfloat16, jnp.float32
    points = lat_rows * lon_cols
    width = lon_cols + 2 * reach
    vmem, anywhere, smem = pltpu.VMEM, pl.ANY, pltpu.SMEM
    cot = cotangent.reshape(points, channels)
    band_shape = (lat_rows, basis_count * lon_cols, 3 * width)
    gemm = 2 * points * channels * hidden_units
    mix_gemm = 2 * points * channels * channels * basis_count
    band_gemm = 2 * lat_rows * basis_count * lon_cols * 3 * width * channels
    (bands,) = call(
        functools.partial(band_kernel, cols=lon_cols),
        (row_reach, kernel_taps),
        [smem, vmem],
        [(band_shape, low)],
        [vmem],
        [pltpu.VMEM((basis_count, 3, width), full)],
        0,
        2 * points * hidden_units * 4,
    )

    half_units, half_channels = hidden_units // 2, channels // 2
    mlp_half = (half_units + channels, channels)
    mix_half = (8, basis_count, half_channels // 8, channels)
    big, wide, many = (points, channels), (points, hidden_units), (basis_count, points, channels)
    core = place.flat % 2
    core_op = core[None].astype(jnp.int32)
    sized = (points // 5, hidden_units)
    feats, hidden, activated, pre_grad, mlp_send, mlp_keep = call(
        forward_kernel,
        (
            core_op, field_in, north, south, west, east, corners_west, corners_east, bands,
            mix_weight, up_weight, down_weight, cot,
        ),
        [smem] + [anywhere] * 12,
        [(many, low), (big, low), (wide, low), (wide, low), (mlp_half, low), (mlp_half, low)],
        [anywhere] * 6,
        [
            pltpu.VMEM((lat_rows + 2, width, channels), low),
            pltpu.VMEM(band_shape, low),
            pltpu.VMEM(mix_weight.shape, low),
            pltpu.VMEM(up_weight.shape, low),
            pltpu.VMEM(down_weight.shape, low),
            pltpu.VMEM(big, low),
            pltpu.VMEM(many, low),
            pltpu.VMEM(big, low),
            pltpu.VMEM(wide, low),
            pltpu.VMEM(wide, low),
            pltpu.VMEM((channels, points), low),
            pltpu.VMEM(sized, full),
            pltpu.VMEM(sized, full),
            pltpu.VMEM(sized, full),
            pltpu.VMEM(sized, full),
            pltpu.VMEM(mlp_half, low),
            pltpu.VMEM(mlp_half, low),
            pltpu.SemaphoreType.DMA((19 + lat_rows,)),
        ],
        band_gemm + mix_gemm + 4 * gemm,
        4 * points * hidden_units * 4,
    )
    def backward(start):
        return call(
            backward_kernel,
            (core_op, after(pre_grad, start), up_weight, cot, feats),
            [smem] + [anywhere] * 4,
            [(big, low), (mix_half, low), (mix_half, low)],
            [anywhere] * 3,
            [
                pltpu.VMEM(wide, low),
                pltpu.VMEM(up_weight.shape, low),
                pltpu.VMEM(big, low),
                pltpu.VMEM(many, low),
                pltpu.VMEM(big, low),
                pltpu.VMEM(mix_half, low),
                pltpu.VMEM(mix_half, low),
                pltpu.SemaphoreType.DMA((10 + basis_count,)),
            ],
            mix_gemm + gemm,
            3 * points * hidden_units * 4,
        )

    def block_of():
        return call(
            out_kernel,
            (hidden, activated, down_weight),
            [anywhere] * 3,
            [(big, low)],
            [anywhere],
            [
                pltpu.VMEM(big, low),
                pltpu.VMEM(wide, low),
                pltpu.VMEM(down_weight.shape, low),
                pltpu.VMEM(big, low),
                pltpu.SemaphoreType.DMA((10,)),
            ],
            gemm,
            2 * points * hidden_units * 4,
        )[0]

    def adjoint_of(hidden_grad, *start):
        side = (lat_rows + 2, reach, channels)
        return call(
            functools.partial(adjoint_kernel, cols=lon_cols),
            (after(hidden_grad, *start), mix_weight, bands),
            [anywhere] * 3,
            [
                (field_in.shape, low), ((2, lon_cols, channels), full), (side, low), (side, low),
            ],
            [anywhere] + [vmem] * 3,
            [
                pltpu.VMEM(big, low),
                pltpu.VMEM(mix_weight.shape, low),
                pltpu.VMEM(band_shape, low),
                pltpu.VMEM((lat_rows, basis_count * lon_cols, channels), low),
                pltpu.VMEM((lat_rows + 2, width, channels), full),
                pltpu.VMEM(field_in.shape, low),
                pltpu.SemaphoreType.DMA((1 + basis_count + 2 * lat_rows,)),
            ],
            band_gemm + mix_gemm,
            3 * points * hidden_units * 4,
        )

    grad_scale = 1.0 / math.sqrt(points * place.count)
    if place.count == 32:
        ring = Ring(place)
        block_shape = (2, 2, 2, mlp_half[0] // 8, channels)
        mlp = ring.to_core(mlp_keep.reshape(block_shape), mlp_send.reshape(block_shape))
        block_out = block_of()
        mlp_out = ring.leaving_first(after(mlp, block_out))
        hidden_grad, mix_send, mix_keep = backward(mlp_out)
        block_shape = (2, 2, 2) + mix_half[1:]
        mix = ring.to_core(mix_keep.reshape(block_shape), mix_send.reshape(block_shape))
        mix_out = ring.leaving_first(mix)
        mlp = after(ring.first_step(mlp, mlp_out), mix_out)
        mlp_out = ring.leaving_second(mlp)
        mix = after(ring.first_step(mix, mix_out), *mlp_out)
        mix_out = ring.leaving_second(mix)
        mlp = after(ring.second_step(mlp, mlp_out), *mix_out)
        inner, rims, to_west, to_east = adjoint_of(hidden_grad, mlp)
        from_east = lax.ppermute(to_west, "lon", place.west)
        from_west = lax.ppermute(to_east, "lon", place.east)
        mix = after(ring.second_step(mix, mix_out), to_west)
        mlp_piece = after(ring.far_step(mlp, grad_scale), mix)
        mix_piece = ring.far_step(mix, grad_scale)
        from_east, from_west, _ = lax.optimization_barrier((from_east, from_west, mlp_piece))
        mlp_halves = ring.gather(mlp_piece)
        mix_halves = ring.gather(mix_piece)
        mlp_halves = [half.reshape(mlp_half) for half in mlp_halves]
        mix_halves = [half.reshape(mix_half) for half in mix_halves]
        down_out = jnp.concatenate([half[:half_units] for half in mlp_halves])
        up_out = jnp.concatenate([half[half_units:] for half in mlp_halves], axis=1)
        mix_out = jnp.stack([half.swapaxes(0, 1) for half in mix_halves], axis=1)
        mix_out = mix_out.reshape(mix_weight.shape)
    else:
        block_out = block_of()
        hidden_grad, mix_send, mix_keep = backward(mlp_send)
        inner, rims, to_west, to_east = adjoint_of(hidden_grad)
        from_east = lax.ppermute(to_west, "lon", place.west)
        from_west = lax.ppermute(to_east, "lon", place.east)

        def whole(keep, send):
            keep, send = keep.astype(full)[None], send.astype(full)[None]
            both = jnp.where(core == 0, jnp.concatenate([keep, send]), jnp.concatenate([send, keep]))
            return lax.psum(both, AXES) * grad_scale

        mlp_sum = whole(mlp_keep, mlp_send).astype(low)
        mix_sum = whole(mix_keep, mix_send).astype(low)
        down_out = mlp_sum[:, :half_units].reshape(down_weight.shape)
        up_out = jnp.concatenate([mlp_sum[0, half_units:], mlp_sum[1, half_units:]], axis=1)
        mix_out = mix_sum.transpose(2, 0, 1, 3, 4).reshape(mix_weight.shape)

    corner_east = jnp.stack([from_east[0], from_east[lat_rows + 1]]).astype(full)
    corner_west = jnp.stack([from_west[0], from_west[lat_rows + 1]]).astype(full)
    rims = rims.at[:, lon_cols - reach :].add(corner_east)
    rims = rims.at[:, :reach].add(corner_west).astype(low)
    near = lax.ppermute(jnp.where(place.even, rims[1], rims[0]), AXES, place.pairs)
    far = lax.ppermute(jnp.where(place.even, rims[0], rims[1]), AXES, place.bridges)
    middle = lon_cols - 2 * reach
    beyond = jnp.stack(
        [jnp.where(place.even, far, near), jnp.where(place.even, near, far)]
    ).astype(full)
    sides = jnp.concatenate(
        [
            from_west[1 : lat_rows + 1].astype(full),
            jnp.zeros((lat_rows, middle, channels), full),
            from_east[1 : lat_rows + 1].astype(full),
        ],
        axis=1,
    )
    nothing = jnp.zeros((lat_rows - 2, lon_cols, channels), full)
    ends = jnp.concatenate([beyond[:1], nothing, beyond[1:]])
    grad_field = (inner.astype(full) + sides + ends).astype(low)
    return (block_out.reshape(field_in.shape), grad_field, mix_out, up_out, down_out)


def solution(mesh):
    placed = (
        P("lat", "lon", None),
        P(None, "lat", None, None),
        P("lat"),
        P(),
        P(),
        P(),
        P("lat", "lon", None),
    )
    return jax.shard_map(
        local,
        mesh=mesh,
        in_specs=placed,
        out_specs=(P("lat", "lon", None), P("lat", "lon", None), P(), P(), P()),
        check_vma=False,
    )
```

```python
import functools
import math

import jax
import jax.numpy as jnp
from jax import lax
from jax.experimental import pallas as pl
from jax.experimental.pallas import tpu as pltpu
from jax.sharding import PartitionSpec as P

inv_root_two = 0.7071067811865476
inv_root_tau = 0.3989422804014327
AXES = ("lat", "lon")


class Place:
    def __init__(self):
        self.lats = lax.axis_size("lat")
        self.lons = lax.axis_size("lon")
        self.count = self.lats * self.lons
        self.lat = lax.axis_index("lat")
        self.lon = lax.axis_index("lon")
        self.flat = self.lat * self.lons + self.lon
        lats, lons = self.lats, self.lons
        self.east = [(i, (i + 1) % lons) for i in range(lons)]
        self.west = [(j, i) for i, j in self.east]
        self.pairs = [
            (r * lons + c, (r ^ 1) * lons + c) for r in range(lats) for c in range(lons)
        ]
        self.bridges = []
        for r in range(lats):
            other = r - 1 if r % 2 == 0 else r + 1
            for c in range(lons):
                if 0 <= other < lats:
                    self.bridges.append((r * lons + c, other * lons + c))
                else:
                    self.bridges.append((r * lons + c, r * lons + (c + lons // 2) % lons))
        self.even = self.lat % 2 == 0


def route(place, mask_of):
    return [(i, i ^ mask_of(i)) for i in range(place.count)]


def send_along(place, block, mask_of):
    return lax.ppermute(block, AXES, route(place, mask_of))


def first_mask(i):
    return 2 if i % 2 == 0 else 4


def second_mask(i):
    return 4 if i % 2 == 0 else 2


def after(value, *others):
    return lax.optimization_barrier((value, *others))[0]


def pick(array, index):
    return lax.dynamic_index_in_dim(array, index, 0, keepdims=False)


def joined(bit, own, other):
    return jnp.concatenate([jnp.where(bit == 0, own, other), jnp.where(bit == 0, other, own)])


class Ring:
    def __init__(self, place):
        self.place = place
        self.core = place.flat % 2
        side_y, side_x = (place.flat // 2) % 2, (place.flat // 4) % 2
        self.first = jnp.where(self.core == 0, side_y, side_x)
        self.second = jnp.where(self.core == 0, side_x, side_y)
        self.near = (place.flat // 8) % 2

    def total(self, parts, *places):
        picked = []
        for part in parts:
            for place in places:
                part = pick(part, place)
            picked.append(part.astype(jnp.float32))
        return sum(picked[1:], picked[0]).astype(jnp.bfloat16)

    def to_core(self, keep, send, *ties):
        return [keep, after(send_along(self.place, send, lambda i: 1), *ties)]

    def leaving_first(self, parts):
        return self.total(parts, 1 - self.first)

    def first_step(self, parts, out, *ties):
        got = after(send_along(self.place, out, first_mask), *ties)
        return [pick(part, self.first) for part in parts] + [got]

    def leaving_second(self, parts):
        second, near = self.second, self.near
        return [
            self.total(parts, *places)
            for places in ((1 - second, near), (second, 1 - near), (1 - second, 1 - near))
        ]

    def masks(self):
        return second_mask, lambda i: 8, lambda i: 8 + second_mask(i)

    def over_masks(self, outs, ties):
        got = [send_along(self.place, out, mask_of) for out, mask_of in zip(outs, self.masks())]
        return lax.optimization_barrier((*got, *ties))[:3]

    def second_step(self, parts, outs, *ties):
        parts = [pick(pick(part, self.second), self.near) for part in parts]
        return self.total(parts + list(self.over_masks(outs, ties)))

    def far_step(self, own, scale, *ties):
        far = after(send_along(self.place, own, lambda i: 16), *ties)
        return ((own.astype(jnp.float32) + far.astype(jnp.float32)) * scale).astype(own.dtype)

    def gather_second(self, piece, *ties):
        piece = piece[None]
        over_second, over_near, over_both = self.over_masks([piece] * 3, ties)
        return joined(
            self.second,
            joined(self.near, piece, over_near),
            joined(self.near, over_second, over_both),
        )

    def gather_first(self, buf, *ties):
        return joined(self.first, buf, after(send_along(self.place, buf, first_mask), *ties))

    def gather_core(self, buf, *ties):
        return after(send_along(self.place, buf, lambda i: 1), *ties)


def halves(core, own, other, axis):
    shape = own.shape[:axis] + (2,) + own.shape[axis:]
    out = jnp.zeros(shape, own.dtype)
    out = lax.dynamic_update_index_in_dim(out, own, core, axis)
    return lax.dynamic_update_index_in_dim(out, other, 1 - core, axis)


OVER_ROWS = (((0,), (0,)), ((), ()))
OVER_LANES = (((1,), (1,)), ((), ()))
VMEM_LIMIT = 56 * 1024 * 1024


def dot(left, right, dims=(((1,), (0,)), ((), ()))):
    return lax.dot_general(left, right, dims, preferred_element_type=jnp.float32)


def tiles(count, size, body):
    def step(i, carry):
        body(pl.ds(pl.multiple_of(i * size, size), size))
        return carry

    lax.fori_loop(0, count // size, step, 0)


def band_kernel(reach_ref, taps, bands, lines, *, cols):
    basis, rows, _, count = taps.shape
    width = lines.shape[2]
    away = jnp.abs(lax.broadcasted_iota(jnp.int32, (3, count), 1) - (count - 1) // 2)
    lines[...] = jnp.zeros(lines.shape, lines.dtype)

    def one_row(r, carry):
        inside = away <= reach_ref[r]
        for k in range(basis):
            lines[k, :, :count] = jnp.where(inside, taps[k, r].astype(jnp.float32), 0.0)
            for d in range(3):
                line = jnp.broadcast_to(lines[k, pl.ds(d, 1)], (cols, width))
                band = pltpu.roll(line, 0, 1, stride=1, stride_axis=0)
                bands[r, k * cols : (k + 1) * cols, d * width : (d + 1) * width] = band.astype(
                    bands.dtype
                )
        return carry

    lax.fori_loop(0, rows, one_row, 0)


def started(pairs, sems, first=0):
    copies = [pltpu.make_async_copy(a, b, sems.at[first + i]) for i, (a, b) in enumerate(pairs)]
    for copy in copies:
        copy.start()
    return copies


def finish(copies):
    for copy in copies:
        copy.wait()


def forward_kernel(
    core_ref, field, north, south, west, east, corners_west, corners_east, bands_in, mix_in,
    up_in, down_in, cot_in,
    feats_out, hidden_out, act_out, pre_out, send_out, keep_out,
    ext, bands, mix, up, down, cot, feats, hidden, act, pre_grad, turned, pre_a, pre_b, ag_a,
    ag_b, send, keep, sems
):
    core = core_ref[0]
    rows, cols, channels = field.shape
    reach = west.shape[1]
    basis = mix.shape[0]
    points = rows * cols
    half_units = up.shape[1] // 2
    body, inner = pl.ds(1, rows), pl.ds(reach, cols)
    begin, end = pl.ds(0, reach), pl.ds(reach + cols, reach)
    loads = started(
        [
            (field, ext.at[body, inner]),
            (west, ext.at[body, begin]),
            (east, ext.at[body, end]),
            (north, ext.at[0, inner]),
            (south, ext.at[rows + 1, inner]),
            (corners_west.at[0], ext.at[0, begin]),
            (corners_west.at[1], ext.at[rows + 1, begin]),
            (corners_east.at[0], ext.at[0, end]),
            (corners_east.at[1], ext.at[rows + 1, end]),
        ],
        sems,
    )
    band_loads = started([(bands_in.at[r], bands.at[r]) for r in range(rows)], sems, 9)
    late = 9 + rows
    weights = started([(mix_in, mix), (up_in, up), (down_in, down), (cot_in, cot)], sems, late)
    finish(loads)

    for r in range(rows):
        finish(band_loads[r : r + 1])
        window = ext[r : r + 3].reshape(3 * ext.shape[1], channels)
        out = dot(bands[r], window).astype(feats.dtype)
        at = pl.ds(r * cols, cols)
        for k in range(basis):
            feats[k, at, :] = out[k * cols : (k + 1) * cols]
        hidden[at, :] = ext[r + 1, inner, :]
    stores = started([(feats, feats_out)], sems, late + 4)
    finish(weights[:1])

    for i in range(3):
        at = pl.ds(i * (points // 3), points // 3)
        total = hidden[at, :].astype(jnp.float32)
        for k in range(basis):
            total = total + dot(feats[k, at, :], mix[k])
        hidden[at, :] = total.astype(hidden.dtype)
    finish(weights[1:])
    stores += started([(hidden, hidden_out)], sems, late + 5)
    size = pre_a.shape[0]
    slots = ((pre_a, ag_a), (pre_b, ag_b))

    def products(i):
        at = pl.ds(i * size, size)
        pre, ag = slots[i % 2]
        pre[...] = dot(hidden[at, :], up[...])
        ag[...] = dot(cot[at, :], down[...], OVER_LANES)

    def activation(i):
        at = pl.ds(i * size, size)
        pre, ag = slots[i % 2]
        value = pre[...]
        phi = 0.5 * (1.0 + lax.erf(value * inv_root_two))
        act[at, :] = (value * phi).astype(act.dtype)
        slope = phi + value * jnp.exp(-0.5 * value * value) * inv_root_tau
        pre_grad[at, :] = (ag[...] * slope).astype(pre_grad.dtype)

    products(0)
    for i in range(points // size):
        if (i + 1) * size < points:
            products(i + 1)
        activation(i)
    stores += started([(act, act_out), (pre_grad, pre_out)], sems, late + 6)
    turned[...] = hidden[...].T

    def sums(half, out):
        at = pl.ds(pl.multiple_of(half * half_units, half_units), half_units)
        out[:half_units] = dot(act[:, at], cot[...], OVER_ROWS).astype(out.dtype)
        out[half_units:] = dot(turned[...], pre_grad[:, at]).astype(out.dtype)

    sums(1 - core, send)
    stores += started([(send, send_out)], sems, late + 8)
    sums(core, keep)
    stores += started([(keep, keep_out)], sems, late + 9)
    finish(stores)


def backward_kernel(
    core_ref, pre_in, up_in, cot_in, feats_in, hg_out, send_out, keep_out,
    pre_grad, up, cot, feats, hg, send, keep, sems
):
    core = core_ref[0]
    basis, points, channels = feats.shape
    half_channels = channels // 2
    parts = [pl.ds(i * (points // 3), points // 3) for i in range(3)]
    weights = started([(up_in, up)], sems)
    loads = started([(pre_in.at[at], pre_grad.at[at]) for at in parts], sems, 1)
    cot_loads = started([(cot_in.at[at], cot.at[at]) for at in parts], sems, 4)
    feat_loads = started([(feats_in.at[k], feats.at[k]) for k in range(basis)], sems, 7)
    late = 7 + basis
    finish(weights)
    for i, at in enumerate(parts):
        finish([loads[i], cot_loads[i]])
        total = cot[at, :].astype(jnp.float32) + dot(pre_grad[at, :], up[...], OVER_LANES)
        hg[at, :] = total.astype(hg.dtype)
    stores = started([(hg, hg_out)], sems, late)
    finish(feat_loads)

    def sums(half, out):
        at = pl.ds(pl.multiple_of(half * half_channels, half_channels), half_channels)
        for k in range(basis):
            part = dot(feats[k, :, at], hg[...], OVER_ROWS).astype(out.dtype)
            out[:, k] = part.reshape(out.shape[0], -1, channels)

    sums(1 - core, send)
    stores += started([(send, send_out)], sems, late + 1)
    sums(core, keep)
    stores += started([(keep, keep_out)], sems, late + 2)
    finish(stores)


def adjoint_kernel(
    hg_in, grads_in, bands_in, inner_out, rim_out, west_out, east_out,
    hg, bands, grads, pulled, inner, sems, *, cols
):
    basis = grads_in.shape[0]
    rows, width, channels = pulled.shape[0] - 2, pulled.shape[1], pulled.shape[2]
    reach = (width - cols) // 2
    loads = []
    for r in range(rows):
        copies = [(bands_in.at[r], bands.at[r])]
        for k in range(basis):
            at = pl.ds(r * cols, cols)
            copies.append((grads_in.at[k, at], grads.at[r, pl.ds(k * cols, cols)]))
        loads.append(started(copies, sems, r * (1 + basis)))
    late = rows * (1 + basis)
    own_load = started([(hg_in, hg)], sems, late)
    pulled[...] = jnp.zeros(pulled.shape, pulled.dtype)
    stores = []

    def give(row):
        own = hg[(row - 1) * cols : row * cols, :].astype(jnp.float32)
        inner[row - 1] = (pulled[row, reach : reach + cols] + own).astype(inner.dtype)
        copies = [(inner.at[row - 1], inner_out.at[row - 1])]
        stores.extend(started(copies, sems, late + row))

    for r in range(rows):
        finish(loads[r])
        part = dot(bands[r], grads[r], OVER_ROWS)
        pulled[r : r + 3] += part.reshape(3, width, channels)
        if r == 0:
            finish(own_load)
        else:
            give(r)
    give(rows)
    west_out[...] = pulled[:, :reach].astype(west_out.dtype)
    east_out[...] = pulled[:, reach + cols :].astype(east_out.dtype)
    for n, r in enumerate((0, rows + 1)):
        rim_out[n] = pulled[r, reach : reach + cols]
    finish(stores)


def call(kernel, operands, kinds, shapes, out_kinds, scratch, flops, nbytes):
    return pl.pallas_call(
        kernel,
        out_shape=[jax.ShapeDtypeStruct(shape, kind) for shape, kind in shapes],
        in_specs=[pl.BlockSpec(memory_space=kind) for kind in kinds],
        out_specs=[pl.BlockSpec(memory_space=kind) for kind in out_kinds],
        scratch_shapes=scratch,
        compiler_params=pltpu.CompilerParams(vmem_limit_bytes=VMEM_LIMIT),
        cost_estimate=pl.CostEstimate(flops=flops, bytes_accessed=nbytes, transcendentals=0),
    )(*operands)


def local(field_in, kernel_taps, row_reach, mix_weight, up_weight, down_weight, cotangent):
    lat_rows, lon_cols, channels = field_in.shape
    basis_count = kernel_taps.shape[0]
    tap_count = kernel_taps.shape[3]
    reach = (tap_count - 1) // 2
    hidden_units = up_weight.shape[1]
    place = Place()

    top, bottom = field_in[0], field_in[lat_rows - 1]
    inner = lax.ppermute(jnp.where(place.even, bottom, top), AXES, place.pairs)
    outer = lax.ppermute(jnp.where(place.even, top, bottom), AXES, place.bridges)
    west = lax.ppermute(field_in[:, lon_cols - reach :], "lon", place.east)
    east = lax.ppermute(field_in[:, :reach], "lon", place.west)
    north = jnp.where(place.even, outer, inner)
    south = jnp.where(place.even, inner, outer)
    corners = jnp.stack([north[lon_cols - reach :], south[lon_cols - reach :]])
    corners_west = lax.ppermute(corners, "lon", place.east)
    corners = jnp.stack([north[:reach], south[:reach]])
    corners_east = lax.ppermute(corners, "lon", place.west)

    low, full = jnp.bfloat16, jnp.float32
    points = lat_rows * lon_cols
    width = lon_cols + 2 * reach
    vmem, anywhere, smem = pltpu.VMEM, pl.ANY, pltpu.SMEM
    cot = cotangent.reshape(points, channels)
    band_shape = (lat_rows, basis_count * lon_cols, 3 * width)
    gemm = 2 * points * channels * hidden_units
    mix_gemm = 2 * points * channels * channels * basis_count
    band_gemm = 2 * lat_rows * basis_count * lon_cols * 3 * width * channels
    (bands,) = call(
        functools.partial(band_kernel, cols=lon_cols),
        (row_reach, kernel_taps),
        [smem, vmem],
        [(band_shape, low)],
        [vmem],
        [pltpu.VMEM((basis_count, 3, width), full)],
        0,
        2 * points * hidden_units * 4,
    )

    half_units, half_channels = hidden_units // 2, channels // 2
    mlp_half = (half_units + channels, channels)
    mix_half = (8, basis_count, half_channels // 8, channels)
    big, wide, many = (points, channels), (points, hidden_units), (basis_count, points, channels)
    core = place.flat % 2
    core_op = core[None].astype(jnp.int32)
    sized = (points // 5, hidden_units)
    feats, hidden, activated, pre_grad, mlp_send, mlp_keep = call(
        forward_kernel,
        (
            core_op, field_in, north, south, west, east, corners_west, corners_east, bands,
            mix_weight, up_weight, down_weight, cot,
        ),
        [smem] + [anywhere] * 12,
        [(many, low), (big, low), (wide, low), (wide, low), (mlp_half, low), (mlp_half, low)],
        [anywhere] * 6,
        [
            pltpu.VMEM((lat_rows + 2, width, channels), low),
            pltpu.VMEM(band_shape, low),
            pltpu.VMEM(mix_weight.shape, low),
            pltpu.VMEM(up_weight.shape, low),
            pltpu.VMEM(down_weight.shape, low),
            pltpu.VMEM(big, low),
            pltpu.VMEM(many, low),
            pltpu.VMEM(big, low),
            pltpu.VMEM(wide, low),
            pltpu.VMEM(wide, low),
            pltpu.VMEM((channels, points), low),
            pltpu.VMEM(sized, full),
            pltpu.VMEM(sized, full),
            pltpu.VMEM(sized, full),
            pltpu.VMEM(sized, full),
            pltpu.VMEM(mlp_half, low),
            pltpu.VMEM(mlp_half, low),
            pltpu.SemaphoreType.DMA((19 + lat_rows,)),
        ],
        band_gemm + mix_gemm + 4 * gemm,
        4 * points * hidden_units * 4,
    )
    def backward(start):
        return call(
            backward_kernel,
            (core_op, after(pre_grad, start), up_weight, cot, feats),
            [smem] + [anywhere] * 4,
            [(big, low), (mix_half, low), (mix_half, low)],
            [anywhere] * 3,
            [
                pltpu.VMEM(wide, low),
                pltpu.VMEM(up_weight.shape, low),
                pltpu.VMEM(big, low),
                pltpu.VMEM(many, low),
                pltpu.VMEM(big, low),
                pltpu.VMEM(mix_half, low),
                pltpu.VMEM(mix_half, low),
                pltpu.SemaphoreType.DMA((10 + basis_count,)),
            ],
            mix_gemm + gemm,
            3 * points * hidden_units * 4,
        )

    def block_of():
        total = hidden.astype(full) + dot(activated, down_weight)
        return total.astype(low)

    def feature_grads(hidden_grad):
        grads = jnp.einsum("pd,kcd->kpc", hidden_grad, mix_weight, preferred_element_type=full)
        return grads.astype(low)

    def adjoint_of(hidden_grad, feat_grads, start):
        side = (lat_rows + 2, reach, channels)
        return call(
            functools.partial(adjoint_kernel, cols=lon_cols),
            (hidden_grad, after(feat_grads, start), bands),
            [anywhere] * 3,
            [
                (field_in.shape, low), ((2, lon_cols, channels), full), (side, low), (side, low),
            ],
            [anywhere] + [vmem] * 3,
            [
                pltpu.VMEM(big, low),
                pltpu.VMEM(band_shape, low),
                pltpu.VMEM((lat_rows, basis_count * lon_cols, channels), low),
                pltpu.VMEM((lat_rows + 2, width, channels), full),
                pltpu.VMEM(field_in.shape, low),
                pltpu.SemaphoreType.DMA((1 + lat_rows * (2 + basis_count),)),
            ],
            band_gemm,
            3 * points * hidden_units * 4,
        )

    grad_scale = 1.0 / math.sqrt(points * place.count)
    if place.count == 32:
        ring = Ring(place)
        block_shape = (2, 2, 2, mlp_half[0] // 8, channels)
        mlp = ring.to_core(mlp_keep.reshape(block_shape), mlp_send.reshape(block_shape))
        mlp[1], block_out = lax.optimization_barrier((mlp[1], block_of()))
        mlp_out = ring.leaving_first(mlp)
        hidden_grad, mix_send, mix_keep = backward(mlp_out)
        mlp = ring.first_step(mlp, mlp_out)
        mlp_out = ring.leaving_second(mlp)
        hidden_grad = after(hidden_grad, *mlp_out)
        feat_grads = feature_grads(hidden_grad)
        block_shape = (2, 2, 2) + mix_half[1:]
        mix = ring.to_core(
            mix_keep.reshape(block_shape), mix_send.reshape(block_shape), feat_grads, *mlp_out
        )
        mix_out = ring.leaving_first(mix)
        mlp = ring.second_step(mlp, mlp_out, mix_out)
        mix = ring.first_step(mix, mix_out, mlp)
        mix_out = ring.leaving_second(mix)
        inner, rims, to_west, to_east = adjoint_of(hidden_grad, feat_grads, mix_out[0])
        from_east = lax.ppermute(to_west, "lon", place.west)
        from_west = lax.ppermute(to_east, "lon", place.east)
        mix = ring.second_step(mix, mix_out, to_west)
        mlp = ring.far_step(mlp, grad_scale, mix)
        mix = ring.far_step(mix, grad_scale, mlp)
        mlp = ring.gather_second(mlp, mix)
        from_east, from_west, _ = lax.optimization_barrier((from_east, from_west, mlp))
        mix = ring.gather_second(mix, mlp)
        mlp = ring.gather_first(mlp, mix)
        mlp_other = ring.gather_core(mlp)
        mix = ring.gather_first(mix, mlp)
        mix_other = ring.gather_core(mix)

        def split(buf):
            flat = buf.reshape(mlp_half)
            return flat[:half_units], flat[half_units:]

        def by_basis(buf):
            return buf.reshape(mix_half).swapaxes(0, 1)

        (own_down, own_up), (other_down, other_up) = split(mlp), split(mlp_other)
        down_out = halves(core, own_down, other_down, 0).reshape(down_weight.shape)
        low_side = jnp.zeros(up_weight.shape, low)
        low_side = lax.dynamic_update_slice_in_dim(low_side, own_up, core * half_units, 1)
        up_out = lax.dynamic_update_slice_in_dim(
            low_side, other_up, (1 - core) * half_units, 1
        )
        mix_out = halves(core, by_basis(mix), by_basis(mix_other), 1)
        mix_out = mix_out.reshape(mix_weight.shape)
    else:
        block_out = block_of()
        hidden_grad, mix_send, mix_keep = backward(mlp_send)
        inner, rims, to_west, to_east = adjoint_of(
            hidden_grad, feature_grads(hidden_grad), mix_send
        )
        from_east = lax.ppermute(to_west, "lon", place.west)
        from_west = lax.ppermute(to_east, "lon", place.east)

        def whole(keep, send):
            keep, send = keep.astype(full)[None], send.astype(full)[None]
            both = jnp.where(core == 0, jnp.concatenate([keep, send]), jnp.concatenate([send, keep]))
            return lax.psum(both, AXES) * grad_scale

        mlp_sum = whole(mlp_keep, mlp_send).astype(low)
        mix_sum = whole(mix_keep, mix_send).astype(low)
        down_out = mlp_sum[:, :half_units].reshape(down_weight.shape)
        up_out = jnp.concatenate([mlp_sum[0, half_units:], mlp_sum[1, half_units:]], axis=1)
        mix_out = mix_sum.transpose(2, 0, 1, 3, 4).reshape(mix_weight.shape)

    corner_east = jnp.stack([from_east[0], from_east[lat_rows + 1]]).astype(full)
    corner_west = jnp.stack([from_west[0], from_west[lat_rows + 1]]).astype(full)
    rims = rims.at[:, lon_cols - reach :].add(corner_east)
    rims = rims.at[:, :reach].add(corner_west).astype(low)
    near = lax.ppermute(jnp.where(place.even, rims[1], rims[0]), AXES, place.pairs)
    far = lax.ppermute(jnp.where(place.even, rims[0], rims[1]), AXES, place.bridges)
    middle = lon_cols - 2 * reach
    beyond = jnp.stack(
        [jnp.where(place.even, far, near), jnp.where(place.even, near, far)]
    ).astype(full)
    sides = jnp.concatenate(
        [
            from_west[1 : lat_rows + 1].astype(full),
            jnp.zeros((lat_rows, middle, channels), full),
            from_east[1 : lat_rows + 1].astype(full),
        ],
        axis=1,
    )
    nothing = jnp.zeros((lat_rows - 2, lon_cols, channels), full)
    ends = jnp.concatenate([beyond[:1], nothing, beyond[1:]])
    grad_field = (inner.astype(full) + sides + ends).astype(low)
    return (block_out.reshape(field_in.shape), grad_field, mix_out, up_out, down_out)


def solution(mesh):
    placed = (
        P("lat", "lon", None),
        P(None, "lat", None, None),
        P("lat"),
        P(),
        P(),
        P(),
        P("lat", "lon", None),
    )
    return jax.shard_map(
        local,
        mesh=mesh,
        in_specs=placed,
        out_specs=(P("lat", "lon", None), P("lat", "lon", None), P(), P(), P()),
        check_vma=False,
    )
```

```python
import functools
import math

import jax
import jax.numpy as jnp
from jax import lax
from jax.experimental import pallas as pl
from jax.experimental.pallas import tpu as pltpu
from jax.sharding import PartitionSpec as P

inv_root_two = 0.7071067811865476
inv_root_tau = 0.3989422804014327
AXES = ("lat", "lon")


class Place:
    def __init__(self):
        self.lats = lax.axis_size("lat")
        self.lons = lax.axis_size("lon")
        self.count = self.lats * self.lons
        self.lat = lax.axis_index("lat")
        self.lon = lax.axis_index("lon")
        self.flat = self.lat * self.lons + self.lon
        lats, lons = self.lats, self.lons
        self.east = [(i, (i + 1) % lons) for i in range(lons)]
        self.west = [(j, i) for i, j in self.east]
        self.pairs = [
            (r * lons + c, (r ^ 1) * lons + c) for r in range(lats) for c in range(lons)
        ]
        self.bridges = []
        for r in range(lats):
            other = r - 1 if r % 2 == 0 else r + 1
            for c in range(lons):
                if 0 <= other < lats:
                    self.bridges.append((r * lons + c, other * lons + c))
                else:
                    self.bridges.append((r * lons + c, r * lons + (c + lons // 2) % lons))
        self.even = self.lat % 2 == 0


def route(place, mask_of):
    return [(i, i ^ mask_of(i)) for i in range(place.count)]


def send_along(place, block, mask_of):
    return lax.ppermute(block, AXES, route(place, mask_of))


def first_mask(i):
    return 2 if i % 2 == 0 else 4


def second_mask(i):
    return 4 if i % 2 == 0 else 2


def after(value, *others):
    return lax.optimization_barrier((value, *others))[0] if others else value


def pick(array, index):
    return lax.dynamic_index_in_dim(array, index, 0, keepdims=False)


def joined(bit, own, other):
    return jnp.concatenate([jnp.where(bit == 0, own, other), jnp.where(bit == 0, other, own)])


class Ring:
    def __init__(self, place):
        self.place = place
        self.core = place.flat % 2
        side_y, side_x = (place.flat // 2) % 2, (place.flat // 4) % 2
        self.first = jnp.where(self.core == 0, side_y, side_x)
        self.second = jnp.where(self.core == 0, side_x, side_y)
        self.near = (place.flat // 8) % 2

    def to_core(self, keep, send):
        got = send_along(self.place, send, lambda i: 1)
        return keep.astype(jnp.float32) + got.astype(jnp.float32)

    def leaving_first(self, buf):
        return pick(buf, 1 - self.first).astype(jnp.bfloat16)

    def first_step(self, buf, out):
        got = send_along(self.place, out, first_mask)
        return pick(buf, self.first) + got.astype(jnp.float32)

    def block(self, buf, over_second, over_near):
        at_second = 1 - self.second if over_second else self.second
        at_near = 1 - self.near if over_near else self.near
        return pick(pick(buf, at_second), at_near)

    def leaving_second(self, buf):
        return [
            self.block(buf, *over).astype(jnp.bfloat16)
            for over in ((True, False), (False, True), (True, True))
        ]

    def masks(self):
        return second_mask, lambda i: 8, lambda i: 8 + second_mask(i)

    def second_step(self, buf, outs):
        total = self.block(buf, False, False)
        for out, mask_of in zip(outs, self.masks()):
            total = total + send_along(self.place, out, mask_of).astype(jnp.float32)
        return total.astype(jnp.bfloat16)

    def far_step(self, own, scale):
        far = send_along(self.place, own, lambda i: 16)
        return ((own.astype(jnp.float32) + far.astype(jnp.float32)) * scale).astype(own.dtype)

    def gather_near(self, piece, *ties):
        piece = piece[None]
        return joined(self.near, piece, after(send_along(self.place, piece, lambda i: 8), *ties))

    def gather_second(self, buf, *ties):
        return joined(self.second, buf, after(send_along(self.place, buf, second_mask), *ties))

    def gather_first(self, buf, *ties):
        return joined(self.first, buf, after(send_along(self.place, buf, first_mask), *ties))

    def gather_core(self, buf, *ties):
        return after(send_along(self.place, buf, lambda i: 1), *ties)


def halves(core, own, other, axis):
    size = own.shape[axis]
    shape = own.shape[:axis] + (2 * size,) + own.shape[axis + 1 :]
    out = jnp.zeros(shape, own.dtype)
    out = lax.dynamic_update_slice_in_dim(out, own, core * size, axis)
    return lax.dynamic_update_slice_in_dim(out, other, (1 - core) * size, axis)


OVER_ROWS = (((0,), (0,)), ((), ()))
OVER_LANES = (((1,), (1,)), ((), ()))
VMEM_LIMIT = 56 * 1024 * 1024


def dot(left, right, dims=(((1,), (0,)), ((), ()))):
    return lax.dot_general(left, right, dims, preferred_element_type=jnp.float32)


def tiles(count, size, body):
    def step(i, carry):
        body(pl.ds(pl.multiple_of(i * size, size), size))
        return carry

    lax.fori_loop(0, count // size, step, 0)


def band_kernel(reach_ref, taps, bands, lines, *, cols):
    basis, rows, _, count = taps.shape
    width = lines.shape[2]
    away = jnp.abs(lax.broadcasted_iota(jnp.int32, (3, count), 1) - (count - 1) // 2)
    lines[...] = jnp.zeros(lines.shape, lines.dtype)

    def one_row(r, carry):
        inside = away <= reach_ref[r]
        for k in range(basis):
            lines[k, :, :count] = jnp.where(inside, taps[k, r].astype(jnp.float32), 0.0)
            for d in range(3):
                line = jnp.broadcast_to(lines[k, pl.ds(d, 1)], (cols, width))
                band = pltpu.roll(line, 0, 1, stride=1, stride_axis=0)
                bands[r, k * cols : (k + 1) * cols, d * width : (d + 1) * width] = band.astype(
                    bands.dtype
                )
        return carry

    lax.fori_loop(0, rows, one_row, 0)


def started(pairs, sems, first=0):
    copies = [pltpu.make_async_copy(a, b, sems.at[first + i]) for i, (a, b) in enumerate(pairs)]
    for copy in copies:
        copy.start()
    return copies


def finish(copies):
    for copy in copies:
        copy.wait()


def forward_kernel(
    core_ref, field, north, south, west, east, corners_west, corners_east, bands_in, mix_in,
    up_in, down_in, cot_in,
    feats_out, hidden_out, act_out, pre_out, send_out, keep_out,
    ext, bands, mix, up, down, cot, feats, hidden, act, pre_grad, turned, pre_a, pre_b, ag_a,
    ag_b, send, keep, sems
):
    core = core_ref[0]
    rows, cols, channels = field.shape
    reach = west.shape[1]
    basis = mix.shape[0]
    points = rows * cols
    half_units = up.shape[1] // 2
    body, inner = pl.ds(1, rows), pl.ds(reach, cols)
    begin, end = pl.ds(0, reach), pl.ds(reach + cols, reach)
    loads = started(
        [
            (field, ext.at[body, inner]),
            (west, ext.at[body, begin]),
            (east, ext.at[body, end]),
            (north, ext.at[0, inner]),
            (south, ext.at[rows + 1, inner]),
            (corners_west.at[0], ext.at[0, begin]),
            (corners_west.at[1], ext.at[rows + 1, begin]),
            (corners_east.at[0], ext.at[0, end]),
            (corners_east.at[1], ext.at[rows + 1, end]),
        ],
        sems,
    )
    band_loads = started([(bands_in.at[r], bands.at[r]) for r in range(rows)], sems, 9)
    late = 9 + rows
    weights = started([(mix_in, mix), (up_in, up), (down_in, down), (cot_in, cot)], sems, late)
    finish(loads)

    for r in range(rows):
        finish(band_loads[r : r + 1])
        window = ext[r : r + 3].reshape(3 * ext.shape[1], channels)
        out = dot(bands[r], window).astype(feats.dtype)
        at = pl.ds(r * cols, cols)
        for k in range(basis):
            feats[k, at, :] = out[k * cols : (k + 1) * cols]
        hidden[at, :] = ext[r + 1, inner, :]
    stores = started([(feats, feats_out)], sems, late + 4)
    finish(weights[:1])

    for i in range(3):
        at = pl.ds(i * (points // 3), points // 3)
        total = hidden[at, :].astype(jnp.float32)
        for k in range(basis):
            total = total + dot(feats[k, at, :], mix[k])
        hidden[at, :] = total.astype(hidden.dtype)
    finish(weights[1:])
    stores += started([(hidden, hidden_out)], sems, late + 5)
    size = pre_a.shape[0]
    slots = ((pre_a, ag_a), (pre_b, ag_b))

    def products(i):
        at = pl.ds(i * size, size)
        pre, ag = slots[i % 2]
        pre[...] = dot(hidden[at, :], up[...])
        ag[...] = dot(cot[at, :], down[...], OVER_LANES)

    def activation(i):
        at = pl.ds(i * size, size)
        pre, ag = slots[i % 2]
        value = pre[...]
        phi = 0.5 * (1.0 + lax.erf(value * inv_root_two))
        act[at, :] = (value * phi).astype(act.dtype)
        slope = phi + value * jnp.exp(-0.5 * value * value) * inv_root_tau
        pre_grad[at, :] = (ag[...] * slope).astype(pre_grad.dtype)

    products(0)
    for i in range(points // size):
        if (i + 1) * size < points:
            products(i + 1)
        activation(i)
    stores += started([(act, act_out), (pre_grad, pre_out)], sems, late + 6)
    turned[...] = hidden[...].T

    def sums(half, out):
        at = pl.ds(pl.multiple_of(half * half_units, half_units), half_units)
        out[:half_units] = dot(act[:, at], cot[...], OVER_ROWS).astype(out.dtype)
        out[half_units:] = dot(turned[...], pre_grad[:, at]).astype(out.dtype)

    sums(1 - core, send)
    stores += started([(send, send_out)], sems, late + 8)
    sums(core, keep)
    stores += started([(keep, keep_out)], sems, late + 9)
    finish(stores)


def backward_kernel(
    core_ref, pre_in, up_in, cot_in, feats_in, hg_out, send_out, keep_out,
    pre_grad, up, cot, feats, hg, send, keep, sems
):
    core = core_ref[0]
    basis, points, channels = feats.shape
    half_channels = channels // 2
    parts = [pl.ds(i * (points // 3), points // 3) for i in range(3)]
    weights = started([(up_in, up)], sems)
    loads = started([(pre_in.at[at], pre_grad.at[at]) for at in parts], sems, 1)
    cot_loads = started([(cot_in.at[at], cot.at[at]) for at in parts], sems, 4)
    feat_loads = started([(feats_in.at[k], feats.at[k]) for k in range(basis)], sems, 7)
    late = 7 + basis
    finish(weights)
    for i, at in enumerate(parts):
        finish([loads[i], cot_loads[i]])
        total = cot[at, :].astype(jnp.float32) + dot(pre_grad[at, :], up[...], OVER_LANES)
        hg[at, :] = total.astype(hg.dtype)
    stores = started([(hg, hg_out)], sems, late)
    finish(feat_loads)

    def sums(half, out):
        at = pl.ds(pl.multiple_of(half * half_channels, half_channels), half_channels)
        for k in range(basis):
            out[k] = dot(feats[k, :, at], hg[...], OVER_ROWS).astype(out.dtype)

    sums(1 - core, send)
    stores += started([(send, send_out)], sems, late + 1)
    sums(core, keep)
    stores += started([(keep, keep_out)], sems, late + 2)
    finish(stores)


def out_kernel(hidden_in, act_in, down_in, block_out, hidden, act, down, block, sems):
    points = hidden.shape[0]
    parts = [pl.ds(i * (points // 3), points // 3) for i in range(3)]
    weights = started([(down_in, down)], sems)
    loads = started([(act_in.at[at], act.at[at]) for at in parts], sems, 1)
    more = started([(hidden_in.at[at], hidden.at[at]) for at in parts], sems, 4)
    finish(weights)
    stores = []
    for i, at in enumerate(parts):
        finish([loads[i], more[i]])
        total = hidden[at, :].astype(jnp.float32) + dot(act[at, :], down[...])
        block[at, :] = total.astype(block.dtype)
        stores += started([(block.at[at], block_out.at[at])], sems, 7 + i)
    finish(stores)


def adjoint_kernel(
    hg_in, mix_in, bands_in, inner_out, rim_out, west_out, east_out,
    hg, mix, bands, grads, pulled, inner, sems, *, cols
):
    basis, channels = mix.shape[0], mix.shape[1]
    rows, width = pulled.shape[0] - 2, pulled.shape[1]
    reach = (width - cols) // 2
    loads = started([(hg_in, hg)], sems)
    loads += started([(mix_in.at[k], mix.at[k]) for k in range(basis)], sems, 1)
    late = 1 + basis
    band_loads = started([(bands_in.at[r], bands.at[r]) for r in range(rows)], sems, late)
    pulled[...] = jnp.zeros(pulled.shape, pulled.dtype)
    group = 5 if rows % 5 == 0 else 1
    finish(loads[:1])
    for k in range(basis):
        finish(loads[1 + k : 2 + k])
        for r in range(0, rows, group):
            part = dot(hg[r * cols : (r + group) * cols, :], mix[k], OVER_LANES)
            grads[r : r + group, k * cols : (k + 1) * cols] = part.astype(grads.dtype).reshape(
                group, cols, channels
            )
    stores = []

    def give(row):
        own = hg[(row - 1) * cols : row * cols, :].astype(jnp.float32)
        inner[row - 1] = (pulled[row, reach : reach + cols] + own).astype(inner.dtype)
        copies = [(inner.at[row - 1], inner_out.at[row - 1])]
        stores.extend(started(copies, sems, late + rows + row - 1))

    for r in range(rows):
        finish(band_loads[r : r + 1])
        part = dot(bands[r], grads[r], OVER_ROWS)
        pulled[r : r + 3] += part.reshape(3, width, channels)
        if r:
            give(r)
    give(rows)
    west_out[...] = pulled[:, :reach].astype(west_out.dtype)
    east_out[...] = pulled[:, reach + cols :].astype(east_out.dtype)
    for n, r in enumerate((0, rows + 1)):
        rim_out[n] = pulled[r, reach : reach + cols]
    finish(stores)


def call(kernel, operands, kinds, shapes, out_kinds, scratch, flops, nbytes):
    return pl.pallas_call(
        kernel,
        out_shape=[jax.ShapeDtypeStruct(shape, kind) for shape, kind in shapes],
        in_specs=[pl.BlockSpec(memory_space=kind) for kind in kinds],
        out_specs=[pl.BlockSpec(memory_space=kind) for kind in out_kinds],
        scratch_shapes=scratch,
        compiler_params=pltpu.CompilerParams(vmem_limit_bytes=VMEM_LIMIT),
        cost_estimate=pl.CostEstimate(flops=flops, bytes_accessed=nbytes, transcendentals=0),
    )(*operands)


def local(field_in, kernel_taps, row_reach, mix_weight, up_weight, down_weight, cotangent):
    lat_rows, lon_cols, channels = field_in.shape
    basis_count = kernel_taps.shape[0]
    tap_count = kernel_taps.shape[3]
    reach = (tap_count - 1) // 2
    hidden_units = up_weight.shape[1]
    place = Place()

    top, bottom = field_in[0], field_in[lat_rows - 1]
    inner = lax.ppermute(jnp.where(place.even, bottom, top), AXES, place.pairs)
    outer = lax.ppermute(jnp.where(place.even, top, bottom), AXES, place.bridges)
    west = lax.ppermute(field_in[:, lon_cols - reach :], "lon", place.east)
    east = lax.ppermute(field_in[:, :reach], "lon", place.west)
    north = jnp.where(place.even, outer, inner)
    south = jnp.where(place.even, inner, outer)
    corners = jnp.stack([north[lon_cols - reach :], south[lon_cols - reach :]])
    corners_west = lax.ppermute(corners, "lon", place.east)
    corners = jnp.stack([north[:reach], south[:reach]])
    corners_east = lax.ppermute(corners, "lon", place.west)

    low, full = jnp.bfloat16, jnp.float32
    points = lat_rows * lon_cols
    width = lon_cols + 2 * reach
    vmem, anywhere, smem = pltpu.VMEM, pl.ANY, pltpu.SMEM
    cot = cotangent.reshape(points, channels)
    band_shape = (lat_rows, basis_count * lon_cols, 3 * width)
    gemm = 2 * points * channels * hidden_units
    mix_gemm = 2 * points * channels * channels * basis_count
    band_gemm = 2 * lat_rows * basis_count * lon_cols * 3 * width * channels
    (bands,) = call(
        functools.partial(band_kernel, cols=lon_cols),
        (row_reach, kernel_taps),
        [smem, vmem],
        [(band_shape, low)],
        [vmem],
        [pltpu.VMEM((basis_count, 3, width), full)],
        0,
        2 * points * hidden_units * 4,
    )

    half_units, half_channels = hidden_units // 2, channels // 2
    mlp_half = (half_units + channels, channels)
    mix_half = (basis_count, half_channels, channels)
    big, wide, many = (points, channels), (points, hidden_units), (basis_count, points, channels)
    core = place.flat % 2
    core_op = core[None].astype(jnp.int32)
    sized = (points // 5, hidden_units)
    feats, hidden, activated, pre_grad, mlp_send, mlp_keep = call(
        forward_kernel,
        (
            core_op, field_in, north, south, west, east, corners_west, corners_east, bands,
            mix_weight, up_weight, down_weight, cot,
        ),
        [smem] + [anywhere] * 12,
        [(many, low), (big, low), (wide, low), (wide, low), (mlp_half, low), (mlp_half, low)],
        [anywhere] * 6,
        [
            pltpu.VMEM((lat_rows + 2, width, channels), low),
            pltpu.VMEM(band_shape, low),
            pltpu.VMEM(mix_weight.shape, low),
            pltpu.VMEM(up_weight.shape, low),
            pltpu.VMEM(down_weight.shape, low),
            pltpu.VMEM(big, low),
            pltpu.VMEM(many, low),
            pltpu.VMEM(big, low),
            pltpu.VMEM(wide, low),
            pltpu.VMEM(wide, low),
            pltpu.VMEM((channels, points), low),
            pltpu.VMEM(sized, full),
            pltpu.VMEM(sized, full),
            pltpu.VMEM(sized, full),
            pltpu.VMEM(sized, full),
            pltpu.VMEM(mlp_half, low),
            pltpu.VMEM(mlp_half, low),
            pltpu.SemaphoreType.DMA((19 + lat_rows,)),
        ],
        band_gemm + mix_gemm + 4 * gemm,
        4 * points * hidden_units * 4,
    )
    def backward(start):
        return call(
            backward_kernel,
            (core_op, after(pre_grad, start), up_weight, cot, feats),
            [smem] + [anywhere] * 4,
            [(big, low), (mix_half, low), (mix_half, low)],
            [anywhere] * 3,
            [
                pltpu.VMEM(wide, low),
                pltpu.VMEM(up_weight.shape, low),
                pltpu.VMEM(big, low),
                pltpu.VMEM(many, low),
                pltpu.VMEM(big, low),
                pltpu.VMEM(mix_half, low),
                pltpu.VMEM(mix_half, low),
                pltpu.SemaphoreType.DMA((10 + basis_count,)),
            ],
            mix_gemm + gemm,
            3 * points * hidden_units * 4,
        )

    def block_of():
        return call(
            out_kernel,
            (hidden, activated, down_weight),
            [anywhere] * 3,
            [(big, low)],
            [anywhere],
            [
                pltpu.VMEM(big, low),
                pltpu.VMEM(wide, low),
                pltpu.VMEM(down_weight.shape, low),
                pltpu.VMEM(big, low),
                pltpu.SemaphoreType.DMA((10,)),
            ],
            gemm,
            2 * points * hidden_units * 4,
        )[0]

    def adjoint_of(hidden_grad, *start):
        side = (lat_rows + 2, reach, channels)
        return call(
            functools.partial(adjoint_kernel, cols=lon_cols),
            (after(hidden_grad, *start), mix_weight, bands),
            [anywhere] * 3,
            [
                (field_in.shape, low), ((2, lon_cols, channels), full), (side, low), (side, low),
            ],
            [anywhere] + [vmem] * 3,
            [
                pltpu.VMEM(big, low),
                pltpu.VMEM(mix_weight.shape, low),
                pltpu.VMEM(band_shape, low),
                pltpu.VMEM((lat_rows, basis_count * lon_cols, channels), low),
                pltpu.VMEM((lat_rows + 2, width, channels), full),
                pltpu.VMEM(field_in.shape, low),
                pltpu.SemaphoreType.DMA((1 + basis_count + 2 * lat_rows,)),
            ],
            band_gemm + mix_gemm,
            3 * points * hidden_units * 4,
        )

    grad_scale = 1.0 / math.sqrt(points * place.count)
    if place.count == 32:
        ring = Ring(place)
        block_shape = (2, 2, 2, mlp_half[0] // 8, channels)
        mlp = ring.to_core(mlp_keep.reshape(block_shape), mlp_send.reshape(block_shape))
        block_out = block_of()
        mlp_out = ring.leaving_first(after(mlp, block_out))
        hidden_grad, mix_send, mix_keep = backward(mlp_out)
        block_shape = (2, 2, 2, basis_count * half_channels // 8, channels)
        mix = ring.to_core(mix_keep.reshape(block_shape), mix_send.reshape(block_shape))
        mix_out = ring.leaving_first(mix)
        mlp = after(ring.first_step(mlp, mlp_out), mix_out)
        mlp_out = ring.leaving_second(mlp)
        mix = after(ring.first_step(mix, mix_out), *mlp_out)
        mix_out = ring.leaving_second(mix)
        mlp = after(ring.second_step(mlp, mlp_out), *mix_out)
        inner, rims, to_west, to_east = adjoint_of(hidden_grad, mlp)
        from_east = lax.ppermute(to_west, "lon", place.west)
        from_west = lax.ppermute(to_east, "lon", place.east)
        mix = after(ring.second_step(mix, mix_out), to_west)
        mlp_piece = after(ring.far_step(mlp, grad_scale), mix)
        mix_piece = ring.far_step(mix, grad_scale)
        mlp = ring.gather_near(mlp_piece)
        mix = ring.gather_near(mix_piece, mlp)
        mlp = ring.gather_second(mlp, mix)
        from_east, from_west, _ = lax.optimization_barrier((from_east, from_west, mlp))
        mix = ring.gather_second(mix, mlp)
        mlp = ring.gather_first(mlp, mix)
        mix = ring.gather_first(mix, mlp)
        mlp_other = ring.gather_core(mlp, mix).reshape(mlp_half)
        mlp = mlp.reshape(mlp_half)
        down_out = halves(core, mlp[:half_units], mlp_other[:half_units], 0)
        up_out = halves(core, mlp[half_units:], mlp_other[half_units:], 1)
        mix_other, down_out, up_out = lax.optimization_barrier(
            (ring.gather_core(mix).reshape(mix_half), down_out, up_out)
        )
        mix_out = halves(core, mix.reshape(mix_half), mix_other, 1)
    else:
        block_out = block_of()
        hidden_grad, mix_send, mix_keep = backward(mlp_send)
        inner, rims, to_west, to_east = adjoint_of(hidden_grad)
        from_east = lax.ppermute(to_west, "lon", place.west)
        from_west = lax.ppermute(to_east, "lon", place.east)

        def whole(keep, send):
            keep, send = keep.astype(full)[None], send.astype(full)[None]
            both = jnp.where(core == 0, jnp.concatenate([keep, send]), jnp.concatenate([send, keep]))
            return lax.psum(both, AXES) * grad_scale

        mlp_sum = whole(mlp_keep, mlp_send).astype(low)
        mix_sum = whole(mix_keep, mix_send).astype(low)
        down_out = mlp_sum[:, :half_units].reshape(down_weight.shape)
        up_out = jnp.concatenate([mlp_sum[0, half_units:], mlp_sum[1, half_units:]], axis=1)
        mix_out = mix_sum.swapaxes(0, 1).reshape(mix_weight.shape)

    corner_east = jnp.stack([from_east[0], from_east[lat_rows + 1]]).astype(full)
    corner_west = jnp.stack([from_west[0], from_west[lat_rows + 1]]).astype(full)
    rims = rims.at[:, lon_cols - reach :].add(corner_east)
    rims = rims.at[:, :reach].add(corner_west).astype(low)
    near = lax.ppermute(jnp.where(place.even, rims[1], rims[0]), AXES, place.pairs)
    far = lax.ppermute(jnp.where(place.even, rims[0], rims[1]), AXES, place.bridges)
    middle = lon_cols - 2 * reach
    beyond = jnp.stack(
        [jnp.where(place.even, far, near), jnp.where(place.even, near, far)]
    ).astype(full)
    sides = jnp.concatenate(
        [
            from_west[1 : lat_rows + 1].astype(full),
            jnp.zeros((lat_rows, middle, channels), full),
            from_east[1 : lat_rows + 1].astype(full),
        ],
        axis=1,
    )
    nothing = jnp.zeros((lat_rows - 2, lon_cols, channels), full)
    ends = jnp.concatenate([beyond[:1], nothing, beyond[1:]])
    grad_field = (inner.astype(full) + sides + ends).astype(low)
    return (block_out.reshape(field_in.shape), grad_field, mix_out, up_out, down_out)


def solution(mesh):
    placed = (
        P("lat", "lon", None),
        P(None, "lat", None, None),
        P("lat"),
        P(),
        P(),
        P(),
        P("lat", "lon", None),
    )
    return jax.shard_map(
        local,
        mesh=mesh,
        in_specs=placed,
        out_specs=(P("lat", "lon", None), P("lat", "lon", None), P(), P(), P()),
        check_vma=False,
    )
```

```python
import functools
import math

import jax
import jax.numpy as jnp
from jax import lax
from jax.experimental import pallas as pl
from jax.experimental.pallas import tpu as pltpu
from jax.sharding import PartitionSpec as P

inv_root_two = 0.7071067811865476
inv_root_tau = 0.3989422804014327
AXES = ("lat", "lon")


class Place:
    def __init__(self):
        self.lats = lax.axis_size("lat")
        self.lons = lax.axis_size("lon")
        self.count = self.lats * self.lons
        self.lat = lax.axis_index("lat")
        self.lon = lax.axis_index("lon")
        self.flat = self.lat * self.lons + self.lon
        lats, lons = self.lats, self.lons
        self.east = [(i, (i + 1) % lons) for i in range(lons)]
        self.west = [(j, i) for i, j in self.east]
        self.pairs = [
            (r * lons + c, (r ^ 1) * lons + c) for r in range(lats) for c in range(lons)
        ]
        self.bridges = []
        for r in range(lats):
            other = r - 1 if r % 2 == 0 else r + 1
            for c in range(lons):
                if 0 <= other < lats:
                    self.bridges.append((r * lons + c, other * lons + c))
                else:
                    self.bridges.append((r * lons + c, r * lons + (c + lons // 2) % lons))
        self.even = self.lat % 2 == 0


def route(place, mask_of):
    return [(i, i ^ mask_of(i)) for i in range(place.count)]


def send_along(place, block, mask_of):
    return lax.ppermute(block, AXES, route(place, mask_of))


def first_mask(i):
    return 2 if i % 2 == 0 else 4


def second_mask(i):
    return 4 if i % 2 == 0 else 2


def after(value, *others):
    return lax.optimization_barrier((value, *others))[0] if others else value


def pick(array, index):
    return lax.dynamic_index_in_dim(array, index, 0, keepdims=False)


def joined(bit, own, other):
    return jnp.concatenate([jnp.where(bit == 0, own, other), jnp.where(bit == 0, other, own)])


class Ring:
    def __init__(self, place):
        self.place = place
        self.core = place.flat % 2
        side_y, side_x = (place.flat // 2) % 2, (place.flat // 4) % 2
        self.first = jnp.where(self.core == 0, side_y, side_x)
        self.second = jnp.where(self.core == 0, side_x, side_y)
        self.near = (place.flat // 8) % 2

    def to_core(self, keep, send, *ties):
        got = [send_along(self.place, part, lambda i: 1) for part in send]
        if ties:
            got = lax.optimization_barrier((*got, *ties))[: len(got)]
        got = jnp.concatenate(got).reshape(keep.shape)
        return keep.astype(jnp.float32) + got.astype(jnp.float32)

    def leaving_first(self, buf):
        return pick(buf, 1 - self.first).astype(jnp.bfloat16)

    def first_step(self, buf, out):
        got = send_along(self.place, out, first_mask)
        return pick(buf, self.first) + got.astype(jnp.float32)

    def block(self, buf, over_second, over_near):
        at_second = 1 - self.second if over_second else self.second
        at_near = 1 - self.near if over_near else self.near
        return pick(pick(buf, at_second), at_near)

    def leaving_second(self, buf):
        return [
            self.block(buf, *over).astype(jnp.bfloat16)
            for over in ((True, False), (False, True), (True, True))
        ]

    def masks(self):
        return second_mask, lambda i: 8, lambda i: 8 + second_mask(i)

    def second_step(self, buf, outs, *ties):
        total = self.block(buf, False, False)
        got = [send_along(self.place, out, mask_of) for out, mask_of in zip(outs, self.masks())]
        for part in lax.optimization_barrier((*got, *ties))[:3]:
            total = total + part.astype(jnp.float32)
        return total.astype(jnp.bfloat16)

    def far_step(self, own, scale, *ties):
        far = after(send_along(self.place, own, lambda i: 16), *ties)
        return ((own.astype(jnp.float32) + far.astype(jnp.float32)) * scale).astype(own.dtype)

    def gather_near(self, piece, *ties):
        piece = piece[None]
        return joined(self.near, piece, after(send_along(self.place, piece, lambda i: 8), *ties))

    def gather_second(self, buf, *ties):
        return joined(self.second, buf, after(send_along(self.place, buf, second_mask), *ties))

    def gather_first(self, buf, *ties):
        return joined(self.first, buf, after(send_along(self.place, buf, first_mask), *ties))

    def gather_core(self, buf, *ties):
        return after(send_along(self.place, buf, lambda i: 1), *ties)


def halves(core, own, other, axis):
    size = own.shape[axis]
    shape = own.shape[:axis] + (2 * size,) + own.shape[axis + 1 :]
    out = jnp.zeros(shape, own.dtype)
    out = lax.dynamic_update_slice_in_dim(out, own, core * size, axis)
    return lax.dynamic_update_slice_in_dim(out, other, (1 - core) * size, axis)


OVER_ROWS = (((0,), (0,)), ((), ()))
OVER_LANES = (((1,), (1,)), ((), ()))
VMEM_LIMIT = 56 * 1024 * 1024


def dot(left, right, dims=(((1,), (0,)), ((), ()))):
    return lax.dot_general(left, right, dims, preferred_element_type=jnp.float32)


def tiles(count, size, body):
    def step(i, carry):
        body(pl.ds(pl.multiple_of(i * size, size), size))
        return carry

    lax.fori_loop(0, count // size, step, 0)


def band_kernel(reach_ref, taps, bands, lines, *, cols):
    basis, rows, _, count = taps.shape
    width = lines.shape[2]
    away = jnp.abs(lax.broadcasted_iota(jnp.int32, (3, count), 1) - (count - 1) // 2)
    lines[...] = jnp.zeros(lines.shape, lines.dtype)

    def one_row(r, carry):
        inside = away <= reach_ref[r]
        for k in range(basis):
            lines[k, :, :count] = jnp.where(inside, taps[k, r].astype(jnp.float32), 0.0)
            for d in range(3):
                line = jnp.broadcast_to(lines[k, pl.ds(d, 1)], (cols, width))
                band = pltpu.roll(line, 0, 1, stride=1, stride_axis=0)
                bands[r, k * cols : (k + 1) * cols, d * width : (d + 1) * width] = band.astype(
                    bands.dtype
                )
        return carry

    lax.fori_loop(0, rows, one_row, 0)


def started(pairs, sems, first=0):
    copies = [pltpu.make_async_copy(a, b, sems.at[first + i]) for i, (a, b) in enumerate(pairs)]
    for copy in copies:
        copy.start()
    return copies


def finish(copies):
    for copy in copies:
        copy.wait()


def forward_kernel(
    core_ref, field, north, south, west, east, corners_west, corners_east, bands_in, mix_in,
    up_in, down_in, cot_in,
    feats_out, hidden_out, act_out, pre_out, send_out, keep_out,
    ext, bands, mix, up, down, cot, feats, hidden, act, pre_grad, turned, pre_a, pre_b, ag_a,
    ag_b, send, keep, sems
):
    core = core_ref[0]
    rows, cols, channels = field.shape
    reach = west.shape[1]
    basis = mix.shape[0]
    points = rows * cols
    half_units = up.shape[1] // 2
    body, inner = pl.ds(1, rows), pl.ds(reach, cols)
    begin, end = pl.ds(0, reach), pl.ds(reach + cols, reach)
    loads = started(
        [
            (field, ext.at[body, inner]),
            (west, ext.at[body, begin]),
            (east, ext.at[body, end]),
            (north, ext.at[0, inner]),
            (south, ext.at[rows + 1, inner]),
            (corners_west.at[0], ext.at[0, begin]),
            (corners_west.at[1], ext.at[rows + 1, begin]),
            (corners_east.at[0], ext.at[0, end]),
            (corners_east.at[1], ext.at[rows + 1, end]),
        ],
        sems,
    )
    band_loads = started([(bands_in.at[r], bands.at[r]) for r in range(rows)], sems, 9)
    late = 9 + rows
    weights = started([(mix_in, mix), (up_in, up), (down_in, down), (cot_in, cot)], sems, late)
    finish(loads)

    for r in range(rows):
        finish(band_loads[r : r + 1])
        window = ext[r : r + 3].reshape(3 * ext.shape[1], channels)
        out = dot(bands[r], window).astype(feats.dtype)
        at = pl.ds(r * cols, cols)
        for k in range(basis):
            feats[k, at, :] = out[k * cols : (k + 1) * cols]
        hidden[at, :] = ext[r + 1, inner, :]
    stores = started([(feats, feats_out)], sems, late + 4)
    finish(weights[:1])

    for i in range(3):
        at = pl.ds(i * (points // 3), points // 3)
        total = hidden[at, :].astype(jnp.float32)
        for k in range(basis):
            total = total + dot(feats[k, at, :], mix[k])
        hidden[at, :] = total.astype(hidden.dtype)
    finish(weights[1:])
    stores += started([(hidden, hidden_out)], sems, late + 5)
    size = pre_a.shape[0]
    slots = ((pre_a, ag_a), (pre_b, ag_b))

    def products(i):
        at = pl.ds(i * size, size)
        pre, ag = slots[i % 2]
        pre[...] = dot(hidden[at, :], up[...])
        ag[...] = dot(cot[at, :], down[...], OVER_LANES)

    def activation(i):
        at = pl.ds(i * size, size)
        pre, ag = slots[i % 2]
        value = pre[...]
        phi = 0.5 * (1.0 + lax.erf(value * inv_root_two))
        act[at, :] = (value * phi).astype(act.dtype)
        slope = phi + value * jnp.exp(-0.5 * value * value) * inv_root_tau
        pre_grad[at, :] = (ag[...] * slope).astype(pre_grad.dtype)

    products(0)
    for i in range(points // size):
        if (i + 1) * size < points:
            products(i + 1)
        activation(i)
    stores += started([(act, act_out), (pre_grad, pre_out)], sems, late + 6)
    turned[...] = hidden[...].T

    def sums(half, out):
        at = pl.ds(pl.multiple_of(half * half_units, half_units), half_units)
        out[:half_units] = dot(act[:, at], cot[...], OVER_ROWS).astype(out.dtype)
        out[half_units:] = dot(turned[...], pre_grad[:, at]).astype(out.dtype)

    sums(1 - core, send)
    stores += started([(send, send_out)], sems, late + 8)
    sums(core, keep)
    stores += started([(keep, keep_out)], sems, late + 9)
    finish(stores)


def backward_kernel(
    core_ref, pre_in, up_in, cot_in, feats_in, hg_out, send_a, send_b, keep_out,
    pre_grad, up, cot, feats, hg, send, keep, sems
):
    core = core_ref[0]
    basis, points, channels = feats.shape
    half_channels = channels // 2
    parts = [pl.ds(i * (points // 3), points // 3) for i in range(3)]
    weights = started([(up_in, up)], sems)
    loads = started([(pre_in.at[at], pre_grad.at[at]) for at in parts], sems, 1)
    cot_loads = started([(cot_in.at[at], cot.at[at]) for at in parts], sems, 4)
    feat_loads = started([(feats_in.at[k], feats.at[k]) for k in range(basis)], sems, 7)
    late = 7 + basis
    finish(weights)
    for i, at in enumerate(parts):
        finish([loads[i], cot_loads[i]])
        total = cot[at, :].astype(jnp.float32) + dot(pre_grad[at, :], up[...], OVER_LANES)
        hg[at, :] = total.astype(hg.dtype)
    stores = started([(hg, hg_out)], sems, late)
    finish(feat_loads)

    def sums(half, out):
        at = pl.ds(pl.multiple_of(half * half_channels, half_channels), half_channels)
        for k in range(basis):
            out[k] = dot(feats[k, :, at], hg[...], OVER_ROWS).astype(out.dtype)

    sums(1 - core, send)
    part = send_a.shape[0]
    for k in range(basis):
        start, stop = k * half_channels, (k + 1) * half_channels
        for n, out in enumerate((send_a, send_b)):
            low, high = max(start, n * part), min(stop, (n + 1) * part)
            if low < high:
                source = send.at[k, pl.ds(low - start, high - low)]
                copies = [(source, out.at[pl.ds(low - n * part, high - low)])]
                stores += started(copies, sems, late + 1 + 2 * k + n)
    sums(core, keep)
    stores += started([(keep, keep_out)], sems, late + 1 + 2 * basis)
    finish(stores)


def out_kernel(hidden_in, act_in, down_in, block_out, hidden, act, down, block, sems):
    points = hidden.shape[0]
    parts = [pl.ds(i * (points // 3), points // 3) for i in range(3)]
    weights = started([(down_in, down)], sems)
    loads = started([(act_in.at[at], act.at[at]) for at in parts], sems, 1)
    more = started([(hidden_in.at[at], hidden.at[at]) for at in parts], sems, 4)
    finish(weights)
    stores = []
    for i, at in enumerate(parts):
        finish([loads[i], more[i]])
        total = hidden[at, :].astype(jnp.float32) + dot(act[at, :], down[...])
        block[at, :] = total.astype(block.dtype)
        stores += started([(block.at[at], block_out.at[at])], sems, 7 + i)
    finish(stores)


def adjoint_kernel(
    carry_in, hg_in, mix_in, bands_in, inner_out, rim_out, west_out, east_out, carry_out,
    hg, mix, bands, grads, pulled, inner, sems, *, cols, first
):
    basis, channels = mix.shape[0], mix.shape[1]
    rows, width = pulled.shape[0] - 2, pulled.shape[1]
    reach = (width - cols) // 2
    whole = west_out.shape[0]
    loads = started([(hg_in, hg)], sems)
    loads += started([(mix_in.at[k], mix.at[k]) for k in range(basis)], sems, 1)
    late = 1 + basis
    band_loads = started(
        [(bands_in.at[first + r], bands.at[r]) for r in range(rows)], sems, late
    )
    late += rows
    pulled[:2] = carry_in[...]
    pulled[2:] = jnp.zeros((rows, width, channels), pulled.dtype)
    finish(loads[:1])
    for k in range(basis):
        finish(loads[1 + k : 2 + k])
        part = dot(hg[first * cols : (first + rows) * cols, :], mix[k], OVER_LANES)
        grads[:, k * cols : (k + 1) * cols] = part.astype(grads.dtype).reshape(
            rows, cols, channels
        )
    stores = []
    skip = 1 if first == 0 else 0

    def give(row):
        at = (first + row - 1) * cols
        own = hg[at : at + cols, :].astype(jnp.float32)
        inner[row - skip] = (pulled[row, reach : reach + cols] + own).astype(inner.dtype)
        copies = [(inner.at[row - skip], inner_out.at[row - skip])]
        stores.extend(started(copies, sems, late + row - skip))

    for r in range(rows):
        finish(band_loads[r : r + 1])
        part = dot(bands[r], grads[r], OVER_ROWS)
        pulled[r : r + 3] += part.reshape(3, width, channels)
        if r >= skip:
            give(r)
    if whole > rows:
        give(rows)
    rim_out[...] = pulled[0 if first == 0 else rows + 1, reach : reach + cols]
    west_out[...] = pulled[:whole, :reach].astype(west_out.dtype)
    east_out[...] = pulled[:whole, reach + cols :].astype(east_out.dtype)
    carry_out[...] = pulled[rows:]
    finish(stores)


def call(kernel, operands, kinds, shapes, out_kinds, scratch, flops, nbytes):
    return pl.pallas_call(
        kernel,
        out_shape=[jax.ShapeDtypeStruct(shape, kind) for shape, kind in shapes],
        in_specs=[pl.BlockSpec(memory_space=kind) for kind in kinds],
        out_specs=[pl.BlockSpec(memory_space=kind) for kind in out_kinds],
        scratch_shapes=scratch,
        compiler_params=pltpu.CompilerParams(vmem_limit_bytes=VMEM_LIMIT),
        cost_estimate=pl.CostEstimate(flops=flops, bytes_accessed=nbytes, transcendentals=0),
    )(*operands)


def local(field_in, kernel_taps, row_reach, mix_weight, up_weight, down_weight, cotangent):
    lat_rows, lon_cols, channels = field_in.shape
    basis_count = kernel_taps.shape[0]
    tap_count = kernel_taps.shape[3]
    reach = (tap_count - 1) // 2
    hidden_units = up_weight.shape[1]
    place = Place()

    top, bottom = field_in[0], field_in[lat_rows - 1]
    inner = lax.ppermute(jnp.where(place.even, bottom, top), AXES, place.pairs)
    outer = lax.ppermute(jnp.where(place.even, top, bottom), AXES, place.bridges)
    west = lax.ppermute(field_in[:, lon_cols - reach :], "lon", place.east)
    east = lax.ppermute(field_in[:, :reach], "lon", place.west)
    north = jnp.where(place.even, outer, inner)
    south = jnp.where(place.even, inner, outer)
    corners = jnp.stack([north[lon_cols - reach :], south[lon_cols - reach :]])
    corners_west = lax.ppermute(corners, "lon", place.east)
    corners = jnp.stack([north[:reach], south[:reach]])
    corners_east = lax.ppermute(corners, "lon", place.west)

    low, full = jnp.bfloat16, jnp.float32
    points = lat_rows * lon_cols
    width = lon_cols + 2 * reach
    vmem, anywhere, smem = pltpu.VMEM, pl.ANY, pltpu.SMEM
    cot = cotangent.reshape(points, channels)
    band_shape = (lat_rows, basis_count * lon_cols, 3 * width)
    gemm = 2 * points * channels * hidden_units
    mix_gemm = 2 * points * channels * channels * basis_count
    band_gemm = 2 * lat_rows * basis_count * lon_cols * 3 * width * channels
    (bands,) = call(
        functools.partial(band_kernel, cols=lon_cols),
        (row_reach, kernel_taps),
        [smem, vmem],
        [(band_shape, low)],
        [vmem],
        [pltpu.VMEM((basis_count, 3, width), full)],
        0,
        2 * points * hidden_units * 4,
    )

    half_units, half_channels = hidden_units // 2, channels // 2
    mlp_half = (half_units + channels, channels)
    mix_half = (basis_count, half_channels, channels)
    mix_part = (basis_count * half_channels // 2, channels)
    big, wide, many = (points, channels), (points, hidden_units), (basis_count, points, channels)
    core = place.flat % 2
    core_op = core[None].astype(jnp.int32)
    sized = (points // 5, hidden_units)
    feats, hidden, activated, pre_grad, mlp_send, mlp_keep = call(
        forward_kernel,
        (
            core_op, field_in, north, south, west, east, corners_west, corners_east, bands,
            mix_weight, up_weight, down_weight, cot,
        ),
        [smem] + [anywhere] * 12,
        [(many, low), (big, low), (wide, low), (wide, low), (mlp_half, low), (mlp_half, low)],
        [anywhere] * 6,
        [
            pltpu.VMEM((lat_rows + 2, width, channels), low),
            pltpu.VMEM(band_shape, low),
            pltpu.VMEM(mix_weight.shape, low),
            pltpu.VMEM(up_weight.shape, low),
            pltpu.VMEM(down_weight.shape, low),
            pltpu.VMEM(big, low),
            pltpu.VMEM(many, low),
            pltpu.VMEM(big, low),
            pltpu.VMEM(wide, low),
            pltpu.VMEM(wide, low),
            pltpu.VMEM((channels, points), low),
            pltpu.VMEM(sized, full),
            pltpu.VMEM(sized, full),
            pltpu.VMEM(sized, full),
            pltpu.VMEM(sized, full),
            pltpu.VMEM(mlp_half, low),
            pltpu.VMEM(mlp_half, low),
            pltpu.SemaphoreType.DMA((19 + lat_rows,)),
        ],
        band_gemm + mix_gemm + 4 * gemm,
        4 * points * hidden_units * 4,
    )
    def backward(start):
        return call(
            backward_kernel,
            (core_op, after(pre_grad, start), up_weight, cot, feats),
            [smem] + [anywhere] * 4,
            [(big, low), (mix_part, low), (mix_part, low), (mix_half, low)],
            [anywhere] * 4,
            [
                pltpu.VMEM(wide, low),
                pltpu.VMEM(up_weight.shape, low),
                pltpu.VMEM(big, low),
                pltpu.VMEM(many, low),
                pltpu.VMEM(big, low),
                pltpu.VMEM(mix_half, low),
                pltpu.VMEM(mix_half, low),
                pltpu.SemaphoreType.DMA((9 + 3 * basis_count,)),
            ],
            mix_gemm + gemm,
            3 * points * hidden_units * 4,
        )

    def block_of():
        return call(
            out_kernel,
            (hidden, activated, down_weight),
            [anywhere] * 3,
            [(big, low)],
            [anywhere],
            [
                pltpu.VMEM(big, low),
                pltpu.VMEM(wide, low),
                pltpu.VMEM(down_weight.shape, low),
                pltpu.VMEM(big, low),
                pltpu.SemaphoreType.DMA((10,)),
            ],
            gemm,
            2 * points * hidden_units * 4,
        )[0]

    def adjoint_of(carry, hidden_grad, first, rows, last):
        side = (rows + 2 if last else rows, reach, channels)
        kept = rows + 1 if last else rows
        inner_rows = kept - 1 if first == 0 else kept
        inner_shape = (inner_rows, lon_cols, channels)
        return call(
            functools.partial(adjoint_kernel, cols=lon_cols, first=first),
            (carry, hidden_grad, mix_weight, bands),
            [vmem] + [anywhere] * 3,
            [
                (inner_shape, low), ((lon_cols, channels), full), (side, low), (side, low),
                ((2, width, channels), full),
            ],
            [anywhere] + [vmem] * 4,
            [
                pltpu.VMEM(big, low),
                pltpu.VMEM(mix_weight.shape, low),
                pltpu.VMEM((rows,) + band_shape[1:], low),
                pltpu.VMEM((rows, basis_count * lon_cols, channels), low),
                pltpu.VMEM((rows + 2, width, channels), full),
                pltpu.VMEM(inner_shape, low),
                pltpu.SemaphoreType.DMA((3 + basis_count + 2 * rows,)),
            ],
            (band_gemm + mix_gemm) // 2,
            2 * points * hidden_units * 4,
        )

    upper = lat_rows // 2

    def adjoint_begin(hidden_grad, *start):
        hidden_grad = after(hidden_grad, *start)
        carry = jnp.zeros((2, width, channels), full)
        return hidden_grad, adjoint_of(carry, hidden_grad, 0, upper, False)

    def adjoint_end(hidden_grad, begun, *start):
        carry = after(begun[4], *start)
        ended = adjoint_of(carry, hidden_grad, upper, lat_rows - upper, True)
        return [
            jnp.concatenate([begun[0], ended[0]]),
            jnp.stack([begun[1], ended[1]]),
            jnp.concatenate([begun[2], ended[2]]),
            jnp.concatenate([begun[3], ended[3]]),
        ]

    grad_scale = 1.0 / math.sqrt(points * place.count)
    if place.count == 32:
        ring = Ring(place)
        block_shape = (2, 2, 2, mlp_half[0] // 8, channels)
        mlp = ring.to_core(mlp_keep.reshape(block_shape), [mlp_send])
        block_out = block_of()
        mlp_out = ring.leaving_first(after(mlp, block_out))
        hidden_grad, *mix_send, mix_keep = backward(mlp_out)
        block_shape = (2, 2, 2, basis_count * half_channels // 8, channels)
        mlp = ring.first_step(mlp, mlp_out)
        mlp_out = ring.leaving_second(mlp)
        mix = ring.to_core(mix_keep.reshape(block_shape), mix_send, *mlp_out)
        mix_out = ring.leaving_first(mix)
        hidden_grad, begun = adjoint_begin(hidden_grad, mix_out, *mlp_out)
        mlp = ring.second_step(mlp, [*mlp_out], begun[4])
        mix = after(ring.first_step(mix, mix_out), mlp)
        mix_out = ring.leaving_second(mix)
        inner, rims, to_west, to_east = adjoint_end(hidden_grad, begun, mlp, *mix_out)
        from_east = lax.ppermute(to_west, "lon", place.west)
        from_west = lax.ppermute(to_east, "lon", place.east)
        mix = after(ring.second_step(mix, mix_out), to_west)
        mlp_piece = ring.far_step(mlp, grad_scale, mix)
        mix_piece = ring.far_step(mix, grad_scale)
        mlp = ring.gather_near(mlp_piece)
        mix = ring.gather_near(mix_piece, mlp)
        mlp = ring.gather_second(mlp, mix)
        from_east, from_west, _ = lax.optimization_barrier((from_east, from_west, mlp))
        mix = ring.gather_second(mix, mlp)
        mlp = ring.gather_first(mlp, mix)
        mix = ring.gather_first(mix, mlp)
        last_block = mix
        mlp_other = ring.gather_core(mlp, mix).reshape(mlp_half)
        mlp = mlp.reshape(mlp_half)
        down_out = halves(core, mlp[:half_units], mlp_other[:half_units], 0)
        up_out = halves(core, mlp[half_units:], mlp_other[half_units:], 1)
        mix_other, down_out, up_out = lax.optimization_barrier(
            (ring.gather_core(mix).reshape(mix_half), down_out, up_out)
        )
        mix_out = halves(core, mix.reshape(mix_half), mix_other, 1)
    else:
        block_out = block_of()
        hidden_grad, *mix_send, mix_keep = backward(mlp_send)
        last_block = mix_keep
        hidden_grad, begun = adjoint_begin(hidden_grad)
        inner, rims, to_west, to_east = adjoint_end(hidden_grad, begun)
        from_east = lax.ppermute(to_west, "lon", place.west)
        from_west = lax.ppermute(to_east, "lon", place.east)

        def whole(keep, send):
            keep, send = keep.astype(full)[None], send.astype(full).reshape((1,) + keep.shape)
            both = jnp.where(core == 0, jnp.concatenate([keep, send]), jnp.concatenate([send, keep]))
            return lax.psum(both, AXES) * grad_scale

        mlp_sum = whole(mlp_keep, mlp_send).astype(low)
        mix_sum = whole(mix_keep, jnp.concatenate(mix_send)).astype(low)
        down_out = mlp_sum[:, :half_units].reshape(down_weight.shape)
        up_out = jnp.concatenate([mlp_sum[0, half_units:], mlp_sum[1, half_units:]], axis=1)
        mix_out = mix_sum.swapaxes(0, 1).reshape(mix_weight.shape)

    corner_east = jnp.stack([from_east[0], from_east[lat_rows + 1]]).astype(full)
    corner_west = jnp.stack([from_west[0], from_west[lat_rows + 1]]).astype(full)
    rims = rims.at[:, lon_cols - reach :].add(corner_east)
    rims = rims.at[:, :reach].add(corner_west).astype(low)
    near = lax.ppermute(jnp.where(place.even, rims[1], rims[0]), AXES, place.pairs)
    far = lax.ppermute(jnp.where(place.even, rims[0], rims[1]), AXES, place.bridges)
    near, far, _ = lax.optimization_barrier((near, far, last_block))
    middle = lon_cols - 2 * reach
    beyond = jnp.stack(
        [jnp.where(place.even, far, near), jnp.where(place.even, near, far)]
    ).astype(full)
    sides = jnp.concatenate(
        [
            from_west[1 : lat_rows + 1].astype(full),
            jnp.zeros((lat_rows, middle, channels), full),
            from_east[1 : lat_rows + 1].astype(full),
        ],
        axis=1,
    )
    nothing = jnp.zeros((lat_rows - 2, lon_cols, channels), full)
    ends = jnp.concatenate([beyond[:1], nothing, beyond[1:]])
    grad_field = (inner.astype(full) + sides + ends).astype(low)
    return (block_out.reshape(field_in.shape), grad_field, mix_out, up_out, down_out)


def solution(mesh):
    placed = (
        P("lat", "lon", None),
        P(None, "lat", None, None),
        P("lat"),
        P(),
        P(),
        P(),
        P("lat", "lon", None),
    )
    return jax.shard_map(
        local,
        mesh=mesh,
        in_specs=placed,
        out_specs=(P("lat", "lon", None), P("lat", "lon", None), P(), P(), P()),
        check_vma=False,
    )
```

```python
import functools
import math

import jax
import jax.numpy as jnp
from jax import lax
from jax.experimental import pallas as pl
from jax.experimental.pallas import tpu as pltpu
from jax.sharding import PartitionSpec as P

inv_root_two = 0.7071067811865476
inv_root_tau = 0.3989422804014327
AXES = ("lat", "lon")


class Place:
    def __init__(self):
        self.lats = lax.axis_size("lat")
        self.lons = lax.axis_size("lon")
        self.count = self.lats * self.lons
        self.lat = lax.axis_index("lat")
        self.lon = lax.axis_index("lon")
        self.flat = self.lat * self.lons + self.lon
        lats, lons = self.lats, self.lons
        self.east = [(i, (i + 1) % lons) for i in range(lons)]
        self.west = [(j, i) for i, j in self.east]
        self.pairs = [
            (r * lons + c, (r ^ 1) * lons + c) for r in range(lats) for c in range(lons)
        ]
        self.bridges = []
        for r in range(lats):
            other = r - 1 if r % 2 == 0 else r + 1
            for c in range(lons):
                if 0 <= other < lats:
                    self.bridges.append((r * lons + c, other * lons + c))
                else:
                    self.bridges.append((r * lons + c, r * lons + (c + lons // 2) % lons))
        self.even = self.lat % 2 == 0


def route(place, mask_of):
    return [(i, i ^ mask_of(i)) for i in range(place.count)]


def send_along(place, block, mask_of):
    return lax.ppermute(block, AXES, route(place, mask_of))


def first_mask(i):
    return 2 if i % 2 == 0 else 4


def second_mask(i):
    return 4 if i % 2 == 0 else 2


def after(value, *others):
    return lax.optimization_barrier((value, *others))[0] if others else value


def near_mask(i):
    return 8


def pick(array, index):
    return lax.dynamic_index_in_dim(array, index, 0, keepdims=False)


def joined(bit, own, other):
    return jnp.concatenate([jnp.where(bit == 0, own, other), jnp.where(bit == 0, other, own)])


class Ring:
    def __init__(self, place):
        self.place = place
        self.core = place.flat % 2
        side_y, side_x = (place.flat // 2) % 2, (place.flat // 4) % 2
        self.first = jnp.where(self.core == 0, side_y, side_x)
        self.second = jnp.where(self.core == 0, side_x, side_y)
        self.near = (place.flat // 8) % 2

    def to_core(self, keep, send):
        got = send_along(self.place, send, lambda i: 1)
        return keep.astype(jnp.float32) + got.astype(jnp.float32)

    def leaving(self, buf, bit):
        return pick(buf, 1 - bit).astype(jnp.bfloat16)

    def step(self, buf, out, mask_of, bit, *ties):
        got = after(send_along(self.place, out, mask_of), *ties)
        return pick(buf, bit) + got.astype(jnp.float32)

    def far_step(self, own, scale, *ties):
        far = after(send_along(self.place, own, lambda i: 16), *ties)
        return ((own.astype(jnp.float32) + far.astype(jnp.float32)) * scale).astype(own.dtype)

    def gather_near(self, piece, *ties):
        piece = piece[None]
        return joined(self.near, piece, after(send_along(self.place, piece, near_mask), *ties))

    def gather_second(self, buf, *ties):
        return joined(self.second, buf, after(send_along(self.place, buf, second_mask), *ties))

    def gather_first(self, buf, *ties):
        return joined(self.first, buf, after(send_along(self.place, buf, first_mask), *ties))

    def gather_core(self, buf, *ties):
        return after(send_along(self.place, buf, lambda i: 1), *ties)


def halves(core, own, other, axis):
    size = own.shape[axis]
    shape = own.shape[:axis] + (2 * size,) + own.shape[axis + 1 :]
    out = jnp.zeros(shape, own.dtype)
    out = lax.dynamic_update_slice_in_dim(out, own, core * size, axis)
    return lax.dynamic_update_slice_in_dim(out, other, (1 - core) * size, axis)


OVER_ROWS = (((0,), (0,)), ((), ()))
OVER_LANES = (((1,), (1,)), ((), ()))
VMEM_LIMIT = 56 * 1024 * 1024


def dot(left, right, dims=(((1,), (0,)), ((), ()))):
    return lax.dot_general(left, right, dims, preferred_element_type=jnp.float32)


def tiles(count, size, body):
    def step(i, carry):
        body(pl.ds(pl.multiple_of(i * size, size), size))
        return carry

    lax.fori_loop(0, count // size, step, 0)


def band_kernel(reach_ref, taps, bands, lines, *, cols):
    basis, rows, _, count = taps.shape
    width = lines.shape[2]
    away = jnp.abs(lax.broadcasted_iota(jnp.int32, (3, count), 1) - (count - 1) // 2)
    lines[...] = jnp.zeros(lines.shape, lines.dtype)

    def one_row(r, carry):
        inside = away <= reach_ref[r]
        for k in range(basis):
            lines[k, :, :count] = jnp.where(inside, taps[k, r].astype(jnp.float32), 0.0)
            for d in range(3):
                line = jnp.broadcast_to(lines[k, pl.ds(d, 1)], (cols, width))
                band = pltpu.roll(line, 0, 1, stride=1, stride_axis=0)
                bands[r, k * cols : (k + 1) * cols, d * width : (d + 1) * width] = band.astype(
                    bands.dtype
                )
        return carry

    lax.fori_loop(0, rows, one_row, 0)


def started(pairs, sems, first=0):
    copies = [pltpu.make_async_copy(a, b, sems.at[first + i]) for i, (a, b) in enumerate(pairs)]
    for copy in copies:
        copy.start()
    return copies


def finish(copies):
    for copy in copies:
        copy.wait()


def main_kernel(
    core_ref, field, north, south, west, east, corners_west, corners_east, bands_in, mix_in,
    up_in, down_in, cot_in,
    block_out, hg_out, mlp_send_out, mlp_keep_out, mix_send_out, mix_keep_out,
    ext, bands, mix, up, down, cot, feats, hidden, act, pre_grad, hg, block, turned, pre_a,
    pre_b, ag_a, ag_b, mlp_send, mlp_keep, mix_send, mix_keep, sems
):
    core = core_ref[0]
    rows, cols, channels = field.shape
    reach = west.shape[1]
    basis = mix.shape[0]
    points = rows * cols
    half_units, half_channels = up.shape[1] // 2, channels // 2
    body, inner = pl.ds(1, rows), pl.ds(reach, cols)
    begin, end = pl.ds(0, reach), pl.ds(reach + cols, reach)
    loads = started(
        [
            (field, ext.at[body, inner]),
            (west, ext.at[body, begin]),
            (east, ext.at[body, end]),
            (north, ext.at[0, inner]),
            (south, ext.at[rows + 1, inner]),
            (corners_west.at[0], ext.at[0, begin]),
            (corners_west.at[1], ext.at[rows + 1, begin]),
            (corners_east.at[0], ext.at[0, end]),
            (corners_east.at[1], ext.at[rows + 1, end]),
        ],
        sems,
    )
    band_loads = started([(bands_in.at[r], bands.at[r]) for r in range(rows)], sems, 9)
    late = 9 + rows
    weights = started([(mix_in, mix), (up_in, up), (down_in, down), (cot_in, cot)], sems, late)
    finish(loads)

    for r in range(rows):
        finish(band_loads[r : r + 1])
        window = ext[r : r + 3].reshape(3 * ext.shape[1], channels)
        out = dot(bands[r], window).astype(feats.dtype)
        at = pl.ds(r * cols, cols)
        for k in range(basis):
            feats[k, at, :] = out[k * cols : (k + 1) * cols]
        hidden[at, :] = ext[r + 1, inner, :]
    finish(weights[:1])

    for i in range(3):
        at = pl.ds(i * (points // 3), points // 3)
        total = hidden[at, :].astype(jnp.float32)
        for k in range(basis):
            total = total + dot(feats[k, at, :], mix[k])
        hidden[at, :] = total.astype(hidden.dtype)
    finish(weights[1:])
    size = pre_a.shape[0]
    slots = ((pre_a, ag_a), (pre_b, ag_b))

    def products(i):
        at = pl.ds(i * size, size)
        pre, ag = slots[i % 2]
        pre[...] = dot(hidden[at, :], up[...])
        ag[...] = dot(cot[at, :], down[...], OVER_LANES)

    def activation(i):
        at = pl.ds(i * size, size)
        pre, ag = slots[i % 2]
        value = pre[...]
        phi = 0.5 * (1.0 + lax.erf(value * inv_root_two))
        act[at, :] = (value * phi).astype(act.dtype)
        slope = phi + value * jnp.exp(-0.5 * value * value) * inv_root_tau
        pre_grad[at, :] = (ag[...] * slope).astype(pre_grad.dtype)

    products(0)
    for i in range(points // size):
        if (i + 1) * size < points:
            products(i + 1)
        activation(i)
    turned[...] = hidden[...].T

    def mlp_sums(half, out):
        at = pl.ds(pl.multiple_of(half * half_units, half_units), half_units)
        out[:half_units] = dot(act[:, at], cot[...], OVER_ROWS).astype(out.dtype)
        out[half_units:] = dot(turned[...], pre_grad[:, at]).astype(out.dtype)

    mlp_sums(1 - core, mlp_send)
    stores = started([(mlp_send, mlp_send_out)], sems, late + 4)
    mlp_sums(core, mlp_keep)
    stores += started([(mlp_keep, mlp_keep_out)], sems, late + 5)

    parts = [pl.ds(i * (points // 3), points // 3) for i in range(3)]
    for at in parts:
        total = cot[at, :].astype(jnp.float32) + dot(pre_grad[at, :], up[...], OVER_LANES)
        hg[at, :] = total.astype(hg.dtype)
    stores += started([(hg, hg_out)], sems, late + 6)

    def mix_sums(half, out):
        at = pl.ds(pl.multiple_of(half * half_channels, half_channels), half_channels)
        for k in range(basis):
            out[k] = dot(feats[k, :, at], hg[...], OVER_ROWS).astype(out.dtype)

    mix_sums(1 - core, mix_send)
    stores += started([(mix_send, mix_send_out)], sems, late + 7)
    mix_sums(core, mix_keep)
    stores += started([(mix_keep, mix_keep_out)], sems, late + 8)

    for i, at in enumerate(parts):
        total = hidden[at, :].astype(jnp.float32) + dot(act[at, :], down[...])
        block[at, :] = total.astype(block.dtype)
        stores += started([(block.at[at], block_out.at[at])], sems, late + 9 + i)
    finish(stores)


def adjoint_kernel(
    hg_in, mix_in, bands_in, inner_out, rim_out, west_out, east_out,
    hg, mix, bands, grads, pulled, inner, sems, *, cols
):
    basis, channels = mix.shape[0], mix.shape[1]
    rows, width = pulled.shape[0] - 2, pulled.shape[1]
    reach = (width - cols) // 2
    loads = started([(hg_in, hg)], sems)
    loads += started([(mix_in.at[k], mix.at[k]) for k in range(basis)], sems, 1)
    late = 1 + basis
    band_loads = started([(bands_in.at[r], bands.at[r]) for r in range(rows)], sems, late)
    pulled[...] = jnp.zeros(pulled.shape, pulled.dtype)
    group = 5 if rows % 5 == 0 else 1
    finish(loads[:1])
    for k in range(basis):
        finish(loads[1 + k : 2 + k])
        for r in range(0, rows, group):
            part = dot(hg[r * cols : (r + group) * cols, :], mix[k], OVER_LANES)
            grads[r : r + group, k * cols : (k + 1) * cols] = part.astype(grads.dtype).reshape(
                group, cols, channels
            )
    stores = []

    def give(row):
        own = hg[(row - 1) * cols : row * cols, :].astype(jnp.float32)
        inner[row - 1] = (pulled[row, reach : reach + cols] + own).astype(inner.dtype)
        copies = [(inner.at[row - 1], inner_out.at[row - 1])]
        stores.extend(started(copies, sems, late + rows + row - 1))

    for r in range(rows):
        finish(band_loads[r : r + 1])
        part = dot(bands[r], grads[r], OVER_ROWS)
        pulled[r : r + 3] += part.reshape(3, width, channels)
        if r:
            give(r)
    give(rows)
    west_out[...] = pulled[:, :reach].astype(west_out.dtype)
    east_out[...] = pulled[:, reach + cols :].astype(east_out.dtype)
    for n, r in enumerate((0, rows + 1)):
        rim_out[n] = pulled[r, reach : reach + cols]
    finish(stores)


def call(kernel, operands, kinds, shapes, out_kinds, scratch, flops, nbytes):
    return pl.pallas_call(
        kernel,
        out_shape=[jax.ShapeDtypeStruct(shape, kind) for shape, kind in shapes],
        in_specs=[pl.BlockSpec(memory_space=kind) for kind in kinds],
        out_specs=[pl.BlockSpec(memory_space=kind) for kind in out_kinds],
        scratch_shapes=scratch,
        compiler_params=pltpu.CompilerParams(vmem_limit_bytes=VMEM_LIMIT),
        cost_estimate=pl.CostEstimate(flops=flops, bytes_accessed=nbytes, transcendentals=0),
    )(*operands)


def local(field_in, kernel_taps, row_reach, mix_weight, up_weight, down_weight, cotangent):
    lat_rows, lon_cols, channels = field_in.shape
    basis_count = kernel_taps.shape[0]
    tap_count = kernel_taps.shape[3]
    reach = (tap_count - 1) // 2
    hidden_units = up_weight.shape[1]
    place = Place()

    top, bottom = field_in[0], field_in[lat_rows - 1]
    inner = lax.ppermute(jnp.where(place.even, bottom, top), AXES, place.pairs)
    outer = lax.ppermute(jnp.where(place.even, top, bottom), AXES, place.bridges)
    west = lax.ppermute(field_in[:, lon_cols - reach :], "lon", place.east)
    east = lax.ppermute(field_in[:, :reach], "lon", place.west)
    north = jnp.where(place.even, outer, inner)
    south = jnp.where(place.even, inner, outer)
    corners = jnp.stack([north[lon_cols - reach :], south[lon_cols - reach :]])
    corners_west = lax.ppermute(corners, "lon", place.east)
    corners = jnp.stack([north[:reach], south[:reach]])
    corners_east = lax.ppermute(corners, "lon", place.west)

    low, full = jnp.bfloat16, jnp.float32
    points = lat_rows * lon_cols
    width = lon_cols + 2 * reach
    vmem, anywhere, smem = pltpu.VMEM, pl.ANY, pltpu.SMEM
    cot = cotangent.reshape(points, channels)
    band_shape = (lat_rows, basis_count * lon_cols, 3 * width)
    gemm = 2 * points * channels * hidden_units
    mix_gemm = 2 * points * channels * channels * basis_count
    band_gemm = 2 * lat_rows * basis_count * lon_cols * 3 * width * channels
    (bands,) = call(
        functools.partial(band_kernel, cols=lon_cols),
        (row_reach, kernel_taps),
        [smem, vmem],
        [(band_shape, low)],
        [vmem],
        [pltpu.VMEM((basis_count, 3, width), full)],
        0,
        2 * points * hidden_units * 4,
    )

    half_units, half_channels = hidden_units // 2, channels // 2
    mlp_half = (half_units + channels, channels)
    mix_half = (basis_count, half_channels, channels)
    big, wide, many = (points, channels), (points, hidden_units), (basis_count, points, channels)
    core = place.flat % 2
    core_op = core[None].astype(jnp.int32)
    sized = (points // 5, hidden_units)
    block_out, hidden_grad, mlp_send, mlp_keep, mix_send, mix_keep = call(
        main_kernel,
        (
            core_op, field_in, north, south, west, east, corners_west, corners_east, bands,
            mix_weight, up_weight, down_weight, cot,
        ),
        [smem] + [anywhere] * 12,
        [(big, low), (big, low), (mlp_half, low), (mlp_half, low), (mix_half, low), (mix_half, low)],
        [anywhere] * 6,
        [
            pltpu.VMEM((lat_rows + 2, width, channels), low),
            pltpu.VMEM(band_shape, low),
            pltpu.VMEM(mix_weight.shape, low),
            pltpu.VMEM(up_weight.shape, low),
            pltpu.VMEM(down_weight.shape, low),
            pltpu.VMEM(big, low),
            pltpu.VMEM(many, low),
            pltpu.VMEM(big, low),
            pltpu.VMEM(wide, low),
            pltpu.VMEM(wide, low),
            pltpu.VMEM(big, low),
            pltpu.VMEM(big, low),
            pltpu.VMEM((channels, points), low),
            pltpu.VMEM(sized, full),
            pltpu.VMEM(sized, full),
            pltpu.VMEM(sized, full),
            pltpu.VMEM(sized, full),
            pltpu.VMEM(mlp_half, low),
            pltpu.VMEM(mlp_half, low),
            pltpu.VMEM(mix_half, low),
            pltpu.VMEM(mix_half, low),
            pltpu.SemaphoreType.DMA((21 + lat_rows,)),
        ],
        band_gemm + 2 * mix_gemm + 6 * gemm,
        7 * points * hidden_units * 2,
    )

    def adjoint_of(hidden_grad, *start):
        side = (lat_rows + 2, reach, channels)
        return call(
            functools.partial(adjoint_kernel, cols=lon_cols),
            (after(hidden_grad, *start), mix_weight, bands),
            [anywhere] * 3,
            [
                (field_in.shape, low), ((2, lon_cols, channels), full), (side, low), (side, low),
            ],
            [anywhere] + [vmem] * 3,
            [
                pltpu.VMEM(big, low),
                pltpu.VMEM(mix_weight.shape, low),
                pltpu.VMEM(band_shape, low),
                pltpu.VMEM((lat_rows, basis_count * lon_cols, channels), low),
                pltpu.VMEM((lat_rows + 2, width, channels), full),
                pltpu.VMEM(field_in.shape, low),
                pltpu.SemaphoreType.DMA((1 + basis_count + 2 * lat_rows,)),
            ],
            band_gemm + mix_gemm,
            3 * points * hidden_units * 4,
        )

    grad_scale = 1.0 / math.sqrt(points * place.count)
    if place.count == 32:
        ring = Ring(place)
        block_shape = (2, 2, 2, mlp_half[0] // 8, channels)
        mlp = ring.to_core(mlp_keep.reshape(block_shape), mlp_send.reshape(block_shape))
        mlp_out = ring.leaving(mlp, ring.first)
        block_shape = (2, 2, 2, basis_count * half_channels // 8, channels)
        mix = ring.to_core(mix_keep.reshape(block_shape), mix_send.reshape(block_shape))
        mix_out = ring.leaving(mix, ring.first)
        inner, rims, to_west, to_east = adjoint_of(hidden_grad, mlp_out, mix_out)
        from_east = lax.ppermute(to_west, "lon", place.west)
        from_west = lax.ppermute(to_east, "lon", place.east)
        mlp = ring.step(mlp, mlp_out, first_mask, ring.first, to_west)
        mlp_out = ring.leaving(mlp, ring.second)
        mix = ring.step(mix, mix_out, first_mask, ring.first, mlp_out)
        mix_out = ring.leaving(mix, ring.second)
        mlp = ring.step(mlp, mlp_out, second_mask, ring.second, mix_out)
        mlp_out = ring.leaving(mlp, ring.near)
        mix = ring.step(mix, mix_out, second_mask, ring.second, mlp_out)
        mix_out = ring.leaving(mix, ring.near)
        mlp = ring.step(mlp, mlp_out, near_mask, ring.near, mix_out).astype(low)
        mix = ring.step(mix, mix_out, near_mask, ring.near, mlp).astype(low)
        mlp_piece = ring.far_step(mlp, grad_scale, mix)
        mix_piece = ring.far_step(mix, grad_scale, mlp_piece)
        mlp = ring.gather_near(mlp_piece)
        mix = ring.gather_near(mix_piece, mlp)
        mlp = ring.gather_second(mlp, mix)
        from_east, from_west, _ = lax.optimization_barrier((from_east, from_west, mlp))
        mix = ring.gather_second(mix, mlp)
        mlp = ring.gather_first(mlp, mix)
        mix = ring.gather_first(mix, mlp)
        last_block = mix
        mlp_other = ring.gather_core(mlp, mix).reshape(mlp_half)
        mlp = mlp.reshape(mlp_half)
        down_out = halves(core, mlp[:half_units], mlp_other[:half_units], 0)
        up_out = halves(core, mlp[half_units:], mlp_other[half_units:], 1)
        mix_other, down_out, up_out = lax.optimization_barrier(
            (ring.gather_core(mix).reshape(mix_half), down_out, up_out)
        )
        mix_out = halves(core, mix.reshape(mix_half), mix_other, 1)
    else:
        last_block = mix_keep
        inner, rims, to_west, to_east = adjoint_of(hidden_grad)
        from_east = lax.ppermute(to_west, "lon", place.west)
        from_west = lax.ppermute(to_east, "lon", place.east)

        def whole(keep, send):
            keep, send = keep.astype(full)[None], send.astype(full)[None]
            both = jnp.where(core == 0, jnp.concatenate([keep, send]), jnp.concatenate([send, keep]))
            return lax.psum(both, AXES) * grad_scale

        mlp_sum = whole(mlp_keep, mlp_send).astype(low)
        mix_sum = whole(mix_keep, mix_send).astype(low)
        down_out = mlp_sum[:, :half_units].reshape(down_weight.shape)
        up_out = jnp.concatenate([mlp_sum[0, half_units:], mlp_sum[1, half_units:]], axis=1)
        mix_out = mix_sum.swapaxes(0, 1).reshape(mix_weight.shape)

    corner_east = jnp.stack([from_east[0], from_east[lat_rows + 1]]).astype(full)
    corner_west = jnp.stack([from_west[0], from_west[lat_rows + 1]]).astype(full)
    rims = rims.at[:, lon_cols - reach :].add(corner_east)
    rims = rims.at[:, :reach].add(corner_west).astype(low)
    near = lax.ppermute(jnp.where(place.even, rims[1], rims[0]), AXES, place.pairs)
    far = lax.ppermute(jnp.where(place.even, rims[0], rims[1]), AXES, place.bridges)
    near, far, _ = lax.optimization_barrier((near, far, last_block))
    middle = lon_cols - 2 * reach
    beyond = jnp.stack(
        [jnp.where(place.even, far, near), jnp.where(place.even, near, far)]
    ).astype(full)
    sides = jnp.concatenate(
        [
            from_west[1 : lat_rows + 1].astype(full),
            jnp.zeros((lat_rows, middle, channels), full),
            from_east[1 : lat_rows + 1].astype(full),
        ],
        axis=1,
    )
    nothing = jnp.zeros((lat_rows - 2, lon_cols, channels), full)
    ends = jnp.concatenate([beyond[:1], nothing, beyond[1:]])
    grad_field = (inner.astype(full) + sides + ends).astype(low)
    return (block_out.reshape(field_in.shape), grad_field, mix_out, up_out, down_out)


def solution(mesh):
    placed = (
        P("lat", "lon", None),
        P(None, "lat", None, None),
        P("lat"),
        P(),
        P(),
        P(),
        P("lat", "lon", None),
    )
    return jax.shard_map(
        local,
        mesh=mesh,
        in_specs=placed,
        out_specs=(P("lat", "lon", None), P("lat", "lon", None), P(), P(), P()),
        check_vma=False,
    )
```

```python
import functools
import math

import jax
import jax.numpy as jnp
from jax import lax
from jax.experimental import pallas as pl
from jax.experimental.pallas import tpu as pltpu
from jax.sharding import PartitionSpec as P

inv_root_two = 0.7071067811865476
inv_root_tau = 0.3989422804014327
AXES = ("lat", "lon")


class Place:
    def __init__(self):
        self.lats = lax.axis_size("lat")
        self.lons = lax.axis_size("lon")
        self.count = self.lats * self.lons
        self.lat = lax.axis_index("lat")
        self.lon = lax.axis_index("lon")
        self.flat = self.lat * self.lons + self.lon
        lats, lons = self.lats, self.lons
        self.east = [(i, (i + 1) % lons) for i in range(lons)]
        self.west = [(j, i) for i, j in self.east]
        self.pairs = [
            (r * lons + c, (r ^ 1) * lons + c) for r in range(lats) for c in range(lons)
        ]
        self.bridges = []
        for r in range(lats):
            other = r - 1 if r % 2 == 0 else r + 1
            for c in range(lons):
                if 0 <= other < lats:
                    self.bridges.append((r * lons + c, other * lons + c))
                else:
                    self.bridges.append((r * lons + c, r * lons + (c + lons // 2) % lons))
        self.even = self.lat % 2 == 0


def route(place, mask_of):
    return [(i, i ^ mask_of(i)) for i in range(place.count)]


def send_along(place, block, mask_of):
    return lax.ppermute(block, AXES, route(place, mask_of))


def first_mask(i):
    return 2 if i % 2 == 0 else 4


def second_mask(i):
    return 4 if i % 2 == 0 else 2


def after(value, *others):
    return lax.optimization_barrier((value, *others))[0] if others else value


def near_mask(i):
    return 8


def pick(array, index):
    return lax.dynamic_index_in_dim(array, index, 0, keepdims=False)


def joined(bit, own, other):
    return jnp.concatenate([jnp.where(bit == 0, own, other), jnp.where(bit == 0, other, own)])


class Ring:
    def __init__(self, place):
        self.place = place
        self.core = place.flat % 2
        side_y, side_x = (place.flat // 2) % 2, (place.flat // 4) % 2
        self.first = jnp.where(self.core == 0, side_y, side_x)
        self.second = jnp.where(self.core == 0, side_x, side_y)
        self.near = (place.flat // 8) % 2

    def to_core(self, keep, send):
        got = send_along(self.place, send, lambda i: 1)
        return keep.astype(jnp.float32) + got.astype(jnp.float32)

    def leaving(self, buf, bit):
        return pick(buf, 1 - bit).astype(jnp.bfloat16)

    def step(self, buf, out, mask_of, bit, *ties):
        got = after(send_along(self.place, out, mask_of), *ties)
        return pick(buf, bit) + got.astype(jnp.float32)

    def far_step(self, own, scale, *ties):
        far = after(send_along(self.place, own, lambda i: 16), *ties)
        return ((own.astype(jnp.float32) + far.astype(jnp.float32)) * scale).astype(own.dtype)

    def gather_near(self, piece, *ties):
        piece = piece[None]
        return joined(self.near, piece, after(send_along(self.place, piece, near_mask), *ties))

    def gather_second(self, buf, *ties):
        return joined(self.second, buf, after(send_along(self.place, buf, second_mask), *ties))

    def gather_first(self, buf, *ties):
        return joined(self.first, buf, after(send_along(self.place, buf, first_mask), *ties))

    def gather_core(self, buf, *ties):
        return after(send_along(self.place, buf, lambda i: 1), *ties)


def first_half(core, own, axis):
    size = own.shape[axis]
    out = jnp.zeros(own.shape[:axis] + (2 * size,) + own.shape[axis + 1 :], own.dtype)
    return lax.dynamic_update_slice_in_dim(out, own, core * size, axis)


def second_half(core, out, other, axis):
    return lax.dynamic_update_slice_in_dim(out, other, (1 - core) * other.shape[axis], axis)


OVER_ROWS = (((0,), (0,)), ((), ()))
OVER_LANES = (((1,), (1,)), ((), ()))
VMEM_LIMIT = 56 * 1024 * 1024


def dot(left, right, dims=(((1,), (0,)), ((), ()))):
    return lax.dot_general(left, right, dims, preferred_element_type=jnp.float32)


def tiles(count, size, body):
    def step(i, carry):
        body(pl.ds(pl.multiple_of(i * size, size), size))
        return carry

    lax.fori_loop(0, count // size, step, 0)


def started(pairs, sems, first=0):
    copies = [pltpu.make_async_copy(a, b, sems.at[first + i]) for i, (a, b) in enumerate(pairs)]
    for copy in copies:
        copy.start()
    return copies


def finish(copies):
    for copy in copies:
        copy.wait()


def main_kernel(
    core_ref, reach_ref, field, north, south, west, east, corners_west, corners_east, taps_in,
    mix_in, up_in, down_in, cot_in,
    block_out, hg_out, bands_out, mlp_send_out, mlp_keep_out, mix_send_out, mix_keep_out,
    ext, taps, lines, bands, mix, up, down, cot, feats, hidden, act, pre_grad, hg, block, turned, pre_a,
    pre_b, ag_a, ag_b, mlp_send, mlp_keep, mix_send, mix_keep, sems
):
    core = core_ref[0]
    rows, cols, channels = field.shape
    reach = west.shape[1]
    basis = mix.shape[0]
    points = rows * cols
    half_units, half_channels = up.shape[1] // 2, channels // 2
    body, inner = pl.ds(1, rows), pl.ds(reach, cols)
    begin, end = pl.ds(0, reach), pl.ds(reach + cols, reach)
    tap_load = started([(taps_in, taps)], sems, 9)
    loads = started(
        [
            (field, ext.at[body, inner]),
            (west, ext.at[body, begin]),
            (east, ext.at[body, end]),
            (north, ext.at[0, inner]),
            (south, ext.at[rows + 1, inner]),
            (corners_west.at[0], ext.at[0, begin]),
            (corners_west.at[1], ext.at[rows + 1, begin]),
            (corners_east.at[0], ext.at[0, end]),
            (corners_east.at[1], ext.at[rows + 1, end]),
        ],
        sems,
    )
    late = 10
    weights = started([(mix_in, mix), (up_in, up), (down_in, down), (cot_in, cot)], sems, late)
    finish(tap_load)

    count, width = taps.shape[3], lines.shape[3]
    away = jnp.abs(lax.broadcasted_iota(jnp.int32, (3, count), 1) - (count - 1) // 2)
    lines[...] = jnp.zeros(lines.shape, lines.dtype)
    for r in range(rows):
        inside = away <= reach_ref[r]
        for k in range(basis):
            lines[r, k, :, :count] = jnp.where(inside, taps[k, r].astype(jnp.float32), 0.0)
            for d in range(3):
                line = jnp.broadcast_to(lines[r, k, d : d + 1], (cols, width))
                band = pltpu.roll(line, 0, 1, stride=1, stride_axis=0)
                bands[r, k * cols : (k + 1) * cols, d * width : (d + 1) * width] = band.astype(
                    bands.dtype
                )
    stores = started([(bands, bands_out)], sems, late + 12)
    finish(loads)

    for r in range(rows):
        window = ext[r : r + 3].reshape(3 * ext.shape[1], channels)
        out = dot(bands[r], window).astype(feats.dtype)
        at = pl.ds(r * cols, cols)
        for k in range(basis):
            feats[k, at, :] = out[k * cols : (k + 1) * cols]
        hidden[at, :] = ext[r + 1, inner, :]
    finish(weights[:1])

    for i in range(3):
        at = pl.ds(i * (points // 3), points // 3)
        total = hidden[at, :].astype(jnp.float32)
        for k in range(basis):
            total = total + dot(feats[k, at, :], mix[k])
        hidden[at, :] = total.astype(hidden.dtype)
    finish(weights[1:])
    size = pre_a.shape[0]
    slots = ((pre_a, ag_a), (pre_b, ag_b))

    def products(i):
        at = pl.ds(i * size, size)
        pre, ag = slots[i % 2]
        pre[...] = dot(hidden[at, :], up[...])
        ag[...] = dot(cot[at, :], down[...], OVER_LANES)

    def activation(i):
        at = pl.ds(i * size, size)
        pre, ag = slots[i % 2]
        value = pre[...]
        phi = 0.5 * (1.0 + lax.erf(value * inv_root_two))
        act[at, :] = (value * phi).astype(act.dtype)
        slope = phi + value * jnp.exp(-0.5 * value * value) * inv_root_tau
        pre_grad[at, :] = (ag[...] * slope).astype(pre_grad.dtype)

    products(0)
    for i in range(points // size):
        if (i + 1) * size < points:
            products(i + 1)
        activation(i)
    turned[...] = hidden[...].T

    def mlp_sums(half, out):
        at = pl.ds(pl.multiple_of(half * half_units, half_units), half_units)
        out[:half_units] = dot(act[:, at], cot[...], OVER_ROWS).astype(out.dtype)
        out[half_units:] = dot(turned[...], pre_grad[:, at]).astype(out.dtype)

    mlp_sums(1 - core, mlp_send)
    stores += started([(mlp_send, mlp_send_out)], sems, late + 4)
    mlp_sums(core, mlp_keep)
    stores += started([(mlp_keep, mlp_keep_out)], sems, late + 5)

    parts = [pl.ds(i * (points // 3), points // 3) for i in range(3)]
    for at in parts:
        total = cot[at, :].astype(jnp.float32) + dot(pre_grad[at, :], up[...], OVER_LANES)
        hg[at, :] = total.astype(hg.dtype)
    stores += started([(hg, hg_out)], sems, late + 6)

    def mix_sums(half, out):
        at = pl.ds(pl.multiple_of(half * half_channels, half_channels), half_channels)
        for k in range(basis):
            out[k] = dot(feats[k, :, at], hg[...], OVER_ROWS).astype(out.dtype)

    mix_sums(1 - core, mix_send)
    stores += started([(mix_send, mix_send_out)], sems, late + 7)
    mix_sums(core, mix_keep)
    stores += started([(mix_keep, mix_keep_out)], sems, late + 8)

    for i, at in enumerate(parts):
        total = hidden[at, :].astype(jnp.float32) + dot(act[at, :], down[...])
        block[at, :] = total.astype(block.dtype)
        stores += started([(block.at[at], block_out.at[at])], sems, late + 9 + i)
    finish(stores)


def adjoint_kernel(
    hg_in, mix_in, bands_in, inner_out, rim_out, west_out, east_out,
    hg, mix, bands, grads, pulled, inner, sems, *, cols
):
    basis, channels = mix.shape[0], mix.shape[1]
    rows, width = pulled.shape[0] - 2, pulled.shape[1]
    reach = (width - cols) // 2
    loads = started([(hg_in, hg)], sems)
    loads += started([(mix_in.at[k], mix.at[k]) for k in range(basis)], sems, 1)
    late = 1 + basis
    band_loads = started([(bands_in.at[r], bands.at[r]) for r in range(rows)], sems, late)
    pulled[...] = jnp.zeros(pulled.shape, pulled.dtype)
    group = 5 if rows % 5 == 0 else 1
    finish(loads[:1])
    for k in range(basis):
        finish(loads[1 + k : 2 + k])
        for r in range(0, rows, group):
            part = dot(hg[r * cols : (r + group) * cols, :], mix[k], OVER_LANES)
            grads[r : r + group, k * cols : (k + 1) * cols] = part.astype(grads.dtype).reshape(
                group, cols, channels
            )
    stores = []

    def give(row):
        own = hg[(row - 1) * cols : row * cols, :].astype(jnp.float32)
        inner[row - 1] = (pulled[row, reach : reach + cols] + own).astype(inner.dtype)
        copies = [(inner.at[row - 1], inner_out.at[row - 1])]
        stores.extend(started(copies, sems, late + rows + row - 1))

    for r in range(rows):
        finish(band_loads[r : r + 1])
        part = dot(bands[r], grads[r], OVER_ROWS)
        pulled[r : r + 3] += part.reshape(3, width, channels)
        if r:
            give(r)
    give(rows)
    west_out[...] = pulled[:, :reach].astype(west_out.dtype)
    east_out[...] = pulled[:, reach + cols :].astype(east_out.dtype)
    for n, r in enumerate((0, rows + 1)):
        rim_out[n] = pulled[r, reach : reach + cols]
    finish(stores)


def call(kernel, operands, kinds, shapes, out_kinds, scratch, flops, nbytes):
    return pl.pallas_call(
        kernel,
        out_shape=[jax.ShapeDtypeStruct(shape, kind) for shape, kind in shapes],
        in_specs=[pl.BlockSpec(memory_space=kind) for kind in kinds],
        out_specs=[pl.BlockSpec(memory_space=kind) for kind in out_kinds],
        scratch_shapes=scratch,
        compiler_params=pltpu.CompilerParams(vmem_limit_bytes=VMEM_LIMIT),
        cost_estimate=pl.CostEstimate(flops=flops, bytes_accessed=nbytes, transcendentals=0),
    )(*operands)


def local(field_in, kernel_taps, row_reach, mix_weight, up_weight, down_weight, cotangent):
    lat_rows, lon_cols, channels = field_in.shape
    basis_count = kernel_taps.shape[0]
    tap_count = kernel_taps.shape[3]
    reach = (tap_count - 1) // 2
    hidden_units = up_weight.shape[1]
    place = Place()

    top, bottom = field_in[0], field_in[lat_rows - 1]
    inner = lax.ppermute(jnp.where(place.even, bottom, top), AXES, place.pairs)
    outer = lax.ppermute(jnp.where(place.even, top, bottom), AXES, place.bridges)
    west = lax.ppermute(field_in[:, lon_cols - reach :], "lon", place.east)
    east = lax.ppermute(field_in[:, :reach], "lon", place.west)
    north = jnp.where(place.even, outer, inner)
    south = jnp.where(place.even, inner, outer)
    corners = jnp.stack([north[lon_cols - reach :], south[lon_cols - reach :]])
    corners_west = lax.ppermute(corners, "lon", place.east)
    corners = jnp.stack([north[:reach], south[:reach]])
    corners_east = lax.ppermute(corners, "lon", place.west)

    low, full = jnp.bfloat16, jnp.float32
    points = lat_rows * lon_cols
    width = lon_cols + 2 * reach
    vmem, anywhere, smem = pltpu.VMEM, pl.ANY, pltpu.SMEM
    cot = cotangent.reshape(points, channels)
    band_shape = (lat_rows, basis_count * lon_cols, 3 * width)
    gemm = 2 * points * channels * hidden_units
    mix_gemm = 2 * points * channels * channels * basis_count
    band_gemm = 2 * lat_rows * basis_count * lon_cols * 3 * width * channels
    half_units, half_channels = hidden_units // 2, channels // 2
    mlp_half = (half_units + channels, channels)
    mix_half = (basis_count, half_channels, channels)
    big, wide, many = (points, channels), (points, hidden_units), (basis_count, points, channels)
    core = place.flat % 2
    core_op = core[None].astype(jnp.int32)
    sized = (points // 5, hidden_units)
    block_out, hidden_grad, bands, mlp_send, mlp_keep, mix_send, mix_keep = call(
        main_kernel,
        (
            core_op, row_reach, field_in, north, south, west, east, corners_west, corners_east,
            kernel_taps, mix_weight, up_weight, down_weight, cot,
        ),
        [smem] * 2 + [anywhere] * 12,
        [(big, low), (big, low), (band_shape, low), (mlp_half, low), (mlp_half, low), (mix_half, low), (mix_half, low)],
        [anywhere] * 7,
        [
            pltpu.VMEM((lat_rows + 2, width, channels), low),
            pltpu.VMEM(kernel_taps.shape, low),
            pltpu.VMEM((lat_rows, basis_count, 3, width), full),
            pltpu.VMEM(band_shape, low),
            pltpu.VMEM(mix_weight.shape, low),
            pltpu.VMEM(up_weight.shape, low),
            pltpu.VMEM(down_weight.shape, low),
            pltpu.VMEM(big, low),
            pltpu.VMEM(many, low),
            pltpu.VMEM(big, low),
            pltpu.VMEM(wide, low),
            pltpu.VMEM(wide, low),
            pltpu.VMEM(big, low),
            pltpu.VMEM(big, low),
            pltpu.VMEM((channels, points), low),
            pltpu.VMEM(sized, full),
            pltpu.VMEM(sized, full),
            pltpu.VMEM(sized, full),
            pltpu.VMEM(sized, full),
            pltpu.VMEM(mlp_half, low),
            pltpu.VMEM(mlp_half, low),
            pltpu.VMEM(mix_half, low),
            pltpu.VMEM(mix_half, low),
            pltpu.SemaphoreType.DMA((23,)),
        ],
        band_gemm + 2 * mix_gemm + 6 * gemm,
        7 * points * hidden_units * 2,
    )

    def adjoint_of(hidden_grad, *start):
        side = (lat_rows + 2, reach, channels)
        return call(
            functools.partial(adjoint_kernel, cols=lon_cols),
            (after(hidden_grad, *start), mix_weight, bands),
            [anywhere] * 3,
            [
                (field_in.shape, low), ((2, lon_cols, channels), full), (side, low), (side, low),
            ],
            [anywhere] + [vmem] * 3,
            [
                pltpu.VMEM(big, low),
                pltpu.VMEM(mix_weight.shape, low),
                pltpu.VMEM(band_shape, low),
                pltpu.VMEM((lat_rows, basis_count * lon_cols, channels), low),
                pltpu.VMEM((lat_rows + 2, width, channels), full),
                pltpu.VMEM(field_in.shape, low),
                pltpu.SemaphoreType.DMA((1 + basis_count + 2 * lat_rows,)),
            ],
            band_gemm + mix_gemm,
            3 * points * hidden_units * 4,
        )

    def rim_blocks(rims, from_east, from_west):
        corner_east = jnp.stack([from_east[0], from_east[lat_rows + 1]]).astype(full)
        corner_west = jnp.stack([from_west[0], from_west[lat_rows + 1]]).astype(full)
        rims = rims.at[:, lon_cols - reach :].add(corner_east)
        rims = rims.at[:, :reach].add(corner_west).astype(low)
        return jnp.where(place.even, rims[1], rims[0]), jnp.where(place.even, rims[0], rims[1])

    def beyond(near, far):
        near = lax.ppermute(near, AXES, place.pairs)
        far = lax.ppermute(far, AXES, place.bridges)
        return near, far

    def whole_field(inner, from_east, from_west, near, far):
        middle = lon_cols - 2 * reach
        ends = jnp.stack([jnp.where(place.even, far, near), jnp.where(place.even, near, far)])
        ends = ends.astype(full)
        sides = jnp.concatenate(
            [
                from_west[1 : lat_rows + 1].astype(full),
                jnp.zeros((lat_rows, middle, channels), full),
                from_east[1 : lat_rows + 1].astype(full),
            ],
            axis=1,
        )
        nothing = jnp.zeros((lat_rows - 2, lon_cols, channels), full)
        ends = jnp.concatenate([ends[:1], nothing, ends[1:]])
        return (inner.astype(full) + sides + ends).astype(low)

    grad_scale = 1.0 / math.sqrt(points * place.count)
    if place.count == 32:
        ring = Ring(place)
        block_shape = (2, 2, 2, mlp_half[0] // 8, channels)
        mlp = ring.to_core(mlp_keep.reshape(block_shape), mlp_send.reshape(block_shape))
        mlp_out = ring.leaving(mlp, ring.first)
        block_shape = (2, 2, 2, basis_count * half_channels // 8, channels)
        mix = ring.to_core(mix_keep.reshape(block_shape), mix_send.reshape(block_shape))
        mix_out = ring.leaving(mix, ring.first)
        inner, rims, to_west, to_east = adjoint_of(hidden_grad, mlp_out, mix_out)
        from_east = lax.ppermute(to_west, "lon", place.west)
        from_west = lax.ppermute(to_east, "lon", place.east)
        mlp = ring.step(mlp, mlp_out, first_mask, ring.first, to_west)
        mlp_out = ring.leaving(mlp, ring.second)
        mix = ring.step(mix, mix_out, first_mask, ring.first, mlp_out)
        mix_out = ring.leaving(mix, ring.second)
        mlp = ring.step(mlp, mlp_out, second_mask, ring.second, mix_out)
        mlp_out = ring.leaving(mlp, ring.near)
        mix = ring.step(mix, mix_out, second_mask, ring.second, mlp_out)
        mix_out = ring.leaving(mix, ring.near)
        mlp = ring.step(mlp, mlp_out, near_mask, ring.near, mix_out).astype(low)
        mix = ring.step(mix, mix_out, near_mask, ring.near, mlp).astype(low)
        from_east, from_west, _ = lax.optimization_barrier((from_east, from_west, mix))
        top_rim, bottom_rim = rim_blocks(rims, from_east, from_west)
        mlp = ring.far_step(mlp, grad_scale, mix)
        mix = ring.far_step(mix, grad_scale, mlp, top_rim, bottom_rim)
        from_north, from_south = beyond(top_rim, bottom_rim)
        mlp = ring.gather_near(mlp)
        mix = ring.gather_near(mix, mlp)
        from_north, from_south, _ = lax.optimization_barrier((from_north, from_south, mlp))
        mlp = ring.gather_second(mlp, mix, from_north, from_south)
        mix = ring.gather_second(mix, mlp)
        mlp = ring.gather_first(mlp, mix)
        mlp_other = ring.gather_core(mlp)
        grad_field = whole_field(inner, from_east, from_west, from_north, from_south)
        own = mlp.reshape(mlp_half)
        down_out = first_half(core, own[:half_units], 0)
        up_out = first_half(core, own[half_units:], 1)
        got = send_along(place, mix, first_mask)
        got, grad_field, down_out, up_out, _ = lax.optimization_barrier(
            (got, grad_field, down_out, up_out, mlp)
        )
        mix = joined(ring.first, mix, got)
        mix_other = ring.gather_core(mix)
        mix_out = first_half(core, mix.reshape(mix_half), 1)
        mlp_other, mix_out, _ = lax.optimization_barrier((mlp_other, mix_out, mix))
        mlp_other = mlp_other.reshape(mlp_half)
        down_out = second_half(core, down_out, mlp_other[:half_units], 0)
        up_out = second_half(core, up_out, mlp_other[half_units:], 1)
        mix_other, down_out, up_out = lax.optimization_barrier((mix_other, down_out, up_out))
        mix_out = second_half(core, mix_out, mix_other.reshape(mix_half), 1)
    else:
        inner, rims, to_west, to_east = adjoint_of(hidden_grad)
        from_east = lax.ppermute(to_west, "lon", place.west)
        from_west = lax.ppermute(to_east, "lon", place.east)

        rim_pair = rim_blocks(rims, from_east, from_west)
        grad_field = whole_field(inner, from_east, from_west, *beyond(*rim_pair))

        def whole(keep, send):
            keep, send = keep.astype(full)[None], send.astype(full)[None]
            both = jnp.where(core == 0, jnp.concatenate([keep, send]), jnp.concatenate([send, keep]))
            return lax.psum(both, AXES) * grad_scale

        mlp_sum = whole(mlp_keep, mlp_send).astype(low)
        mix_sum = whole(mix_keep, mix_send).astype(low)
        down_out = mlp_sum[:, :half_units].reshape(down_weight.shape)
        up_out = jnp.concatenate([mlp_sum[0, half_units:], mlp_sum[1, half_units:]], axis=1)
        mix_out = mix_sum.swapaxes(0, 1).reshape(mix_weight.shape)

    return (block_out.reshape(field_in.shape), grad_field, mix_out, up_out, down_out)


def solution(mesh):
    placed = (
        P("lat", "lon", None),
        P(None, "lat", None, None),
        P("lat"),
        P(),
        P(),
        P(),
        P("lat", "lon", None),
    )
    return jax.shard_map(
        local,
        mesh=mesh,
        in_specs=placed,
        out_specs=(P("lat", "lon", None), P("lat", "lon", None), P(), P(), P()),
        check_vma=False,
    )
```

```python
import functools
import math

import jax
import jax.numpy as jnp
from jax import lax
from jax.experimental import pallas as pl
from jax.experimental.pallas import tpu as pltpu
from jax.sharding import PartitionSpec as P

inv_root_two = 0.7071067811865476
inv_root_tau = 0.3989422804014327
AXES = ("lat", "lon")


class Place:
    def __init__(self):
        self.lats = lax.axis_size("lat")
        self.lons = lax.axis_size("lon")
        self.count = self.lats * self.lons
        self.lat = lax.axis_index("lat")
        self.lon = lax.axis_index("lon")
        self.flat = self.lat * self.lons + self.lon
        lats, lons = self.lats, self.lons
        self.east = [(i, (i + 1) % lons) for i in range(lons)]
        self.west = [(j, i) for i, j in self.east]
        self.pairs = [
            (r * lons + c, (r ^ 1) * lons + c) for r in range(lats) for c in range(lons)
        ]
        self.bridges = []
        for r in range(lats):
            other = r - 1 if r % 2 == 0 else r + 1
            for c in range(lons):
                if 0 <= other < lats:
                    self.bridges.append((r * lons + c, other * lons + c))
                else:
                    self.bridges.append((r * lons + c, r * lons + (c + lons // 2) % lons))
        self.even = self.lat % 2 == 0


def route(place, mask_of):
    return [(i, i ^ mask_of(i)) for i in range(place.count)]


def send_along(place, block, mask_of):
    return lax.ppermute(block, AXES, route(place, mask_of))


def first_mask(i):
    return 2 if i % 2 == 0 else 4


def second_mask(i):
    return 4 if i % 2 == 0 else 2


def after(value, *others):
    return lax.optimization_barrier((value, *others))[0] if others else value


def near_mask(i):
    return 8


def pick(array, index):
    return lax.dynamic_index_in_dim(array, index, 0, keepdims=False)


def joined(bit, own, other):
    return jnp.concatenate([jnp.where(bit == 0, own, other), jnp.where(bit == 0, other, own)])


class Ring:
    def __init__(self, place):
        self.place = place
        self.core = place.flat % 2
        side_y, side_x = (place.flat // 2) % 2, (place.flat // 4) % 2
        self.first = jnp.where(self.core == 0, side_y, side_x)
        self.second = jnp.where(self.core == 0, side_x, side_y)
        self.near = (place.flat // 8) % 2

    def to_core(self, keep, send):
        return keep, send_along(self.place, send, lambda i: 1)

    def split(self, keep, got):
        leaving, staying = [
            pick(keep, at).astype(jnp.float32) + pick(got, at).astype(jnp.float32)
            for at in (1 - self.first, self.first)
        ]
        return leaving.astype(jnp.bfloat16), staying

    def leaving(self, buf, bit):
        return pick(buf, 1 - bit).astype(jnp.bfloat16)

    def first_step(self, staying, out, *ties):
        return staying + after(send_along(self.place, out, first_mask), *ties).astype(jnp.float32)

    def step(self, buf, out, mask_of, bit, *ties):
        got = after(send_along(self.place, out, mask_of), *ties)
        return pick(buf, bit) + got.astype(jnp.float32)

    def far_step(self, own, scale, *ties):
        far = after(send_along(self.place, own, lambda i: 16), *ties)
        return ((own.astype(jnp.float32) + far.astype(jnp.float32)) * scale).astype(own.dtype)

    def gather_near(self, piece, *ties):
        piece = piece[None]
        return joined(self.near, piece, after(send_along(self.place, piece, near_mask), *ties))

    def gather_second(self, buf, *ties):
        return joined(self.second, buf, after(send_along(self.place, buf, second_mask), *ties))

    def gather_first(self, buf, *ties):
        return joined(self.first, buf, after(send_along(self.place, buf, first_mask), *ties))

    def gather_core(self, buf, *ties):
        return after(send_along(self.place, buf, lambda i: 1), *ties)


def first_half(core, own, axis):
    size = own.shape[axis]
    out = jnp.zeros(own.shape[:axis] + (2 * size,) + own.shape[axis + 1 :], own.dtype)
    return lax.dynamic_update_slice_in_dim(out, own, core * size, axis)


def second_half(core, out, other, axis):
    return lax.dynamic_update_slice_in_dim(out, other, (1 - core) * other.shape[axis], axis)


OVER_ROWS = (((0,), (0,)), ((), ()))
OVER_LANES = (((1,), (1,)), ((), ()))
VMEM_LIMIT = 56 * 1024 * 1024


def dot(left, right, dims=(((1,), (0,)), ((), ()))):
    return lax.dot_general(left, right, dims, preferred_element_type=jnp.float32)


def tiles(count, size, body):
    def step(i, carry):
        body(pl.ds(pl.multiple_of(i * size, size), size))
        return carry

    lax.fori_loop(0, count // size, step, 0)


def started(pairs, sems, first=0):
    copies = [pltpu.make_async_copy(a, b, sems.at[first + i]) for i, (a, b) in enumerate(pairs)]
    for copy in copies:
        copy.start()
    return copies


def finish(copies):
    for copy in copies:
        copy.wait()


def main_kernel(
    core_ref, reach_ref, field, north, south, west, east, corners_west, corners_east, taps_in,
    mix_in, up_in, down_in, cot_in,
    block_out, hg_out, bands_out, mlp_send_out, mlp_keep_out, mix_send_out, mix_keep_out,
    ext, taps, lines, bands, mix, up, down, cot, feats, hidden, act, pre_grad, hg, block, turned, pre_a,
    pre_b, ag_a, ag_b, mlp_send, mlp_keep, mix_send, mix_keep, sems
):
    core = core_ref[0]
    rows, cols, channels = field.shape
    reach = west.shape[1]
    basis = mix.shape[0]
    points = rows * cols
    half_units, half_channels = up.shape[1] // 2, channels // 2
    body, inner = pl.ds(1, rows), pl.ds(reach, cols)
    begin, end = pl.ds(0, reach), pl.ds(reach + cols, reach)
    tap_load = started([(taps_in, taps)], sems, 9)
    loads = started(
        [
            (field, ext.at[body, inner]),
            (west, ext.at[body, begin]),
            (east, ext.at[body, end]),
            (north, ext.at[0, inner]),
            (south, ext.at[rows + 1, inner]),
            (corners_west.at[0], ext.at[0, begin]),
            (corners_west.at[1], ext.at[rows + 1, begin]),
            (corners_east.at[0], ext.at[0, end]),
            (corners_east.at[1], ext.at[rows + 1, end]),
        ],
        sems,
    )
    late = 10
    finish(tap_load)

    count, width = taps.shape[3], lines.shape[3]
    away = jnp.abs(lax.broadcasted_iota(jnp.int32, (3, count), 1) - (count - 1) // 2)
    lines[...] = jnp.zeros(lines.shape, lines.dtype)
    for r in range(rows):
        inside = away <= reach_ref[r]
        for k in range(basis):
            lines[r, k, :, :count] = jnp.where(inside, taps[k, r].astype(jnp.float32), 0.0)
            for d in range(3):
                line = jnp.broadcast_to(lines[r, k, d : d + 1], (cols, width))
                band = pltpu.roll(line, 0, 1, stride=1, stride_axis=0)
                bands[r, k * cols : (k + 1) * cols, d * width : (d + 1) * width] = band.astype(
                    bands.dtype
                )
    finish(loads)
    weights = started([(mix_in, mix), (up_in, up), (down_in, down), (cot_in, cot)], sems, late)

    for r in range(rows):
        window = ext[r : r + 3].reshape(3 * ext.shape[1], channels)
        out = dot(bands[r], window).astype(feats.dtype)
        at = pl.ds(r * cols, cols)
        for k in range(basis):
            feats[k, at, :] = out[k * cols : (k + 1) * cols]
        hidden[at, :] = ext[r + 1, inner, :]
    finish(weights[:1])

    for i in range(3):
        at = pl.ds(i * (points // 3), points // 3)
        total = hidden[at, :].astype(jnp.float32)
        for k in range(basis):
            total = total + dot(feats[k, at, :], mix[k])
        hidden[at, :] = total.astype(hidden.dtype)
    finish(weights[1:])
    size = pre_a.shape[0]
    slots = ((pre_a, ag_a), (pre_b, ag_b))

    def products(i):
        at = pl.ds(i * size, size)
        pre, ag = slots[i % 2]
        pre[...] = dot(hidden[at, :], up[...])
        ag[...] = dot(cot[at, :], down[...], OVER_LANES)

    def activation(i):
        at = pl.ds(i * size, size)
        pre, ag = slots[i % 2]
        value = pre[...]
        phi = 0.5 * (1.0 + lax.erf(value * inv_root_two))
        act[at, :] = (value * phi).astype(act.dtype)
        slope = phi + value * jnp.exp(-0.5 * value * value) * inv_root_tau
        pre_grad[at, :] = (ag[...] * slope).astype(pre_grad.dtype)

    products(0)
    for i in range(points // size):
        if (i + 1) * size < points:
            products(i + 1)
        activation(i)
    turned[...] = hidden[...].T

    def mlp_sums(half, out):
        at = pl.ds(pl.multiple_of(half * half_units, half_units), half_units)
        out[:half_units] = dot(act[:, at], cot[...], OVER_ROWS).astype(out.dtype)
        out[half_units:] = dot(turned[...], pre_grad[:, at]).astype(out.dtype)

    mlp_sums(1 - core, mlp_send)
    stores = started([(mlp_send, mlp_send_out), (bands, bands_out)], sems, late + 4)
    mlp_sums(core, mlp_keep)
    stores += started([(mlp_keep, mlp_keep_out)], sems, late + 6)

    parts = [pl.ds(i * (points // 3), points // 3) for i in range(3)]
    for at in parts:
        total = cot[at, :].astype(jnp.float32) + dot(pre_grad[at, :], up[...], OVER_LANES)
        hg[at, :] = total.astype(hg.dtype)
    stores += started([(hg, hg_out)], sems, late + 7)

    def mix_sums(half, out):
        at = pl.ds(pl.multiple_of(half * half_channels, half_channels), half_channels)
        for k in range(basis):
            out[k] = dot(feats[k, :, at], hg[...], OVER_ROWS).astype(out.dtype)

    mix_sums(1 - core, mix_send)
    stores += started([(mix_send, mix_send_out)], sems, late + 8)
    mix_sums(core, mix_keep)
    stores += started([(mix_keep, mix_keep_out)], sems, late + 9)

    for i, at in enumerate(parts):
        total = hidden[at, :].astype(jnp.float32) + dot(act[at, :], down[...])
        block[at, :] = total.astype(block.dtype)
        stores += started([(block.at[at], block_out.at[at])], sems, late + 10 + i)
    finish(stores)


def adjoint_kernel(
    hg_in, mix_in, bands_in, inner_out, rim_out, west_out, east_out,
    hg, mix, bands, grads, pulled, inner, sems, *, cols
):
    basis, channels = mix.shape[0], mix.shape[1]
    rows, width = pulled.shape[0] - 2, pulled.shape[1]
    reach = (width - cols) // 2
    loads = started([(hg_in, hg)], sems)
    loads += started([(mix_in.at[k], mix.at[k]) for k in range(basis)], sems, 1)
    late = 1 + basis
    band_loads = started([(bands_in.at[r], bands.at[r]) for r in range(rows)], sems, late)
    pulled[...] = jnp.zeros(pulled.shape, pulled.dtype)
    group = 5 if rows % 5 == 0 else 1
    finish(loads[:1])
    for k in range(basis):
        finish(loads[1 + k : 2 + k])
        for r in range(0, rows, group):
            part = dot(hg[r * cols : (r + group) * cols, :], mix[k], OVER_LANES)
            grads[r : r + group, k * cols : (k + 1) * cols] = part.astype(grads.dtype).reshape(
                group, cols, channels
            )
    stores = []

    def give(row):
        own = hg[(row - 1) * cols : row * cols, :].astype(jnp.float32)
        inner[row - 1] = (pulled[row, reach : reach + cols] + own).astype(inner.dtype)
        copies = [(inner.at[row - 1], inner_out.at[row - 1])]
        stores.extend(started(copies, sems, late + rows + row - 1))

    for r in range(rows):
        finish(band_loads[r : r + 1])
        part = dot(bands[r], grads[r], OVER_ROWS)
        pulled[r : r + 3] += part.reshape(3, width, channels)
        if r:
            give(r)
    give(rows)
    west_out[...] = pulled[:, :reach].astype(west_out.dtype)
    east_out[...] = pulled[:, reach + cols :].astype(east_out.dtype)
    for n, r in enumerate((0, rows + 1)):
        rim_out[n] = pulled[r, reach : reach + cols]
    finish(stores)


def call(kernel, operands, kinds, shapes, out_kinds, scratch, flops, nbytes):
    return pl.pallas_call(
        kernel,
        out_shape=[jax.ShapeDtypeStruct(shape, kind) for shape, kind in shapes],
        in_specs=[pl.BlockSpec(memory_space=kind) for kind in kinds],
        out_specs=[pl.BlockSpec(memory_space=kind) for kind in out_kinds],
        scratch_shapes=scratch,
        compiler_params=pltpu.CompilerParams(vmem_limit_bytes=VMEM_LIMIT),
        cost_estimate=pl.CostEstimate(flops=flops, bytes_accessed=nbytes, transcendentals=0),
    )(*operands)


def local(field_in, kernel_taps, row_reach, mix_weight, up_weight, down_weight, cotangent):
    lat_rows, lon_cols, channels = field_in.shape
    basis_count = kernel_taps.shape[0]
    tap_count = kernel_taps.shape[3]
    reach = (tap_count - 1) // 2
    hidden_units = up_weight.shape[1]
    place = Place()

    west = lax.ppermute(field_in[:, lon_cols - reach :], "lon", place.east)
    east = lax.ppermute(field_in[:, :reach], "lon", place.west)
    top, bottom = field_in[0], field_in[lat_rows - 1]
    inner = lax.ppermute(jnp.where(place.even, bottom, top), AXES, place.pairs)
    outer = lax.ppermute(jnp.where(place.even, top, bottom), AXES, place.bridges)
    inner, outer, west, east = lax.optimization_barrier((inner, outer, west, east))
    north = jnp.where(place.even, outer, inner)
    south = jnp.where(place.even, inner, outer)
    corners = jnp.stack([north[lon_cols - reach :], south[lon_cols - reach :]])
    corners_west = lax.ppermute(corners, "lon", place.east)
    corners = jnp.stack([north[:reach], south[:reach]])
    corners_east = lax.ppermute(corners, "lon", place.west)

    low, full = jnp.bfloat16, jnp.float32
    points = lat_rows * lon_cols
    width = lon_cols + 2 * reach
    vmem, anywhere, smem = pltpu.VMEM, pl.ANY, pltpu.SMEM
    cot = cotangent.reshape(points, channels)
    band_shape = (lat_rows, basis_count * lon_cols, 3 * width)
    gemm = 2 * points * channels * hidden_units
    mix_gemm = 2 * points * channels * channels * basis_count
    band_gemm = 2 * lat_rows * basis_count * lon_cols * 3 * width * channels
    half_units, half_channels = hidden_units // 2, channels // 2
    mlp_half = (half_units + channels, channels)
    mix_half = (basis_count, half_channels, channels)
    big, wide, many = (points, channels), (points, hidden_units), (basis_count, points, channels)
    core = place.flat % 2
    core_op = core[None].astype(jnp.int32)
    sized = (points // 5, hidden_units)
    block_out, hidden_grad, bands, mlp_send, mlp_keep, mix_send, mix_keep = call(
        main_kernel,
        (
            core_op, row_reach, field_in, north, south, west, east, corners_west, corners_east,
            kernel_taps, mix_weight, up_weight, down_weight, cot,
        ),
        [smem] * 2 + [anywhere] * 12,
        [(big, low), (big, low), (band_shape, low), (mlp_half, low), (mlp_half, low), (mix_half, low), (mix_half, low)],
        [anywhere] * 7,
        [
            pltpu.VMEM((lat_rows + 2, width, channels), low),
            pltpu.VMEM(kernel_taps.shape, low),
            pltpu.VMEM((lat_rows, basis_count, 3, width), full),
            pltpu.VMEM(band_shape, low),
            pltpu.VMEM(mix_weight.shape, low),
            pltpu.VMEM(up_weight.shape, low),
            pltpu.VMEM(down_weight.shape, low),
            pltpu.VMEM(big, low),
            pltpu.VMEM(many, low),
            pltpu.VMEM(big, low),
            pltpu.VMEM(wide, low),
            pltpu.VMEM(wide, low),
            pltpu.VMEM(big, low),
            pltpu.VMEM(big, low),
            pltpu.VMEM((channels, points), low),
            pltpu.VMEM(sized, full),
            pltpu.VMEM(sized, full),
            pltpu.VMEM(sized, full),
            pltpu.VMEM(sized, full),
            pltpu.VMEM(mlp_half, low),
            pltpu.VMEM(mlp_half, low),
            pltpu.VMEM(mix_half, low),
            pltpu.VMEM(mix_half, low),
            pltpu.SemaphoreType.DMA((23,)),
        ],
        band_gemm + 2 * mix_gemm + 6 * gemm,
        7 * points * hidden_units * 2,
    )

    def adjoint_of(hidden_grad, *start):
        side = (lat_rows + 2, reach, channels)
        return call(
            functools.partial(adjoint_kernel, cols=lon_cols),
            (after(hidden_grad, *start), mix_weight, bands),
            [anywhere] * 3,
            [
                (field_in.shape, low), ((2, lon_cols, channels), full), (side, low), (side, low),
            ],
            [anywhere] + [vmem] * 3,
            [
                pltpu.VMEM(big, low),
                pltpu.VMEM(mix_weight.shape, low),
                pltpu.VMEM(band_shape, low),
                pltpu.VMEM((lat_rows, basis_count * lon_cols, channels), low),
                pltpu.VMEM((lat_rows + 2, width, channels), full),
                pltpu.VMEM(field_in.shape, low),
                pltpu.SemaphoreType.DMA((1 + basis_count + 2 * lat_rows,)),
            ],
            band_gemm + mix_gemm,
            3 * points * hidden_units * 4,
        )

    def rim_blocks(rims, from_east, from_west):
        corner_east = jnp.stack([from_east[0], from_east[lat_rows + 1]]).astype(full)
        corner_west = jnp.stack([from_west[0], from_west[lat_rows + 1]]).astype(full)
        rims = rims.at[:, lon_cols - reach :].add(corner_east)
        rims = rims.at[:, :reach].add(corner_west).astype(low)
        return jnp.where(place.even, rims[1], rims[0]), jnp.where(place.even, rims[0], rims[1])

    def beyond(near, far):
        near = lax.ppermute(near, AXES, place.pairs)
        far = lax.ppermute(far, AXES, place.bridges)
        return near, far

    def whole_field(inner, from_east, from_west, near, far):
        middle = lon_cols - 2 * reach
        ends = jnp.stack([jnp.where(place.even, far, near), jnp.where(place.even, near, far)])
        ends = ends.astype(full)
        sides = jnp.concatenate(
            [
                from_west[1 : lat_rows + 1].astype(full),
                jnp.zeros((lat_rows, middle, channels), full),
                from_east[1 : lat_rows + 1].astype(full),
            ],
            axis=1,
        )
        nothing = jnp.zeros((lat_rows - 2, lon_cols, channels), full)
        ends = jnp.concatenate([ends[:1], nothing, ends[1:]])
        return (inner.astype(full) + sides + ends).astype(low)

    grad_scale = 1.0 / math.sqrt(points * place.count)
    if place.count == 32:
        ring = Ring(place)
        block_shape = (2, 2, 2, mlp_half[0] // 8, channels)
        mlp = ring.to_core(mlp_keep.reshape(block_shape), mlp_send.reshape(block_shape))
        mlp_out, mlp = ring.split(*mlp)
        block_shape = (2, 2, 2, basis_count * half_channels // 8, channels)
        mix = ring.to_core(mix_keep.reshape(block_shape), mix_send.reshape(block_shape))
        mix_out, mix = ring.split(*mix)
        inner, rims, to_west, to_east = adjoint_of(hidden_grad, mlp_out, mix_out)
        from_east = lax.ppermute(to_west, "lon", place.west)
        from_west = lax.ppermute(to_east, "lon", place.east)
        mlp = ring.first_step(mlp, mlp_out, to_west)
        mlp_out = ring.leaving(mlp, ring.second)
        mix = ring.first_step(mix, mix_out, mlp_out)
        mix_out = ring.leaving(mix, ring.second)
        mlp = ring.step(mlp, mlp_out, second_mask, ring.second, mix_out)
        mlp_out = ring.leaving(mlp, ring.near)
        mix = ring.step(mix, mix_out, second_mask, ring.second, mlp_out)
        mix_out = ring.leaving(mix, ring.near)
        mlp = ring.step(mlp, mlp_out, near_mask, ring.near, mix_out).astype(low)
        mix = ring.step(mix, mix_out, near_mask, ring.near, mlp).astype(low)
        from_east, from_west, _ = lax.optimization_barrier((from_east, from_west, mix))
        top_rim, bottom_rim = rim_blocks(rims, from_east, from_west)
        mlp = ring.far_step(mlp, grad_scale, mix)
        mix = ring.far_step(mix, grad_scale, mlp, top_rim, bottom_rim)
        from_north, from_south = beyond(top_rim, bottom_rim)
        mlp = ring.gather_near(mlp)
        mix = ring.gather_near(mix, mlp)
        from_north, from_south, _ = lax.optimization_barrier((from_north, from_south, mlp))
        mlp = ring.gather_second(mlp, mix, from_north, from_south)
        mix = ring.gather_second(mix, mlp)
        mlp = ring.gather_first(mlp, mix)
        mlp_other = ring.gather_core(mlp)
        grad_field = whole_field(inner, from_east, from_west, from_north, from_south)
        own = mlp.reshape(mlp_half)
        down_out = first_half(core, own[:half_units], 0)
        up_out = first_half(core, own[half_units:], 1)
        got = send_along(place, mix, first_mask)
        got, grad_field, down_out, up_out, _ = lax.optimization_barrier(
            (got, grad_field, down_out, up_out, mlp)
        )
        mix = joined(ring.first, mix, got)
        mix_other = ring.gather_core(mix)
        mix_out = first_half(core, mix.reshape(mix_half), 1)
        mlp_other, mix_out, _ = lax.optimization_barrier((mlp_other, mix_out, mix))
        mlp_other = mlp_other.reshape(mlp_half)
        down_out = second_half(core, down_out, mlp_other[:half_units], 0)
        up_out = second_half(core, up_out, mlp_other[half_units:], 1)
        mix_other, down_out, up_out = lax.optimization_barrier((mix_other, down_out, up_out))
        mix_out = second_half(core, mix_out, mix_other.reshape(mix_half), 1)
    else:
        inner, rims, to_west, to_east = adjoint_of(hidden_grad)
        from_east = lax.ppermute(to_west, "lon", place.west)
        from_west = lax.ppermute(to_east, "lon", place.east)

        rim_pair = rim_blocks(rims, from_east, from_west)
        grad_field = whole_field(inner, from_east, from_west, *beyond(*rim_pair))

        def whole(keep, send):
            keep, send = keep.astype(full)[None], send.astype(full)[None]
            both = jnp.where(core == 0, jnp.concatenate([keep, send]), jnp.concatenate([send, keep]))
            return lax.psum(both, AXES) * grad_scale

        mlp_sum = whole(mlp_keep, mlp_send).astype(low)
        mix_sum = whole(mix_keep, mix_send).astype(low)
        down_out = mlp_sum[:, :half_units].reshape(down_weight.shape)
        up_out = jnp.concatenate([mlp_sum[0, half_units:], mlp_sum[1, half_units:]], axis=1)
        mix_out = mix_sum.swapaxes(0, 1).reshape(mix_weight.shape)

    return (block_out.reshape(field_in.shape), grad_field, mix_out, up_out, down_out)


def solution(mesh):
    placed = (
        P("lat", "lon", None),
        P(None, "lat", None, None),
        P("lat"),
        P(),
        P(),
        P(),
        P("lat", "lon", None),
    )
    return jax.shard_map(
        local,
        mesh=mesh,
        in_specs=placed,
        out_specs=(P("lat", "lon", None), P("lat", "lon", None), P(), P(), P()),
        check_vma=False,
    )
```

```python
import functools
import math

import jax
import jax.numpy as jnp
from jax import lax
from jax.experimental import pallas as pl
from jax.experimental.pallas import tpu as pltpu
from jax.sharding import PartitionSpec as P

inv_root_two = 0.7071067811865476
inv_root_tau = 0.3989422804014327
AXES = ("lat", "lon")


class Place:
    def __init__(self):
        self.lats = lax.axis_size("lat")
        self.lons = lax.axis_size("lon")
        self.count = self.lats * self.lons
        self.lat = lax.axis_index("lat")
        self.lon = lax.axis_index("lon")
        self.flat = self.lat * self.lons + self.lon
        lats, lons = self.lats, self.lons
        self.east = [(i, (i + 1) % lons) for i in range(lons)]
        self.west = [(j, i) for i, j in self.east]
        self.pairs = [
            (r * lons + c, (r ^ 1) * lons + c) for r in range(lats) for c in range(lons)
        ]
        self.bridges = []
        for r in range(lats):
            other = r - 1 if r % 2 == 0 else r + 1
            for c in range(lons):
                if 0 <= other < lats:
                    self.bridges.append((r * lons + c, other * lons + c))
                else:
                    self.bridges.append((r * lons + c, r * lons + (c + lons // 2) % lons))
        self.even = self.lat % 2 == 0


def route(place, mask_of):
    return [(i, i ^ mask_of(i)) for i in range(place.count)]


def send_along(place, block, mask_of):
    return lax.ppermute(block, AXES, route(place, mask_of))


def first_mask(i):
    return 2 if i % 2 == 0 else 4


def second_mask(i):
    return 4 if i % 2 == 0 else 2


def after(value, *others):
    return lax.optimization_barrier((value, *others))[0] if others else value


def near_mask(i):
    return 8


def pick(array, index):
    return lax.dynamic_index_in_dim(array, index, 0, keepdims=False)


def joined(bit, own, other):
    return jnp.concatenate([jnp.where(bit == 0, own, other), jnp.where(bit == 0, other, own)])


class Ring:
    def __init__(self, place):
        self.place = place
        self.core = place.flat % 2
        side_y, side_x = (place.flat // 2) % 2, (place.flat // 4) % 2
        self.first = jnp.where(self.core == 0, side_y, side_x)
        self.second = jnp.where(self.core == 0, side_x, side_y)
        self.near = (place.flat // 8) % 2

    def to_core(self, keep, send):
        got = send_along(self.place, send, lambda i: 1)
        return keep.astype(jnp.float32) + got.astype(jnp.float32)

    def leaving(self, buf, bit):
        return pick(buf, 1 - bit).astype(jnp.bfloat16)

    def step(self, buf, out, mask_of, bit, *ties):
        got = after(send_along(self.place, out, mask_of), *ties)
        return pick(buf, bit) + got.astype(jnp.float32)

    def far_step(self, own, scale, *ties):
        far = after(send_along(self.place, own, lambda i: 16), *ties)
        return ((own.astype(jnp.float32) + far.astype(jnp.float32)) * scale).astype(own.dtype)

    def gather_near(self, buf, *ties):
        return joined(self.near, buf, after(send_along(self.place, buf, near_mask), *ties))

    def gather_second(self, buf, *ties):
        return joined(self.second, buf, after(send_along(self.place, buf, second_mask), *ties))

    def gather_first(self, buf, *ties):
        return joined(self.first, buf, after(send_along(self.place, buf, first_mask), *ties))

    def gather_core(self, buf, *ties):
        return after(send_along(self.place, buf, lambda i: 1), *ties)


def first_half(core, own, axis):
    size = own.shape[axis]
    out = jnp.zeros(own.shape[:axis] + (2 * size,) + own.shape[axis + 1 :], own.dtype)
    return lax.dynamic_update_slice_in_dim(out, own, core * size, axis)


def second_half(core, out, other, axis):
    return lax.dynamic_update_slice_in_dim(out, other, (1 - core) * other.shape[axis], axis)


OVER_ROWS = (((0,), (0,)), ((), ()))
OVER_LANES = (((1,), (1,)), ((), ()))
VMEM_LIMIT = 56 * 1024 * 1024


def dot(left, right, dims=(((1,), (0,)), ((), ()))):
    return lax.dot_general(left, right, dims, preferred_element_type=jnp.float32)


def tiles(count, size, body):
    def step(i, carry):
        body(pl.ds(pl.multiple_of(i * size, size), size))
        return carry

    lax.fori_loop(0, count // size, step, 0)


def started(pairs, sems, first=0):
    copies = [pltpu.make_async_copy(a, b, sems.at[first + i]) for i, (a, b) in enumerate(pairs)]
    for copy in copies:
        copy.start()
    return copies


def finish(copies):
    for copy in copies:
        copy.wait()


def main_kernel(
    core_ref, reach_ref, field, north, south, west, east, corners_west, corners_east, taps_in,
    mix_in, up_in, down_in, cot_in,
    block_out, hg_out, bands_out, mlp_send_out, mlp_keep_out, mix_send_out, mix_keep_out,
    ext, taps, lines, bands, mix, up, down, cot, feats, hidden, act, pre_grad, hg, block, turned, pre_a,
    pre_b, ag_a, ag_b, mlp_send, mlp_keep, mix_send, mix_keep, sems
):
    core = core_ref[0]
    rows, cols, channels = field.shape
    reach = west.shape[1]
    basis = mix.shape[0]
    points = rows * cols
    half_units, half_channels = up.shape[1] // 2, channels // 2
    body, inner = pl.ds(1, rows), pl.ds(reach, cols)
    begin, end = pl.ds(0, reach), pl.ds(reach + cols, reach)
    tap_load = started([(taps_in, taps)], sems, 9)
    loads = started(
        [
            (field, ext.at[body, inner]),
            (west, ext.at[body, begin]),
            (east, ext.at[body, end]),
            (north, ext.at[0, inner]),
            (south, ext.at[rows + 1, inner]),
            (corners_west.at[0], ext.at[0, begin]),
            (corners_west.at[1], ext.at[rows + 1, begin]),
            (corners_east.at[0], ext.at[0, end]),
            (corners_east.at[1], ext.at[rows + 1, end]),
        ],
        sems,
    )
    late = 10
    weights = started([(mix_in, mix), (up_in, up), (down_in, down), (cot_in, cot)], sems, late)
    finish(tap_load)

    count, width = taps.shape[3], lines.shape[3]
    away = jnp.abs(lax.broadcasted_iota(jnp.int32, (3, count), 1) - (count - 1) // 2)
    lines[...] = jnp.zeros(lines.shape, lines.dtype)
    for r in range(rows):
        inside = away <= reach_ref[r]
        for k in range(basis):
            lines[r, k, :, :count] = jnp.where(inside, taps[k, r].astype(jnp.float32), 0.0)
            for d in range(3):
                line = jnp.broadcast_to(lines[r, k, d : d + 1], (cols, width))
                band = pltpu.roll(line, 0, 1, stride=1, stride_axis=0)
                bands[r, k * cols : (k + 1) * cols, d * width : (d + 1) * width] = band.astype(
                    bands.dtype
                )
    stores = started([(bands, bands_out)], sems, late + 12)
    finish(loads)

    for r in range(rows):
        window = ext[r : r + 3].reshape(3 * ext.shape[1], channels)
        out = dot(bands[r], window).astype(feats.dtype)
        at = pl.ds(r * cols, cols)
        for k in range(basis):
            feats[k, at, :] = out[k * cols : (k + 1) * cols]
        hidden[at, :] = ext[r + 1, inner, :]
    finish(weights[:1])

    for i in range(3):
        at = pl.ds(i * (points // 3), points // 3)
        total = hidden[at, :].astype(jnp.float32)
        for k in range(basis):
            total = total + dot(feats[k, at, :], mix[k])
        hidden[at, :] = total.astype(hidden.dtype)
    finish(weights[1:])
    size = pre_a.shape[0]
    slots = ((pre_a, ag_a), (pre_b, ag_b))

    def products(i):
        at = pl.ds(i * size, size)
        pre, ag = slots[i % 2]
        pre[...] = dot(hidden[at, :], up[...])
        ag[...] = dot(cot[at, :], down[...], OVER_LANES)

    def activation(i):
        at = pl.ds(i * size, size)
        pre, ag = slots[i % 2]
        value = pre[...]
        phi = 0.5 * (1.0 + lax.erf(value * inv_root_two))
        act[at, :] = (value * phi).astype(act.dtype)
        slope = phi + value * jnp.exp(-0.5 * value * value) * inv_root_tau
        pre_grad[at, :] = (ag[...] * slope).astype(pre_grad.dtype)

    products(0)
    for i in range(points // size):
        if (i + 1) * size < points:
            products(i + 1)
        activation(i)
    turned[...] = hidden[...].T

    def mlp_sums(half, out):
        at = pl.ds(pl.multiple_of(half * half_units, half_units), half_units)
        out[:half_units] = dot(act[:, at], cot[...], OVER_ROWS).astype(out.dtype)
        out[half_units:] = dot(turned[...], pre_grad[:, at]).astype(out.dtype)

    mlp_sums(1 - core, mlp_send)
    stores += started([(mlp_send, mlp_send_out)], sems, late + 4)
    mlp_sums(core, mlp_keep)
    stores += started([(mlp_keep, mlp_keep_out)], sems, late + 5)

    parts = [pl.ds(i * (points // 3), points // 3) for i in range(3)]
    for at in parts:
        total = cot[at, :].astype(jnp.float32) + dot(pre_grad[at, :], up[...], OVER_LANES)
        hg[at, :] = total.astype(hg.dtype)
    stores += started([(hg, hg_out)], sems, late + 6)

    def mix_sums(half, out):
        at = pl.ds(pl.multiple_of(half * half_channels, half_channels), half_channels)
        for k in range(basis):
            out[k] = dot(feats[k, :, at], hg[...], OVER_ROWS).astype(out.dtype)

    mix_sums(1 - core, mix_send)
    stores += started([(mix_send, mix_send_out)], sems, late + 7)
    mix_sums(core, mix_keep)
    stores += started([(mix_keep, mix_keep_out)], sems, late + 8)

    for i, at in enumerate(parts):
        total = hidden[at, :].astype(jnp.float32) + dot(act[at, :], down[...])
        block[at, :] = total.astype(block.dtype)
        stores += started([(block.at[at], block_out.at[at])], sems, late + 9 + i)
    finish(stores)


def adjoint_kernel(
    hg_in, mix_in, bands_in, inner_out, rim_out, west_out, east_out,
    hg, mix, bands, grads, pulled, inner, sems, *, cols
):
    basis, channels = mix.shape[0], mix.shape[1]
    rows, width = pulled.shape[0] - 2, pulled.shape[1]
    reach = (width - cols) // 2
    loads = started([(hg_in, hg)], sems)
    loads += started([(mix_in.at[k], mix.at[k]) for k in range(basis)], sems, 1)
    late = 1 + basis
    band_loads = started([(bands_in.at[r], bands.at[r]) for r in range(rows)], sems, late)
    pulled[...] = jnp.zeros(pulled.shape, pulled.dtype)
    group = 5 if rows % 5 == 0 else 1
    finish(loads[:1])
    for k in range(basis):
        finish(loads[1 + k : 2 + k])
        for r in range(0, rows, group):
            part = dot(hg[r * cols : (r + group) * cols, :], mix[k], OVER_LANES)
            grads[r : r + group, k * cols : (k + 1) * cols] = part.astype(grads.dtype).reshape(
                group, cols, channels
            )
    stores = []

    def give(row):
        own = hg[(row - 1) * cols : row * cols, :].astype(jnp.float32)
        inner[row - 1] = (pulled[row, reach : reach + cols] + own).astype(inner.dtype)
        copies = [(inner.at[row - 1], inner_out.at[row - 1])]
        stores.extend(started(copies, sems, late + rows + row - 1))

    for r in range(rows):
        finish(band_loads[r : r + 1])
        part = dot(bands[r], grads[r], OVER_ROWS)
        pulled[r : r + 3] += part.reshape(3, width, channels)
        if r:
            give(r)
    give(rows)
    west_out[...] = pulled[:, :reach].astype(west_out.dtype)
    east_out[...] = pulled[:, reach + cols :].astype(east_out.dtype)
    for n, r in enumerate((0, rows + 1)):
        rim_out[n] = pulled[r, reach : reach + cols]
    finish(stores)


def call(kernel, operands, kinds, shapes, out_kinds, scratch, flops, nbytes):
    return pl.pallas_call(
        kernel,
        out_shape=[jax.ShapeDtypeStruct(shape, kind) for shape, kind in shapes],
        in_specs=[pl.BlockSpec(memory_space=kind) for kind in kinds],
        out_specs=[pl.BlockSpec(memory_space=kind) for kind in out_kinds],
        scratch_shapes=scratch,
        compiler_params=pltpu.CompilerParams(vmem_limit_bytes=VMEM_LIMIT),
        cost_estimate=pl.CostEstimate(flops=flops, bytes_accessed=nbytes, transcendentals=0),
    )(*operands)


def local(field_in, kernel_taps, row_reach, mix_weight, up_weight, down_weight, cotangent):
    lat_rows, lon_cols, channels = field_in.shape
    basis_count = kernel_taps.shape[0]
    tap_count = kernel_taps.shape[3]
    reach = (tap_count - 1) // 2
    hidden_units = up_weight.shape[1]
    place = Place()

    top, bottom = field_in[0], field_in[lat_rows - 1]
    inner = lax.ppermute(jnp.where(place.even, bottom, top), AXES, place.pairs)
    outer = lax.ppermute(jnp.where(place.even, top, bottom), AXES, place.bridges)
    west = lax.ppermute(field_in[:, lon_cols - reach :], "lon", place.east)
    east = lax.ppermute(field_in[:, :reach], "lon", place.west)
    north = jnp.where(place.even, outer, inner)
    south = jnp.where(place.even, inner, outer)
    corners = jnp.stack([north[lon_cols - reach :], south[lon_cols - reach :]])
    corners_west = lax.ppermute(corners, "lon", place.east)
    corners = jnp.stack([north[:reach], south[:reach]])
    corners_east = lax.ppermute(corners, "lon", place.west)

    low, full = jnp.bfloat16, jnp.float32
    points = lat_rows * lon_cols
    width = lon_cols + 2 * reach
    vmem, anywhere, smem = pltpu.VMEM, pl.ANY, pltpu.SMEM
    cot = cotangent.reshape(points, channels)
    band_shape = (lat_rows, basis_count * lon_cols, 3 * width)
    gemm = 2 * points * channels * hidden_units
    mix_gemm = 2 * points * channels * channels * basis_count
    band_gemm = 2 * lat_rows * basis_count * lon_cols * 3 * width * channels
    half_units, half_channels = hidden_units // 2, channels // 2
    mlp_half = (half_units + channels, channels)
    mix_half = (basis_count, half_channels, channels)
    big, wide, many = (points, channels), (points, hidden_units), (basis_count, points, channels)
    core = place.flat % 2
    core_op = core[None].astype(jnp.int32)
    sized = (points // 5, hidden_units)
    block_out, hidden_grad, bands, mlp_send, mlp_keep, mix_send, mix_keep = call(
        main_kernel,
        (
            core_op, row_reach, field_in, north, south, west, east, corners_west, corners_east,
            kernel_taps, mix_weight, up_weight, down_weight, cot,
        ),
        [smem] * 2 + [anywhere] * 12,
        [(big, low), (big, low), (band_shape, low), (mlp_half, low), (mlp_half, low), (mix_half, low), (mix_half, low)],
        [anywhere] * 7,
        [
            pltpu.VMEM((lat_rows + 2, width, channels), low),
            pltpu.VMEM(kernel_taps.shape, low),
            pltpu.VMEM((lat_rows, basis_count, 3, width), full),
            pltpu.VMEM(band_shape, low),
            pltpu.VMEM(mix_weight.shape, low),
            pltpu.VMEM(up_weight.shape, low),
            pltpu.VMEM(down_weight.shape, low),
            pltpu.VMEM(big, low),
            pltpu.VMEM(many, low),
            pltpu.VMEM(big, low),
            pltpu.VMEM(wide, low),
            pltpu.VMEM(wide, low),
            pltpu.VMEM(big, low),
            pltpu.VMEM(big, low),
            pltpu.VMEM((channels, points), low),
            pltpu.VMEM(sized, full),
            pltpu.VMEM(sized, full),
            pltpu.VMEM(sized, full),
            pltpu.VMEM(sized, full),
            pltpu.VMEM(mlp_half, low),
            pltpu.VMEM(mlp_half, low),
            pltpu.VMEM(mix_half, low),
            pltpu.VMEM(mix_half, low),
            pltpu.SemaphoreType.DMA((23,)),
        ],
        band_gemm + 2 * mix_gemm + 6 * gemm,
        7 * points * hidden_units * 2,
    )

    def adjoint_of(hidden_grad, *start):
        side = (lat_rows + 2, reach, channels)
        return call(
            functools.partial(adjoint_kernel, cols=lon_cols),
            (after(hidden_grad, *start), mix_weight, bands),
            [anywhere] * 3,
            [
                (field_in.shape, low), ((2, lon_cols, channels), full), (side, low), (side, low),
            ],
            [anywhere] + [vmem] * 3,
            [
                pltpu.VMEM(big, low),
                pltpu.VMEM(mix_weight.shape, low),
                pltpu.VMEM(band_shape, low),
                pltpu.VMEM((lat_rows, basis_count * lon_cols, channels), low),
                pltpu.VMEM((lat_rows + 2, width, channels), full),
                pltpu.VMEM(field_in.shape, low),
                pltpu.SemaphoreType.DMA((1 + basis_count + 2 * lat_rows,)),
            ],
            band_gemm + mix_gemm,
            3 * points * hidden_units * 4,
        )

    def rim_blocks(rims, from_east, from_west):
        corner_east = jnp.stack([from_east[0], from_east[lat_rows + 1]]).astype(full)
        corner_west = jnp.stack([from_west[0], from_west[lat_rows + 1]]).astype(full)
        rims = rims.at[:, lon_cols - reach :].add(corner_east)
        rims = rims.at[:, :reach].add(corner_west).astype(low)
        return jnp.where(place.even, rims[1], rims[0]), jnp.where(place.even, rims[0], rims[1])

    def beyond(near, far):
        near = lax.ppermute(near, AXES, place.pairs)
        far = lax.ppermute(far, AXES, place.bridges)
        return near, far

    def whole_field(inner, from_east, from_west, near, far):
        middle = lon_cols - 2 * reach
        ends = jnp.stack([jnp.where(place.even, far, near), jnp.where(place.even, near, far)])
        ends = ends.astype(full)
        sides = jnp.concatenate(
            [
                from_west[1 : lat_rows + 1].astype(full),
                jnp.zeros((lat_rows, middle, channels), full),
                from_east[1 : lat_rows + 1].astype(full),
            ],
            axis=1,
        )
        nothing = jnp.zeros((lat_rows - 2, lon_cols, channels), full)
        ends = jnp.concatenate([ends[:1], nothing, ends[1:]])
        return (inner.astype(full) + sides + ends).astype(low)

    grad_scale = 1.0 / math.sqrt(points * place.count)
    if place.count == 32:
        ring = Ring(place)
        block_shape = (2, 2, 2, mlp_half[0] // 8, channels)
        mlp = ring.to_core(mlp_keep.reshape(block_shape), mlp_send.reshape(block_shape))
        mlp_out = ring.leaving(mlp, ring.first)
        block_shape = (2, 2, 2, basis_count * half_channels // 8, channels)
        mix = ring.to_core(mix_keep.reshape(block_shape), mix_send.reshape(block_shape))
        mix_out = ring.leaving(mix, ring.first)
        inner, rims, to_west, to_east = adjoint_of(hidden_grad, mlp_out, mix_out)
        from_east = lax.ppermute(to_west, "lon", place.west)
        from_west = lax.ppermute(to_east, "lon", place.east)
        mlp = ring.step(mlp, mlp_out, first_mask, ring.first, to_west)
        mlp_out = ring.leaving(mlp, ring.second)
        mix = ring.step(mix, mix_out, first_mask, ring.first, mlp_out)
        mix_out = ring.leaving(mix, ring.near)
        mlp = ring.step(mlp, mlp_out, second_mask, ring.second, mix_out)
        mlp_out = ring.leaving(mlp, ring.near)
        mix = ring.step(mix, mix_out, near_mask, ring.near, mlp_out)
        mix_out = ring.leaving(mix, ring.second)
        mlp = ring.step(mlp, mlp_out, near_mask, ring.near, mix_out).astype(low)
        mix = ring.step(mix, mix_out, second_mask, ring.second, mlp).astype(low)
        from_east, from_west, _ = lax.optimization_barrier((from_east, from_west, mix))
        top_rim, bottom_rim = rim_blocks(rims, from_east, from_west)
        mlp = ring.far_step(mlp, grad_scale, mix)[None]
        mix = ring.far_step(mix, grad_scale, mlp, top_rim, bottom_rim)[None]
        from_north, from_south = beyond(top_rim, bottom_rim)
        mlp = ring.gather_near(mlp)
        mix = ring.gather_second(mix, mlp)
        from_north, from_south, _ = lax.optimization_barrier((from_north, from_south, mlp))
        mlp = ring.gather_second(mlp, mix, from_north, from_south)
        mix = ring.gather_near(mix, mlp)
        mlp = ring.gather_first(mlp, mix)
        mlp_other = ring.gather_core(mlp)
        grad_field = whole_field(inner, from_east, from_west, from_north, from_south)
        own = mlp.reshape(mlp_half)
        down_out = first_half(core, own[:half_units], 0)
        up_out = first_half(core, own[half_units:], 1)
        got = send_along(place, mix, first_mask)
        got, grad_field, down_out, up_out, _ = lax.optimization_barrier(
            (got, grad_field, down_out, up_out, mlp)
        )
        mix = joined(ring.first, mix, got)
        mix_other = ring.gather_core(mix)
        mix_out = first_half(core, mix.reshape(mix_half), 1)
        mlp_other, mix_out, _ = lax.optimization_barrier((mlp_other, mix_out, mix))
        mlp_other = mlp_other.reshape(mlp_half)
        down_out = second_half(core, down_out, mlp_other[:half_units], 0)
        up_out = second_half(core, up_out, mlp_other[half_units:], 1)
        mix_other, down_out, up_out = lax.optimization_barrier((mix_other, down_out, up_out))
        mix_out = second_half(core, mix_out, mix_other.reshape(mix_half), 1)
    else:
        inner, rims, to_west, to_east = adjoint_of(hidden_grad)
        from_east = lax.ppermute(to_west, "lon", place.west)
        from_west = lax.ppermute(to_east, "lon", place.east)

        rim_pair = rim_blocks(rims, from_east, from_west)
        grad_field = whole_field(inner, from_east, from_west, *beyond(*rim_pair))

        def whole(keep, send):
            keep, send = keep.astype(full)[None], send.astype(full)[None]
            both = jnp.where(core == 0, jnp.concatenate([keep, send]), jnp.concatenate([send, keep]))
            return lax.psum(both, AXES) * grad_scale

        mlp_sum = whole(mlp_keep, mlp_send).astype(low)
        mix_sum = whole(mix_keep, mix_send).astype(low)
        down_out = mlp_sum[:, :half_units].reshape(down_weight.shape)
        up_out = jnp.concatenate([mlp_sum[0, half_units:], mlp_sum[1, half_units:]], axis=1)
        mix_out = mix_sum.swapaxes(0, 1).reshape(mix_weight.shape)

    return (block_out.reshape(field_in.shape), grad_field, mix_out, up_out, down_out)


def solution(mesh):
    placed = (
        P("lat", "lon", None),
        P(None, "lat", None, None),
        P("lat"),
        P(),
        P(),
        P(),
        P("lat", "lon", None),
    )
    return jax.shard_map(
        local,
        mesh=mesh,
        in_specs=placed,
        out_specs=(P("lat", "lon", None), P("lat", "lon", None), P(), P(), P()),
        check_vma=False,
    )
```

```python
import functools
import math

import jax
import jax.numpy as jnp
from jax import lax
from jax.experimental import pallas as pl
from jax.experimental.pallas import tpu as pltpu
from jax.sharding import PartitionSpec as P

inv_root_two = 0.7071067811865476
inv_root_tau = 0.3989422804014327
AXES = ("lat", "lon")


class Place:
    def __init__(self):
        self.lats = lax.axis_size("lat")
        self.lons = lax.axis_size("lon")
        self.count = self.lats * self.lons
        self.lat = lax.axis_index("lat")
        self.lon = lax.axis_index("lon")
        self.flat = self.lat * self.lons + self.lon
        lats, lons = self.lats, self.lons
        self.east = [(i, (i + 1) % lons) for i in range(lons)]
        self.west = [(j, i) for i, j in self.east]
        self.pairs = [
            (r * lons + c, (r ^ 1) * lons + c) for r in range(lats) for c in range(lons)
        ]
        self.bridges = []
        for r in range(lats):
            other = r - 1 if r % 2 == 0 else r + 1
            for c in range(lons):
                if 0 <= other < lats:
                    self.bridges.append((r * lons + c, other * lons + c))
                else:
                    self.bridges.append((r * lons + c, r * lons + (c + lons // 2) % lons))
        self.even = self.lat % 2 == 0


def route(place, mask_of):
    return [(i, i ^ mask_of(i)) for i in range(place.count)]


def send_along(place, block, mask_of):
    return lax.ppermute(block, AXES, route(place, mask_of))


def first_mask(i):
    return 2 if i % 2 == 0 else 4


def second_mask(i):
    return 4 if i % 2 == 0 else 2


def after(value, *others):
    return lax.optimization_barrier((value, *others))[0] if others else value


def near_mask(i):
    return 8


def pick(array, index):
    return lax.dynamic_index_in_dim(array, index, 0, keepdims=False)


def joined(bit, own, other):
    return jnp.concatenate([jnp.where(bit == 0, own, other), jnp.where(bit == 0, other, own)])


class Ring:
    def __init__(self, place):
        self.place = place
        self.core = place.flat % 2
        side_y, side_x = (place.flat // 2) % 2, (place.flat // 4) % 2
        self.first = jnp.where(self.core == 0, side_y, side_x)
        self.second = jnp.where(self.core == 0, side_x, side_y)
        self.near = (place.flat // 8) % 2

    def to_core(self, keep, send):
        got = send_along(self.place, send, lambda i: 1)
        return keep.astype(jnp.float32) + got.astype(jnp.float32)

    def leaving(self, buf, bit):
        return pick(buf, 1 - bit).astype(jnp.bfloat16)

    def step(self, buf, out, mask_of, bit, *ties):
        got = after(send_along(self.place, out, mask_of), *ties)
        return pick(buf, bit) + got.astype(jnp.float32)

    def far_step(self, own, scale, *ties):
        far = after(send_along(self.place, own, lambda i: 16), *ties)
        return ((own.astype(jnp.float32) + far.astype(jnp.float32)) * scale).astype(own.dtype)

    def gather_near(self, buf, *ties):
        return joined(self.near, buf, after(send_along(self.place, buf, near_mask), *ties))

    def gather_second(self, buf, *ties):
        return joined(self.second, buf, after(send_along(self.place, buf, second_mask), *ties))

    def gather_first(self, buf, *ties):
        return joined(self.first, buf, after(send_along(self.place, buf, first_mask), *ties))

    def gather_core(self, buf, *ties):
        return after(send_along(self.place, buf, lambda i: 1), *ties)


def first_half(core, own, axis):
    size = own.shape[axis]
    out = jnp.zeros(own.shape[:axis] + (2 * size,) + own.shape[axis + 1 :], own.dtype)
    return lax.dynamic_update_slice_in_dim(out, own, core * size, axis)


def second_half(core, out, other, axis):
    return lax.dynamic_update_slice_in_dim(out, other, (1 - core) * other.shape[axis], axis)


OVER_ROWS = (((0,), (0,)), ((), ()))
OVER_LANES = (((1,), (1,)), ((), ()))
VMEM_LIMIT = 56 * 1024 * 1024


def dot(left, right, dims=(((1,), (0,)), ((), ()))):
    return lax.dot_general(left, right, dims, preferred_element_type=jnp.float32)


def tiles(count, size, body):
    def step(i, carry):
        body(pl.ds(pl.multiple_of(i * size, size), size))
        return carry

    lax.fori_loop(0, count // size, step, 0)


def started(pairs, sems, first=0):
    copies = [pltpu.make_async_copy(a, b, sems.at[first + i]) for i, (a, b) in enumerate(pairs)]
    for copy in copies:
        copy.start()
    return copies


def finish(copies):
    for copy in copies:
        copy.wait()


def act_grad_kernel(cot_in, down_in, out, cot, down, ag, sems):
    points = cot.shape[0]
    parts = [pl.ds(i * (points // 3), points // 3) for i in range(3)]
    weights = started([(down_in, down)], sems)
    loads = started([(cot_in.at[at], cot.at[at]) for at in parts], sems, 1)
    finish(weights)
    stores = []
    for i, at in enumerate(parts):
        finish(loads[i : i + 1])
        ag[at, :] = dot(cot[at, :], down[...], OVER_LANES).astype(ag.dtype)
        stores += started([(ag.at[at], out.at[at])], sems, 4 + i)
    finish(stores)


def main_kernel(
    core_ref, reach_ref, field, north, south, west, east, corners_west, corners_east, taps_in,
    mix_in, up_in, down_in, cot_in, ag_in,
    block_out, hg_out, bands_out, mlp_send_out, mlp_keep_out, mix_send_out, mix_keep_out,
    ext, taps, lines, bands, mix, up, down, cot, feats, hidden, act, pre_grad, hg, block, turned, pre_a,
    pre_b, ag, mlp_send, mlp_keep, mix_send, mix_keep, sems
):
    core = core_ref[0]
    rows, cols, channels = field.shape
    reach = west.shape[1]
    basis = mix.shape[0]
    points = rows * cols
    half_units, half_channels = up.shape[1] // 2, channels // 2
    body, inner = pl.ds(1, rows), pl.ds(reach, cols)
    begin, end = pl.ds(0, reach), pl.ds(reach + cols, reach)
    tap_load = started([(taps_in, taps)], sems, 9)
    loads = started(
        [
            (field, ext.at[body, inner]),
            (west, ext.at[body, begin]),
            (east, ext.at[body, end]),
            (north, ext.at[0, inner]),
            (south, ext.at[rows + 1, inner]),
            (corners_west.at[0], ext.at[0, begin]),
            (corners_west.at[1], ext.at[rows + 1, begin]),
            (corners_east.at[0], ext.at[0, end]),
            (corners_east.at[1], ext.at[rows + 1, end]),
        ],
        sems,
    )
    late = 10
    weights = started([(mix_in, mix), (up_in, up), (ag_in, ag), (cot_in, cot)], sems, late)
    weights += started([(down_in, down)], sems, late + 13)
    finish(tap_load)

    count, width = taps.shape[3], lines.shape[3]
    away = jnp.abs(lax.broadcasted_iota(jnp.int32, (3, count), 1) - (count - 1) // 2)
    lines[...] = jnp.zeros(lines.shape, lines.dtype)
    for r in range(rows):
        inside = away <= reach_ref[r]
        for k in range(basis):
            lines[r, k, :, :count] = jnp.where(inside, taps[k, r].astype(jnp.float32), 0.0)
            for d in range(3):
                line = jnp.broadcast_to(lines[r, k, d : d + 1], (cols, width))
                band = pltpu.roll(line, 0, 1, stride=1, stride_axis=0)
                bands[r, k * cols : (k + 1) * cols, d * width : (d + 1) * width] = band.astype(
                    bands.dtype
                )
    stores = started([(bands, bands_out)], sems, late + 12)
    finish(loads)

    for r in range(rows):
        window = ext[r : r + 3].reshape(3 * ext.shape[1], channels)
        out = dot(bands[r], window).astype(feats.dtype)
        at = pl.ds(r * cols, cols)
        for k in range(basis):
            feats[k, at, :] = out[k * cols : (k + 1) * cols]
        hidden[at, :] = ext[r + 1, inner, :]
    finish(weights[:1])

    for i in range(3):
        at = pl.ds(i * (points // 3), points // 3)
        total = hidden[at, :].astype(jnp.float32)
        for k in range(basis):
            total = total + dot(feats[k, at, :], mix[k])
        hidden[at, :] = total.astype(hidden.dtype)
    finish(weights[1:])
    size = pre_a.shape[0]
    slots = (pre_a, pre_b)

    def products(i):
        at = pl.ds(i * size, size)
        slots[i % 2][...] = dot(hidden[at, :], up[...])

    def activation(i):
        at = pl.ds(i * size, size)
        value = slots[i % 2][...]
        phi = 0.5 * (1.0 + lax.erf(value * inv_root_two))
        act[at, :] = (value * phi).astype(act.dtype)
        slope = phi + value * jnp.exp(-0.5 * value * value) * inv_root_tau
        pre_grad[at, :] = (ag[at, :].astype(jnp.float32) * slope).astype(pre_grad.dtype)

    products(0)
    for i in range(points // size):
        if (i + 1) * size < points:
            products(i + 1)
        activation(i)
    turned[...] = hidden[...].T

    def mlp_sums(half, out):
        at = pl.ds(pl.multiple_of(half * half_units, half_units), half_units)
        out[:half_units] = dot(act[:, at], cot[...], OVER_ROWS).astype(out.dtype)
        out[half_units:] = dot(turned[...], pre_grad[:, at]).astype(out.dtype)

    mlp_sums(1 - core, mlp_send)
    stores += started([(mlp_send, mlp_send_out)], sems, late + 4)
    mlp_sums(core, mlp_keep)
    stores += started([(mlp_keep, mlp_keep_out)], sems, late + 5)

    parts = [pl.ds(i * (points // 3), points // 3) for i in range(3)]
    for at in parts:
        total = cot[at, :].astype(jnp.float32) + dot(pre_grad[at, :], up[...], OVER_LANES)
        hg[at, :] = total.astype(hg.dtype)
    stores += started([(hg, hg_out)], sems, late + 6)

    def mix_sums(half, out):
        at = pl.ds(pl.multiple_of(half * half_channels, half_channels), half_channels)
        for k in range(basis):
            out[k] = dot(feats[k, :, at], hg[...], OVER_ROWS).astype(out.dtype)

    mix_sums(1 - core, mix_send)
    stores += started([(mix_send, mix_send_out)], sems, late + 7)
    mix_sums(core, mix_keep)
    stores += started([(mix_keep, mix_keep_out)], sems, late + 8)

    for i, at in enumerate(parts):
        total = hidden[at, :].astype(jnp.float32) + dot(act[at, :], down[...])
        block[at, :] = total.astype(block.dtype)
        stores += started([(block.at[at], block_out.at[at])], sems, late + 9 + i)
    finish(stores)


def adjoint_kernel(
    hg_in, mix_in, bands_in, inner_out, rim_out, west_out, east_out,
    hg, mix, bands, grads, pulled, inner, sems, *, cols
):
    basis, channels = mix.shape[0], mix.shape[1]
    rows, width = pulled.shape[0] - 2, pulled.shape[1]
    reach = (width - cols) // 2
    loads = started([(hg_in, hg)], sems)
    loads += started([(mix_in.at[k], mix.at[k]) for k in range(basis)], sems, 1)
    late = 1 + basis
    band_loads = started([(bands_in.at[r], bands.at[r]) for r in range(rows)], sems, late)
    pulled[...] = jnp.zeros(pulled.shape, pulled.dtype)
    group = 5 if rows % 5 == 0 else 1
    finish(loads[:1])
    for k in range(basis):
        finish(loads[1 + k : 2 + k])
        for r in range(0, rows, group):
            part = dot(hg[r * cols : (r + group) * cols, :], mix[k], OVER_LANES)
            grads[r : r + group, k * cols : (k + 1) * cols] = part.astype(grads.dtype).reshape(
                group, cols, channels
            )
    stores = []

    def give(row):
        own = hg[(row - 1) * cols : row * cols, :].astype(jnp.float32)
        inner[row - 1] = (pulled[row, reach : reach + cols] + own).astype(inner.dtype)
        copies = [(inner.at[row - 1], inner_out.at[row - 1])]
        stores.extend(started(copies, sems, late + rows + row - 1))

    for r in range(rows):
        finish(band_loads[r : r + 1])
        part = dot(bands[r], grads[r], OVER_ROWS)
        pulled[r : r + 3] += part.reshape(3, width, channels)
        if r:
            give(r)
    give(rows)
    west_out[...] = pulled[:, :reach].astype(west_out.dtype)
    east_out[...] = pulled[:, reach + cols :].astype(east_out.dtype)
    for n, r in enumerate((0, rows + 1)):
        rim_out[n] = pulled[r, reach : reach + cols]
    finish(stores)


def call(kernel, operands, kinds, shapes, out_kinds, scratch, flops, nbytes):
    return pl.pallas_call(
        kernel,
        out_shape=[jax.ShapeDtypeStruct(shape, kind) for shape, kind in shapes],
        in_specs=[pl.BlockSpec(memory_space=kind) for kind in kinds],
        out_specs=[pl.BlockSpec(memory_space=kind) for kind in out_kinds],
        scratch_shapes=scratch,
        compiler_params=pltpu.CompilerParams(vmem_limit_bytes=VMEM_LIMIT),
        cost_estimate=pl.CostEstimate(flops=flops, bytes_accessed=nbytes, transcendentals=0),
    )(*operands)


def local(field_in, kernel_taps, row_reach, mix_weight, up_weight, down_weight, cotangent):
    lat_rows, lon_cols, channels = field_in.shape
    basis_count = kernel_taps.shape[0]
    tap_count = kernel_taps.shape[3]
    reach = (tap_count - 1) // 2
    hidden_units = up_weight.shape[1]
    place = Place()

    top, bottom = field_in[0], field_in[lat_rows - 1]
    inner = lax.ppermute(jnp.where(place.even, bottom, top), AXES, place.pairs)
    outer = lax.ppermute(jnp.where(place.even, top, bottom), AXES, place.bridges)
    west = lax.ppermute(field_in[:, lon_cols - reach :], "lon", place.east)
    east = lax.ppermute(field_in[:, :reach], "lon", place.west)
    north = jnp.where(place.even, outer, inner)
    south = jnp.where(place.even, inner, outer)
    corners = jnp.stack([north[lon_cols - reach :], south[lon_cols - reach :]])
    corners_west = lax.ppermute(corners, "lon", place.east)
    corners = jnp.stack([north[:reach], south[:reach]])
    corners_east = lax.ppermute(corners, "lon", place.west)

    low, full = jnp.bfloat16, jnp.float32
    points = lat_rows * lon_cols
    width = lon_cols + 2 * reach
    vmem, anywhere, smem = pltpu.VMEM, pl.ANY, pltpu.SMEM
    cot = cotangent.reshape(points, channels)
    band_shape = (lat_rows, basis_count * lon_cols, 3 * width)
    gemm = 2 * points * channels * hidden_units
    mix_gemm = 2 * points * channels * channels * basis_count
    band_gemm = 2 * lat_rows * basis_count * lon_cols * 3 * width * channels
    half_units, half_channels = hidden_units // 2, channels // 2
    mlp_half = (half_units + channels, channels)
    mix_half = (basis_count, half_channels, channels)
    big, wide, many = (points, channels), (points, hidden_units), (basis_count, points, channels)
    core = place.flat % 2
    core_op = core[None].astype(jnp.int32)
    sized = (points // 5, hidden_units)
    (act_grad,) = call(
        act_grad_kernel,
        (cot, down_weight),
        [anywhere] * 2,
        [(wide, low)],
        [anywhere],
        [
            pltpu.VMEM(big, low),
            pltpu.VMEM(down_weight.shape, low),
            pltpu.VMEM(wide, low),
            pltpu.SemaphoreType.DMA((7,)),
        ],
        gemm,
        3 * points * hidden_units * 2,
    )
    block_out, hidden_grad, bands, mlp_send, mlp_keep, mix_send, mix_keep = call(
        main_kernel,
        (
            core_op, row_reach, field_in, north, south, west, east, corners_west, corners_east,
            kernel_taps, mix_weight, up_weight, down_weight, cot, act_grad,
        ),
        [smem] * 2 + [anywhere] * 13,
        [(big, low), (big, low), (band_shape, low), (mlp_half, low), (mlp_half, low), (mix_half, low), (mix_half, low)],
        [anywhere] * 7,
        [
            pltpu.VMEM((lat_rows + 2, width, channels), low),
            pltpu.VMEM(kernel_taps.shape, low),
            pltpu.VMEM((lat_rows, basis_count, 3, width), full),
            pltpu.VMEM(band_shape, low),
            pltpu.VMEM(mix_weight.shape, low),
            pltpu.VMEM(up_weight.shape, low),
            pltpu.VMEM(down_weight.shape, low),
            pltpu.VMEM(big, low),
            pltpu.VMEM(many, low),
            pltpu.VMEM(big, low),
            pltpu.VMEM(wide, low),
            pltpu.VMEM(wide, low),
            pltpu.VMEM(big, low),
            pltpu.VMEM(big, low),
            pltpu.VMEM((channels, points), low),
            pltpu.VMEM(sized, full),
            pltpu.VMEM(sized, full),
            pltpu.VMEM(wide, low),
            pltpu.VMEM(mlp_half, low),
            pltpu.VMEM(mlp_half, low),
            pltpu.VMEM(mix_half, low),
            pltpu.VMEM(mix_half, low),
            pltpu.SemaphoreType.DMA((24,)),
        ],
        band_gemm + 2 * mix_gemm + 6 * gemm,
        7 * points * hidden_units * 2,
    )

    def adjoint_of(hidden_grad, *start):
        side = (lat_rows + 2, reach, channels)
        return call(
            functools.partial(adjoint_kernel, cols=lon_cols),
            (after(hidden_grad, *start), mix_weight, bands),
            [anywhere] * 3,
            [
                (field_in.shape, low), ((2, lon_cols, channels), full), (side, low), (side, low),
            ],
            [anywhere] + [vmem] * 3,
            [
                pltpu.VMEM(big, low),
                pltpu.VMEM(mix_weight.shape, low),
                pltpu.VMEM(band_shape, low),
                pltpu.VMEM((lat_rows, basis_count * lon_cols, channels), low),
                pltpu.VMEM((lat_rows + 2, width, channels), full),
                pltpu.VMEM(field_in.shape, low),
                pltpu.SemaphoreType.DMA((1 + basis_count + 2 * lat_rows,)),
            ],
            band_gemm + mix_gemm,
            3 * points * hidden_units * 4,
        )

    def rim_blocks(rims, from_east, from_west):
        corner_east = jnp.stack([from_east[0], from_east[lat_rows + 1]]).astype(full)
        corner_west = jnp.stack([from_west[0], from_west[lat_rows + 1]]).astype(full)
        rims = rims.at[:, lon_cols - reach :].add(corner_east)
        rims = rims.at[:, :reach].add(corner_west).astype(low)
        return jnp.where(place.even, rims[1], rims[0]), jnp.where(place.even, rims[0], rims[1])

    def beyond(near, far):
        near = lax.ppermute(near, AXES, place.pairs)
        far = lax.ppermute(far, AXES, place.bridges)
        return near, far

    def whole_field(inner, from_east, from_west, near, far):
        middle = lon_cols - 2 * reach
        ends = jnp.stack([jnp.where(place.even, far, near), jnp.where(place.even, near, far)])
        ends = ends.astype(full)
        sides = jnp.concatenate(
            [
                from_west[1 : lat_rows + 1].astype(full),
                jnp.zeros((lat_rows, middle, channels), full),
                from_east[1 : lat_rows + 1].astype(full),
            ],
            axis=1,
        )
        nothing = jnp.zeros((lat_rows - 2, lon_cols, channels), full)
        ends = jnp.concatenate([ends[:1], nothing, ends[1:]])
        return (inner.astype(full) + sides + ends).astype(low)

    grad_scale = 1.0 / math.sqrt(points * place.count)
    if place.count == 32:
        ring = Ring(place)
        block_shape = (2, 2, 2, mlp_half[0] // 8, channels)
        mlp = ring.to_core(mlp_keep.reshape(block_shape), mlp_send.reshape(block_shape))
        mlp_out = ring.leaving(mlp, ring.first)
        block_shape = (2, 2, 2, basis_count * half_channels // 8, channels)
        mix = ring.to_core(mix_keep.reshape(block_shape), mix_send.reshape(block_shape))
        mix_out = ring.leaving(mix, ring.first)
        inner, rims, to_west, to_east = adjoint_of(hidden_grad, mlp_out, mix_out)
        mlp = ring.step(mlp, mlp_out, first_mask, ring.first, to_west)
        mlp_out = ring.leaving(mlp, ring.second)
        mix = ring.step(mix, mix_out, first_mask, ring.first, mlp_out)
        mix_out = ring.leaving(mix, ring.near)
        mlp = ring.step(mlp, mlp_out, second_mask, ring.second, mix_out)
        mlp_out = ring.leaving(mlp, ring.near)
        to_west, to_east, _ = lax.optimization_barrier((to_west, to_east, mlp_out))
        from_east = lax.ppermute(to_west, "lon", place.west)
        from_west = lax.ppermute(to_east, "lon", place.east)
        mix = ring.step(mix, mix_out, near_mask, ring.near, mlp_out)
        mix_out = ring.leaving(mix, ring.second)
        mlp = ring.step(mlp, mlp_out, near_mask, ring.near, mix_out).astype(low)
        mix = ring.step(mix, mix_out, second_mask, ring.second, mlp).astype(low)
        from_east, from_west, _ = lax.optimization_barrier((from_east, from_west, mix))
        top_rim, bottom_rim = rim_blocks(rims, from_east, from_west)
        mlp = ring.far_step(mlp, grad_scale, mix)[None]
        mix = ring.far_step(mix, grad_scale, mlp, top_rim, bottom_rim)[None]
        from_north, from_south = beyond(top_rim, bottom_rim)
        mlp = ring.gather_near(mlp)
        mix = ring.gather_second(mix, mlp)
        from_north, from_south, _ = lax.optimization_barrier((from_north, from_south, mlp))
        mlp = ring.gather_second(mlp, mix, from_north, from_south)
        mix = ring.gather_near(mix, mlp)
        mlp = ring.gather_first(mlp, mix)
        mlp_other = ring.gather_core(mlp)
        grad_field = whole_field(inner, from_east, from_west, from_north, from_south)
        own = mlp.reshape(mlp_half)
        down_out = first_half(core, own[:half_units], 0)
        up_out = first_half(core, own[half_units:], 1)
        got = send_along(place, mix, first_mask)
        got, grad_field, down_out, up_out, _ = lax.optimization_barrier(
            (got, grad_field, down_out, up_out, mlp)
        )
        mix = joined(ring.first, mix, got)
        mix_other = ring.gather_core(mix)
        mix_out = first_half(core, mix.reshape(mix_half), 1)
        mlp_other, mix_out, _ = lax.optimization_barrier((mlp_other, mix_out, mix))
        mlp_other = mlp_other.reshape(mlp_half)
        down_out = second_half(core, down_out, mlp_other[:half_units], 0)
        up_out = second_half(core, up_out, mlp_other[half_units:], 1)
        mix_other, down_out, up_out = lax.optimization_barrier((mix_other, down_out, up_out))
        mix_out = second_half(core, mix_out, mix_other.reshape(mix_half), 1)
    else:
        inner, rims, to_west, to_east = adjoint_of(hidden_grad)
        from_east = lax.ppermute(to_west, "lon", place.west)
        from_west = lax.ppermute(to_east, "lon", place.east)

        rim_pair = rim_blocks(rims, from_east, from_west)
        grad_field = whole_field(inner, from_east, from_west, *beyond(*rim_pair))

        def whole(keep, send):
            keep, send = keep.astype(full)[None], send.astype(full)[None]
            both = jnp.where(core == 0, jnp.concatenate([keep, send]), jnp.concatenate([send, keep]))
            return lax.psum(both, AXES) * grad_scale

        mlp_sum = whole(mlp_keep, mlp_send).astype(low)
        mix_sum = whole(mix_keep, mix_send).astype(low)
        down_out = mlp_sum[:, :half_units].reshape(down_weight.shape)
        up_out = jnp.concatenate([mlp_sum[0, half_units:], mlp_sum[1, half_units:]], axis=1)
        mix_out = mix_sum.swapaxes(0, 1).reshape(mix_weight.shape)

    return (block_out.reshape(field_in.shape), grad_field, mix_out, up_out, down_out)


def solution(mesh):
    placed = (
        P("lat", "lon", None),
        P(None, "lat", None, None),
        P("lat"),
        P(),
        P(),
        P(),
        P("lat", "lon", None),
    )
    return jax.shard_map(
        local,
        mesh=mesh,
        in_specs=placed,
        out_specs=(P("lat", "lon", None), P("lat", "lon", None), P(), P(), P()),
        check_vma=False,
    )
```

```python
import functools
import math

import jax
import jax.numpy as jnp
from jax import lax
from jax.experimental import pallas as pl
from jax.experimental.pallas import tpu as pltpu
from jax.sharding import PartitionSpec as P

inv_root_two = 0.7071067811865476
inv_root_tau = 0.3989422804014327
AXES = ("lat", "lon")


class Place:
    def __init__(self):
        self.lats = lax.axis_size("lat")
        self.lons = lax.axis_size("lon")
        self.count = self.lats * self.lons
        self.lat = lax.axis_index("lat")
        self.lon = lax.axis_index("lon")
        self.flat = self.lat * self.lons + self.lon
        lats, lons = self.lats, self.lons
        self.east = [(i, (i + 1) % lons) for i in range(lons)]
        self.west = [(j, i) for i, j in self.east]
        self.pairs = [
            (r * lons + c, (r ^ 1) * lons + c) for r in range(lats) for c in range(lons)
        ]
        self.bridges = []
        for r in range(lats):
            other = r - 1 if r % 2 == 0 else r + 1
            for c in range(lons):
                if 0 <= other < lats:
                    self.bridges.append((r * lons + c, other * lons + c))
                else:
                    self.bridges.append((r * lons + c, r * lons + (c + lons // 2) % lons))
        self.even = self.lat % 2 == 0


def route(place, mask_of):
    return [(i, i ^ mask_of(i)) for i in range(place.count)]


def send_along(place, block, mask_of):
    return lax.ppermute(block, AXES, route(place, mask_of))


def first_mask(i):
    return 2 if i % 2 == 0 else 4


def second_mask(i):
    return 4 if i % 2 == 0 else 2


def after(value, *others):
    return lax.optimization_barrier((value, *others))[0] if others else value


def near_mask(i):
    return 8


def pick(array, index):
    return lax.dynamic_index_in_dim(array, index, 0, keepdims=False)


def joined(bit, own, other):
    return jnp.concatenate([jnp.where(bit == 0, own, other), jnp.where(bit == 0, other, own)])


class Ring:
    def __init__(self, place):
        self.place = place
        self.core = place.flat % 2
        side_y, side_x = (place.flat // 2) % 2, (place.flat // 4) % 2
        self.first = jnp.where(self.core == 0, side_y, side_x)
        self.second = jnp.where(self.core == 0, side_x, side_y)
        self.near = (place.flat // 8) % 2

    def to_core(self, keep, send):
        got = send_along(self.place, send, lambda i: 1)
        return keep.astype(jnp.float32) + got.astype(jnp.float32)

    def leaving(self, buf, bit):
        return pick(buf, 1 - bit).astype(jnp.bfloat16)

    def step(self, buf, out, mask_of, bit, *ties):
        got = after(send_along(self.place, out, mask_of), *ties)
        return pick(buf, bit) + got.astype(jnp.float32)

    def far_step(self, own, scale, *ties):
        far = after(send_along(self.place, own, lambda i: 16), *ties)
        return ((own.astype(jnp.float32) + far.astype(jnp.float32)) * scale).astype(own.dtype)

    def gather_near(self, buf, *ties):
        return joined(self.near, buf, after(send_along(self.place, buf, near_mask), *ties))

    def gather_second(self, buf, *ties):
        return joined(self.second, buf, after(send_along(self.place, buf, second_mask), *ties))

    def gather_first(self, buf, *ties):
        return joined(self.first, buf, after(send_along(self.place, buf, first_mask), *ties))

    def gather_core(self, buf, *ties):
        return after(send_along(self.place, buf, lambda i: 1), *ties)


def first_half(core, own, axis):
    size = own.shape[axis]
    out = jnp.zeros(own.shape[:axis] + (2 * size,) + own.shape[axis + 1 :], own.dtype)
    return lax.dynamic_update_slice_in_dim(out, own, core * size, axis)


def second_half(core, out, other, axis):
    return lax.dynamic_update_slice_in_dim(out, other, (1 - core) * other.shape[axis], axis)


OVER_ROWS = (((0,), (0,)), ((), ()))
OVER_LANES = (((1,), (1,)), ((), ()))
VMEM_LIMIT = 56 * 1024 * 1024


def dot(left, right, dims=(((1,), (0,)), ((), ()))):
    return lax.dot_general(left, right, dims, preferred_element_type=jnp.float32)


def tiles(count, size, body):
    def step(i, carry):
        body(pl.ds(pl.multiple_of(i * size, size), size))
        return carry

    lax.fori_loop(0, count // size, step, 0)


def started(pairs, sems, first=0):
    copies = [pltpu.make_async_copy(a, b, sems.at[first + i]) for i, (a, b) in enumerate(pairs)]
    for copy in copies:
        copy.start()
    return copies


def finish(copies):
    for copy in copies:
        copy.wait()


def main_kernel(
    core_ref, reach_ref, field, north, south, west, east, corners_west, corners_east, taps_in,
    mix_in, up_in, down_in, cot_in,
    block_out, hg_out, bands_out, mlp_send_out, mlp_keep_out, mix_send_out, mix_keep_out,
    ext, taps, lines, bands, mix, up, down, cot, feats, hidden, act, pre_grad, hg, block, turned, pre_a,
    pre_b, ag_a, ag_b, mlp_send, mlp_keep, mix_send, mix_keep, sems
):
    core = core_ref[0]
    rows, cols, channels = field.shape
    reach = west.shape[1]
    basis = mix_in.shape[0]
    points = rows * cols
    half_units, half_channels = up.shape[1] // 2, channels // 2
    body, inner = pl.ds(1, rows), pl.ds(reach, cols)
    begin, end = pl.ds(0, reach), pl.ds(reach + cols, reach)
    tap_load = started([(taps_in, taps)], sems, 9)
    loads = started(
        [
            (field, ext.at[body, inner]),
            (west, ext.at[body, begin]),
            (east, ext.at[body, end]),
            (north, ext.at[0, inner]),
            (south, ext.at[rows + 1, inner]),
            (corners_west.at[0], ext.at[0, begin]),
            (corners_west.at[1], ext.at[rows + 1, begin]),
            (corners_east.at[0], ext.at[0, end]),
            (corners_east.at[1], ext.at[rows + 1, end]),
        ],
        sems,
    )
    late = 10
    mix_loads = started(
        [(mix_in.at[k], mix.at[pl.ds(k * channels, channels)]) for k in range(basis)], sems, late + 13
    )
    weights = started([(up_in, up), (down_in, down), (cot_in, cot)], sems, late)
    finish(tap_load)

    count, width = taps.shape[3], lines.shape[3]
    away = jnp.abs(lax.broadcasted_iota(jnp.int32, (3, count), 1) - (count - 1) // 2)
    lines[...] = jnp.zeros(lines.shape, lines.dtype)
    for r in range(rows):
        inside = away <= reach_ref[r]
        for k in range(basis):
            lines[r, k, :, :count] = jnp.where(inside, taps[k, r].astype(jnp.float32), 0.0)
            for d in range(3):
                line = jnp.broadcast_to(lines[r, k, d : d + 1], (cols, width))
                band = pltpu.roll(line, 0, 1, stride=1, stride_axis=0)
                bands[r, k * cols : (k + 1) * cols, d * width : (d + 1) * width] = band.astype(
                    bands.dtype
                )
    stores = started([(bands, bands_out)], sems, late + 12)
    finish(loads)

    for r in range(rows):
        window = ext[r : r + 3].reshape(3 * ext.shape[1], channels)
        out = dot(bands[r], window).astype(feats.dtype)
        at = pl.ds(r * cols, cols)
        for k in range(basis):
            feats[at, k * channels : (k + 1) * channels] = out[k * cols : (k + 1) * cols]
        hidden[at, :] = ext[r + 1, inner, :]
    finish(mix_loads)

    for i in range(3):
        at = pl.ds(i * (points // 3), points // 3)
        total = hidden[at, :].astype(jnp.float32) + dot(feats[at, :], mix[...])
        hidden[at, :] = total.astype(hidden.dtype)
    finish(weights)
    size = pre_a.shape[0]
    slots = ((pre_a, ag_a), (pre_b, ag_b))

    def products(i):
        at = pl.ds(i * size, size)
        pre, ag = slots[i % 2]
        pre[...] = dot(hidden[at, :], up[...])
        ag[...] = dot(cot[at, :], down[...], OVER_LANES)

    def activation(i):
        at = pl.ds(i * size, size)
        pre, ag = slots[i % 2]
        value = pre[...]
        phi = 0.5 * (1.0 + lax.erf(value * inv_root_two))
        act[at, :] = (value * phi).astype(act.dtype)
        slope = phi + value * jnp.exp(-0.5 * value * value) * inv_root_tau
        pre_grad[at, :] = (ag[...] * slope).astype(pre_grad.dtype)

    products(0)
    for i in range(points // size):
        if (i + 1) * size < points:
            products(i + 1)
        activation(i)
    turned[...] = hidden[...].T

    def mlp_sums(half, out):
        at = pl.ds(pl.multiple_of(half * half_units, half_units), half_units)
        out[:half_units] = dot(act[:, at], cot[...], OVER_ROWS).astype(out.dtype)
        out[half_units:] = dot(turned[...], pre_grad[:, at]).astype(out.dtype)

    mlp_sums(1 - core, mlp_send)
    stores += started([(mlp_send, mlp_send_out)], sems, late + 4)
    mlp_sums(core, mlp_keep)
    stores += started([(mlp_keep, mlp_keep_out)], sems, late + 5)

    parts = [pl.ds(i * (points // 3), points // 3) for i in range(3)]
    for at in parts:
        total = cot[at, :].astype(jnp.float32) + dot(pre_grad[at, :], up[...], OVER_LANES)
        hg[at, :] = total.astype(hg.dtype)
    stores += started([(hg, hg_out)], sems, late + 6)

    def mix_sums(half, out):
        for k in range(basis):
            start = k * channels + half * half_channels
            at = pl.ds(pl.multiple_of(start, half_channels), half_channels)
            out[k] = dot(feats[:, at], hg[...], OVER_ROWS).astype(out.dtype)

    mix_sums(1 - core, mix_send)
    stores += started([(mix_send, mix_send_out)], sems, late + 7)
    mix_sums(core, mix_keep)
    stores += started([(mix_keep, mix_keep_out)], sems, late + 8)

    for i, at in enumerate(parts):
        total = hidden[at, :].astype(jnp.float32) + dot(act[at, :], down[...])
        block[at, :] = total.astype(block.dtype)
        stores += started([(block.at[at], block_out.at[at])], sems, late + 9 + i)
    finish(stores)


def adjoint_kernel(
    hg_in, mix_in, bands_in, inner_out, rim_out, west_out, east_out,
    hg, mix, bands, grads, pulled, inner, sems, *, cols
):
    basis, channels = mix.shape[0], mix.shape[1]
    rows, width = pulled.shape[0] - 2, pulled.shape[1]
    reach = (width - cols) // 2
    loads = started([(hg_in, hg)], sems)
    loads += started([(mix_in.at[k], mix.at[k]) for k in range(basis)], sems, 1)
    late = 1 + basis
    pulled[...] = jnp.zeros(pulled.shape, pulled.dtype)
    group = 5 if rows % 5 == 0 else 1
    finish(loads[:2])
    band_loads = started([(bands_in.at[r], bands.at[r]) for r in range(rows)], sems, late)
    for k in range(basis):
        finish(loads[1 + k : 2 + k] if k else [])
        for r in range(0, rows, group):
            part = dot(hg[r * cols : (r + group) * cols, :], mix[k], OVER_LANES)
            grads[r : r + group, k * cols : (k + 1) * cols] = part.astype(grads.dtype).reshape(
                group, cols, channels
            )
    stores = []

    def give(row):
        own = hg[(row - 1) * cols : row * cols, :].astype(jnp.float32)
        inner[row - 1] = (pulled[row, reach : reach + cols] + own).astype(inner.dtype)
        copies = [(inner.at[row - 1], inner_out.at[row - 1])]
        stores.extend(started(copies, sems, late + rows + row - 1))

    for r in range(rows):
        finish(band_loads[r : r + 1])
        part = dot(bands[r], grads[r], OVER_ROWS)
        pulled[r : r + 3] += part.reshape(3, width, channels)
        if r:
            give(r)
    give(rows)
    west_out[...] = pulled[:, :reach].astype(west_out.dtype)
    east_out[...] = pulled[:, reach + cols :].astype(east_out.dtype)
    for n, r in enumerate((0, rows + 1)):
        rim_out[n] = pulled[r, reach : reach + cols]
    finish(stores)


def call(kernel, operands, kinds, shapes, out_kinds, scratch, flops, nbytes):
    return pl.pallas_call(
        kernel,
        out_shape=[jax.ShapeDtypeStruct(shape, kind) for shape, kind in shapes],
        in_specs=[pl.BlockSpec(memory_space=kind) for kind in kinds],
        out_specs=[pl.BlockSpec(memory_space=kind) for kind in out_kinds],
        scratch_shapes=scratch,
        compiler_params=pltpu.CompilerParams(vmem_limit_bytes=VMEM_LIMIT),
        cost_estimate=pl.CostEstimate(flops=flops, bytes_accessed=nbytes, transcendentals=0),
    )(*operands)


def local(field_in, kernel_taps, row_reach, mix_weight, up_weight, down_weight, cotangent):
    lat_rows, lon_cols, channels = field_in.shape
    basis_count = kernel_taps.shape[0]
    tap_count = kernel_taps.shape[3]
    reach = (tap_count - 1) // 2
    hidden_units = up_weight.shape[1]
    place = Place()

    top, bottom = field_in[0], field_in[lat_rows - 1]
    inner = lax.ppermute(jnp.where(place.even, bottom, top), AXES, place.pairs)
    outer = lax.ppermute(jnp.where(place.even, top, bottom), AXES, place.bridges)
    west = lax.ppermute(field_in[:, lon_cols - reach :], "lon", place.east)
    east = lax.ppermute(field_in[:, :reach], "lon", place.west)
    north = jnp.where(place.even, outer, inner)
    south = jnp.where(place.even, inner, outer)
    corners = jnp.stack([north[lon_cols - reach :], south[lon_cols - reach :]])
    corners_west = lax.ppermute(corners, "lon", place.east)
    corners = jnp.stack([north[:reach], south[:reach]])
    corners_east = lax.ppermute(corners, "lon", place.west)

    low, full = jnp.bfloat16, jnp.float32
    points = lat_rows * lon_cols
    width = lon_cols + 2 * reach
    vmem, anywhere, smem = pltpu.VMEM, pl.ANY, pltpu.SMEM
    cot = cotangent.reshape(points, channels)
    band_shape = (lat_rows, basis_count * lon_cols, 3 * width)
    gemm = 2 * points * channels * hidden_units
    mix_gemm = 2 * points * channels * channels * basis_count
    band_gemm = 2 * lat_rows * basis_count * lon_cols * 3 * width * channels
    half_units, half_channels = hidden_units // 2, channels // 2
    mlp_half = (half_units + channels, channels)
    mix_half = (basis_count, half_channels, channels)
    big, wide = (points, channels), (points, hidden_units)
    core = place.flat % 2
    core_op = core[None].astype(jnp.int32)
    sized = (points // 5, hidden_units)
    block_out, hidden_grad, bands, mlp_send, mlp_keep, mix_send, mix_keep = call(
        main_kernel,
        (
            core_op, row_reach, field_in, north, south, west, east, corners_west, corners_east,
            kernel_taps, mix_weight, up_weight, down_weight, cot,
        ),
        [smem] * 2 + [anywhere] * 12,
        [(big, low), (big, low), (band_shape, low), (mlp_half, low), (mlp_half, low), (mix_half, low), (mix_half, low)],
        [anywhere] * 7,
        [
            pltpu.VMEM((lat_rows + 2, width, channels), low),
            pltpu.VMEM(kernel_taps.shape, low),
            pltpu.VMEM((lat_rows, basis_count, 3, width), full),
            pltpu.VMEM(band_shape, low),
            pltpu.VMEM((basis_count * channels, channels), low),
            pltpu.VMEM(up_weight.shape, low),
            pltpu.VMEM(down_weight.shape, low),
            pltpu.VMEM(big, low),
            pltpu.VMEM((points, basis_count * channels), low),
            pltpu.VMEM(big, low),
            pltpu.VMEM(wide, low),
            pltpu.VMEM(wide, low),
            pltpu.VMEM(big, low),
            pltpu.VMEM(big, low),
            pltpu.VMEM((channels, points), low),
            pltpu.VMEM(sized, full),
            pltpu.VMEM(sized, full),
            pltpu.VMEM(sized, full),
            pltpu.VMEM(sized, full),
            pltpu.VMEM(mlp_half, low),
            pltpu.VMEM(mlp_half, low),
            pltpu.VMEM(mix_half, low),
            pltpu.VMEM(mix_half, low),
            pltpu.SemaphoreType.DMA((23 + basis_count,)),
        ],
        band_gemm + 2 * mix_gemm + 6 * gemm,
        7 * points * hidden_units * 2,
    )

    def adjoint_of(hidden_grad, *start):
        side = (lat_rows + 2, reach, channels)
        return call(
            functools.partial(adjoint_kernel, cols=lon_cols),
            (after(hidden_grad, *start), mix_weight, bands),
            [anywhere] * 3,
            [
                (field_in.shape, low), ((2, lon_cols, channels), full), (side, low), (side, low),
            ],
            [anywhere] + [vmem] * 3,
            [
                pltpu.VMEM(big, low),
                pltpu.VMEM(mix_weight.shape, low),
                pltpu.VMEM(band_shape, low),
                pltpu.VMEM((lat_rows, basis_count * lon_cols, channels), low),
                pltpu.VMEM((lat_rows + 2, width, channels), full),
                pltpu.VMEM(field_in.shape, low),
                pltpu.SemaphoreType.DMA((1 + basis_count + 2 * lat_rows,)),
            ],
            band_gemm + mix_gemm,
            3 * points * hidden_units * 4,
        )

    def rim_blocks(rims, from_east, from_west):
        corner_east = jnp.stack([from_east[0], from_east[lat_rows + 1]]).astype(full)
        corner_west = jnp.stack([from_west[0], from_west[lat_rows + 1]]).astype(full)
        rims = rims.at[:, lon_cols - reach :].add(corner_east)
        rims = rims.at[:, :reach].add(corner_west).astype(low)
        return jnp.where(place.even, rims[1], rims[0]), jnp.where(place.even, rims[0], rims[1])

    def beyond(near, far):
        near = lax.ppermute(near, AXES, place.pairs)
        far = lax.ppermute(far, AXES, place.bridges)
        return near, far

    def whole_field(inner, from_east, from_west, near, far):
        middle = lon_cols - 2 * reach
        ends = jnp.stack([jnp.where(place.even, far, near), jnp.where(place.even, near, far)])
        ends = ends.astype(full)
        sides = jnp.concatenate(
            [
                from_west[1 : lat_rows + 1].astype(full),
                jnp.zeros((lat_rows, middle, channels), full),
                from_east[1 : lat_rows + 1].astype(full),
            ],
            axis=1,
        )
        nothing = jnp.zeros((lat_rows - 2, lon_cols, channels), full)
        ends = jnp.concatenate([ends[:1], nothing, ends[1:]])
        return (inner.astype(full) + sides + ends).astype(low)

    grad_scale = 1.0 / math.sqrt(points * place.count)
    if place.count == 32:
        ring = Ring(place)
        block_shape = (2, 2, 2, mlp_half[0] // 8, channels)
        mlp = ring.to_core(mlp_keep.reshape(block_shape), mlp_send.reshape(block_shape))
        mlp_out = ring.leaving(mlp, ring.first)
        block_shape = (2, 2, 2, basis_count * half_channels // 8, channels)
        mix = ring.to_core(mix_keep.reshape(block_shape), mix_send.reshape(block_shape))
        mix_out = ring.leaving(mix, ring.first)
        inner, rims, to_west, to_east = adjoint_of(hidden_grad, mlp_out, mix_out)
        from_east = lax.ppermute(to_west, "lon", place.west)
        from_west = lax.ppermute(to_east, "lon", place.east)
        mlp = ring.step(mlp, mlp_out, first_mask, ring.first, to_west)
        mlp_out = ring.leaving(mlp, ring.second)
        mix = ring.step(mix, mix_out, first_mask, ring.first, mlp_out)
        mix_out = ring.leaving(mix, ring.near)
        mlp = ring.step(mlp, mlp_out, second_mask, ring.second, mix_out)
        mlp_out = ring.leaving(mlp, ring.near)
        mix = ring.step(mix, mix_out, near_mask, ring.near, mlp_out)
        mix_out = ring.leaving(mix, ring.second)
        mlp = ring.step(mlp, mlp_out, near_mask, ring.near, mix_out).astype(low)
        mix = ring.step(mix, mix_out, second_mask, ring.second, mlp).astype(low)
        from_east, from_west, _ = lax.optimization_barrier((from_east, from_west, mix))
        top_rim, bottom_rim = rim_blocks(rims, from_east, from_west)
        mlp = ring.far_step(mlp, grad_scale, mix)[None]
        mix = ring.far_step(mix, grad_scale, mlp, top_rim, bottom_rim)[None]
        from_north, from_south = beyond(top_rim, bottom_rim)
        mlp = ring.gather_near(mlp)
        mix = ring.gather_second(mix, mlp)
        from_north, from_south, _ = lax.optimization_barrier((from_north, from_south, mlp))
        mlp = ring.gather_second(mlp, mix, from_north, from_south)
        mix = ring.gather_near(mix, mlp)
        mlp = ring.gather_first(mlp, mix)
        mlp_other = ring.gather_core(mlp)
        grad_field = whole_field(inner, from_east, from_west, from_north, from_south)
        own = mlp.reshape(mlp_half)
        down_out = first_half(core, own[:half_units], 0)
        up_out = first_half(core, own[half_units:], 1)
        got = send_along(place, mix, first_mask)
        got, grad_field, down_out, up_out, _ = lax.optimization_barrier(
            (got, grad_field, down_out, up_out, mlp)
        )
        mix = joined(ring.first, mix, got)
        mix_other = ring.gather_core(mix)
        mix_out = first_half(core, mix.reshape(mix_half), 1)
        mlp_other, mix_out, _ = lax.optimization_barrier((mlp_other, mix_out, mix))
        mlp_other = mlp_other.reshape(mlp_half)
        down_out = second_half(core, down_out, mlp_other[:half_units], 0)
        up_out = second_half(core, up_out, mlp_other[half_units:], 1)
        mix_other, down_out, up_out = lax.optimization_barrier((mix_other, down_out, up_out))
        mix_out = second_half(core, mix_out, mix_other.reshape(mix_half), 1)
    else:
        inner, rims, to_west, to_east = adjoint_of(hidden_grad)
        from_east = lax.ppermute(to_west, "lon", place.west)
        from_west = lax.ppermute(to_east, "lon", place.east)

        rim_pair = rim_blocks(rims, from_east, from_west)
        grad_field = whole_field(inner, from_east, from_west, *beyond(*rim_pair))

        def whole(keep, send):
            keep, send = keep.astype(full)[None], send.astype(full)[None]
            both = jnp.where(core == 0, jnp.concatenate([keep, send]), jnp.concatenate([send, keep]))
            return lax.psum(both, AXES) * grad_scale

        mlp_sum = whole(mlp_keep, mlp_send).astype(low)
        mix_sum = whole(mix_keep, mix_send).astype(low)
        down_out = mlp_sum[:, :half_units].reshape(down_weight.shape)
        up_out = jnp.concatenate([mlp_sum[0, half_units:], mlp_sum[1, half_units:]], axis=1)
        mix_out = mix_sum.swapaxes(0, 1).reshape(mix_weight.shape)

    return (block_out.reshape(field_in.shape), grad_field, mix_out, up_out, down_out)


def solution(mesh):
    placed = (
        P("lat", "lon", None),
        P(None, "lat", None, None),
        P("lat"),
        P(),
        P(),
        P(),
        P("lat", "lon", None),
    )
    return jax.shard_map(
        local,
        mesh=mesh,
        in_specs=placed,
        out_specs=(P("lat", "lon", None), P("lat", "lon", None), P(), P(), P()),
        check_vma=False,
    )
```
